32 devices in a mesh: grp: 2 (over y), inst: 4 (over x, core), slab: 4 (over z).
Axes of the slice: x: 2, y: 2, z: 4, core: 2. Of those that a mesh axis runs over, the one named last changes fastest.
Arguments:
- states: float32 [8, 5, 256, 256], P(('grp', 'inst'), None, 'slab'), parts along dimension 0, may hold values from -6 to 6
- volumes: float32 [8, 256, 256], P(('grp', 'inst'), 'slab'), parts along dimension 0, may hold values from 0.5 to 2
- row_normals: float32 [8, 2, 256, 256], P(('grp', 'inst'), None, 'slab'), parts along dimension 0, may hold values from -4 to 4
- col_normals: float32 [8, 2, 256, 256], P(('grp', 'inst'), None, 'slab'), parts along dimension 0, may hold values from -4 to 4
- face_links: int32 [4, 256], P('slab'), may hold values from 0 to 255, each once within a row
- jacobians: float32 [2, 5, 5], replicated, may hold values from -2.5 to 2.5
Outputs:
- solution: float32 [8, 5, 256, 256], P(('grp', 'inst'), None, 'slab'), parts along dimension 0
The draws below stay inside these ranges and needn't reach their ends.
There are 2 independent parts, one for each index of `grp`. The reference program is written for one: setup_inputs(seed, part) draws one part's arguments, and reference() takes and returns one part's arrays. A program takes and returns all parts, laid end to end along the dimension named above; an argument that names none is the same for every part. Nothing has to cross between parts.
Inputs may be any that keep to these rules, and one draw needn't show every extreme that they name: Each row of face_links names every one of the 256 columns once.
All inputs are finite; a program needn't handle non-finite values.
Results may differ from the reference program's by a relative error of at most 0.0001.
Values sent between devices are 32-bit elements; how exact they have to be, the bound alone decides.
No kernel may reach another device: no remote copies, remote signals or barrier semaphores. Data moves between devices by JAX's collectives and lax.ppermute only.
A program may use at most 64 MiB of HBM per device.

```python
import math
import jax
import jax.numpy as jnp
import numpy as np
from jax import lax

NVAR = 5
CA = 64
CB = 256
ITERS = 2
INST = 4
NA = 256
N_SLAB = 4


def levels(rng, extent, shards, smallest, high):
    factor_of = 1.0
    for axis_at, blocks in shards:
        draws = jax.random.uniform(jax.random.fold_in(jax.random.fold_in(rng, 6), axis_at), (blocks,), jnp.float32, smallest / len(shards), high / len(shards))
        factor_of = factor_of * jnp.repeat(jnp.exp(draws), extent[axis_at] // blocks).reshape((-1,) + (1,) * (len(extent) - 1 - axis_at))
    return factor_of


def bell_draw(stream_key, shape, deviation, most, split=(), held_as=jnp.bfloat16):
    drawn = jax.random.normal(stream_key, shape, jnp.float32) * deviation
    if len(split) > 0:
        drawn = levels(stream_key, shape, split, -0.22, 0.18) * drawn
    return jnp.clip(drawn, min=-most, max=most).astype(held_as)


def setup_inputs(seed: int = 0, part: int = 0) -> dict:
    keys = jax.random.split(jax.random.key(seed), 7)
    part_keys = jax.random.split(jax.random.fold_in(keys[6], part), 7)
    return {
        "states": bell_draw(part_keys[0], (INST, NVAR, NA, CB), 1.0, 6.0, ((0, 4), (2, 4)), jnp.float32),
        "volumes": jnp.clip(jnp.exp(math.log(2.0) - 1.3862944 * jax.random.uniform(part_keys[1], (INST, NA, CB), jnp.float32) ** levels(part_keys[1], (INST, NA, CB), ((0, 4), (1, 4)), -0.2, 0.2)), 0.5, 2.0),
        "row_normals": bell_draw(part_keys[2], (INST, 2, NA, CB), 1.0, 4.0, ((0, 4), (2, 4)), jnp.float32),
        "col_normals": bell_draw(part_keys[3], (INST, 2, NA, CB), 1.0, 4.0, ((0, 4), (2, 4)), jnp.float32),
        "face_links": jax.vmap(lambda own: jax.random.permutation(own, CB))(jax.random.split(keys[4], N_SLAB)).reshape((N_SLAB, CB)).astype(jnp.int32),
        "jacobians": bell_draw(keys[5], (2, NVAR, NVAR), NVAR ** -0.5, 2.5, (), jnp.float32),
    }


frequency = 0.5
pseudo_step = 0.2
nyquist_damping = 0.25


def spectral_table(instances):
    offsets = np.arange(instances)[:, None] - np.arange(instances)[None, :]
    phases = np.pi * offsets / instances
    sine_safe = np.where(offsets == 0, 1.0, np.sin(phases))
    parity = np.where(offsets % 2 == 0, 1.0, -1.0)
    matrix = np.where(offsets == 0, 0.0, 0.5 * frequency * parity * np.cos(phases) / sine_safe)
    matrix = matrix + nyquist_damping * parity
    return jnp.asarray(matrix, jnp.float32)


def face_flux(normals, lower_side, upper_side, jacobians):
    summed = lower_side + upper_side
    first_part = jnp.einsum('vw,nwac->nvac', jacobians[0], summed, precision=lax.Precision.HIGHEST)
    second_part = jnp.einsum('vw,nwac->nvac', jacobians[1], summed, precision=lax.Precision.HIGHEST)
    along_x = normals[:, 0:1]
    along_y = normals[:, 1:2]
    return 0.5 * (along_x * first_part + along_y * second_part) - 0.5 * (jnp.abs(along_x) + jnp.abs(along_y)) * (upper_side - lower_side)


def reference(states, volumes, row_normals, col_normals, face_links, jacobians):
    spectral = spectral_table(INST)
    volume_rate = jnp.einsum('nm,mac->nac', spectral, volumes, precision=lax.Precision.HIGHEST)
    order = jnp.argsort(face_links, axis=1).astype(jnp.int32)
    links_full = jnp.broadcast_to(face_links.astype(jnp.int32)[None, None], (INST, NVAR, N_SLAB, CB))
    order_full = jnp.broadcast_to(order[None, None], (INST, NVAR, N_SLAB, CB))
    flow_field = states
    for iteration in range(ITERS):
        time_rate = jnp.einsum('nm,mvac->nvac', spectral, flow_field, precision=lax.Precision.HIGHEST)
        cell_blocks = flow_field.reshape(INST, NVAR, N_SLAB, CA, CB)
        previous = jnp.roll(cell_blocks[:, :, :, CA - 1, :], 1, axis=2)
        ghost_row = jnp.take_along_axis(previous, links_full, axis=3)
        lower_cells = jnp.concatenate([ghost_row[:, :, :, None, :], cell_blocks[:, :, :, :-1, :]], axis=3).reshape(flow_field.shape)
        row_flux = face_flux(row_normals, lower_cells, flow_field, jacobians)
        flux_blocks = row_flux.reshape(INST, NVAR, N_SLAB, CA, CB)
        sent_flux = jnp.take_along_axis(flux_blocks[:, :, :, 0, :], order_full, axis=3)
        arriving = jnp.roll(sent_flux, -1, axis=2)
        row_above = jnp.concatenate([flux_blocks[:, :, :, 1:, :], arriving[:, :, :, None, :]], axis=3).reshape(flow_field.shape)
        col_flux = face_flux(col_normals, jnp.roll(flow_field, 1, axis=3), flow_field, jacobians)
        col_right = jnp.roll(col_flux, -1, axis=3)
        rate = volumes[:, None] * time_rate + flow_field * volume_rate[:, None] + (row_above - row_flux) + (col_right - col_flux)
        flow_field = flow_field - pseudo_step * rate / volumes[:, None]
    return flow_field
```

```python
import functools

import jax
import jax.numpy as jnp
import numpy as np
from jax import lax
from jax.experimental import pallas as pl
from jax.experimental.pallas import tpu as pltpu
from jax.sharding import PartitionSpec as P

ITERS = 2


frequency = 0.5
pseudo_step = 0.2
nyquist_damping = 0.25


def spectral_table(instances):
    offsets = np.arange(instances)[:, None] - np.arange(instances)[None, :]
    phases = np.pi * offsets / instances
    sine_safe = np.where(offsets == 0, 1.0, np.sin(phases))
    parity = np.where(offsets % 2 == 0, 1.0, -1.0)
    matrix = np.where(offsets == 0, 0.0, 0.5 * frequency * parity * np.cos(phases) / sine_safe)
    matrix = matrix + nyquist_damping * parity
    return jnp.asarray(matrix, jnp.float32)


def row_step(rows):
    return rows if rows % 8 == 0 else 1


def pack_kernel(n, rows, states, volumes, row_normals, col_normals, links, *outs):
    nvar, depth = states.shape[1], states.shape[2]
    bufs, edges = outs[:n], outs[n:]
    me = lax.axis_index("inst")

    def put(ref, at, row_below, row_in, row_outer):
        for v in range(nvar):
            ref[pl.ds(at + v, 1), :] = states[0, v, pl.ds(row_below, 1), :]
            ref[pl.ds(at + nvar + v, 1), :] = states[0, v, pl.ds(row_in, 1), :]
        at = at + 2 * nvar
        ref[pl.ds(at, 1), :] = volumes[0, pl.ds(row_in, 1), :]
        for d in range(2):
            ref[pl.ds(at + 1 + d, 1), :] = row_normals[0, d, pl.ds(row_outer, 1), :]
            ref[pl.ds(at + 3 + d, 1), :] = col_normals[0, d, pl.ds(row_in, 1), :]

    def put_inner(ref, at, row):
        for d in range(2):
            ref[pl.ds(at + d, 1), :] = row_normals[0, d, pl.ds(row, 1), :]

    for k in range(n):
        buf = bufs[k]
        block = jnp.bitwise_xor(me, k)
        lo = pl.multiple_of(block * rows, rows)
        at = 0
        step = row_step(rows)
        for r in range(0, rows, step):
            here = pl.ds(lo + r, step)
            for v in range(nvar):
                buf[pl.ds(v * rows + r, step), :] = states[0, v, here, :]
            buf[pl.ds(nvar * rows + r, step), :] = volumes[0, here, :]
            for d in range(2):
                buf[pl.ds((nvar + 1 + d) * rows + r, step), :] = row_normals[0, d, here, :]
                buf[pl.ds((nvar + 3 + d) * rows + r, step), :] = col_normals[0, d, here, :]
        at = (nvar + 5) * rows
        below_1, below_2 = jnp.maximum(lo - 1, 0), jnp.maximum(lo - 2, 0)
        above_1, above_2 = jnp.minimum(lo + rows, depth - 1), jnp.minimum(lo + rows + 1, depth - 1)
        put(buf, at, below_2, below_1, below_1)
        at += 2 * nvar + 5
        put(buf, at, above_2, above_1, above_2)
        put_inner(buf, at + 2 * nvar + 5, above_1)
    for k in range(n):
        edge = edges[k]
        upward = me == k
        put(
            edge,
            0,
            jnp.where(upward, depth - 2, 1),
            jnp.where(upward, depth - 1, 0),
            jnp.where(upward, depth - 1, 1),
        )
        put_inner(edge, 2 * nvar + 5, 0)
        edge[pl.ds(2 * nvar + 7, 1), :] = links[...].astype(jnp.float32)


def split_dot(x, onehot, transposed):
    high = x.astype(jnp.bfloat16)
    rest = x - high.astype(jnp.float32)
    middle = rest.astype(jnp.bfloat16)
    low = (rest - middle.astype(jnp.float32)).astype(jnp.bfloat16)
    count = x.shape[0]
    stacked = jnp.concatenate([high, middle, low], axis=0)
    out = lax.dot_general(
        stacked,
        onehot,
        (((1,), (1 if transposed else 0,)), ((), ())),
        preferred_element_type=jnp.float32,
    )
    return out[:count] + (out[count : 2 * count] + out[2 * count :])


def compute_kernel(n, rows, nvar, iterations, table, jacobians, links, *refs):
    bufs, edges, outs = refs[:n], refs[n : 2 * n], refs[2 * n : 3 * n]
    halo, rim, flow = refs[3 * n :]
    columns = links.shape[1]
    main = (nvar + 5) * rows
    below_at, above_at = main, main + 2 * nvar + 5
    me = lax.axis_index("inst")
    first, last = me == 0, me == n - 1
    half = [[[0.5 * jacobians[d, v, w] for w in range(nvar)] for v in range(nvar)] for d in range(2)]
    weights = [
        [pseudo_step * table[jnp.bitwise_xor(me, k), jnp.bitwise_xor(me, j)] for j in range(n)]
        for k in range(n)
    ]

    for k in range(n):
        for t in range(2 * nvar + 5):
            halo[t, pl.ds(k, 1), :] = jnp.where(
                first, edges[k][pl.ds(t, 1), :], bufs[k][pl.ds(below_at + t, 1), :]
            )
        for t in range(2 * nvar + 7):
            halo[t, pl.ds(n + k, 1), :] = jnp.where(
                last, edges[k][pl.ds(t, 1), :], bufs[k][pl.ds(above_at + t, 1), :]
            )
        for d in range(2):
            halo[2 * nvar + 5 + d, pl.ds(k, 1), :] = bufs[k][pl.ds((nvar + 1 + d) * rows, 1), :]

    own = lax.broadcasted_iota(jnp.int32, (1, columns), 1)
    cell = lax.broadcasted_iota(jnp.int32, (columns, columns), 0)
    links_above = edges[0][pl.ds(2 * nvar + 7, 1), :].astype(jnp.int32)
    onehot_below = (cell == jnp.where(first, links[...], own)).astype(jnp.float32).astype(jnp.bfloat16)
    onehot_above = (cell == jnp.where(last, links_above, own)).astype(jnp.float32).astype(jnp.bfloat16)
    side = lax.broadcasted_iota(jnp.int32, (2 * n, columns), 0)
    is_below = side < n
    place = jnp.where(is_below, side, side - n)

    def crossed(values, back):
        stacked = jnp.concatenate(values, axis=0)
        through_below = split_dot(stacked, onehot_below, back)
        through_above = split_dot(stacked, onehot_above, back)
        return [
            jnp.where(
                is_below,
                through_below[2 * n * v : 2 * n * (v + 1)],
                through_above[2 * n * v : 2 * n * (v + 1)],
            )
            for v in range(nvar)
        ]

    def transformed(values):
        return [
            [sum(half[d][v][w] * values[w] for w in range(nvar)) for v in range(nvar)] for d in range(2)
        ]

    def flux(normal, lower, lower_j, upper, upper_j):
        spread = 0.5 * (jnp.abs(normal[0]) + jnp.abs(normal[1]))
        return [
            normal[0] * (lower_j[0][v] + upper_j[0][v])
            + normal[1] * (lower_j[1][v] + upper_j[1][v])
            - spread * (upper[v] - lower[v])
            for v in range(nvar)
        ]

    def col_change(normal, values, values_j):
        left = [pltpu.roll(x, 1, 1) for x in values]
        left_j = [[pltpu.roll(x, 1, 1) for x in values_j[d]] for d in range(2)]
        across = flux(normal, left, left_j, values, values_j)
        return [pltpu.roll(x, columns - 1, 1) - x for x in across]

    def pick(mask, a, b):
        return [jnp.where(mask, x, y) for x, y in zip(a, b)]

    def spread_sum(x):
        total = None
        for j in range(n):
            factor = jnp.zeros(x.shape, jnp.float32)
            for k in range(n):
                factor = jnp.where(place == k, weights[k][j], factor)
            row = jnp.where(is_below, x[j : j + 1], x[n + j : n + j + 1])
            total = factor * row if total is None else total + factor * row
        return total

    row_index = lax.broadcasted_iota(jnp.int32, (rows, columns), 0)

    def plane(k, p):
        return bufs[k][pl.ds(p * rows, rows), :]

    inner = [halo[nvar + v] for v in range(nvar)]
    for iteration in range(iterations):
        final = iteration == iterations - 1

        def cells(k, v):
            return plane(k, v) if iteration == 0 else flow[iteration - 1, k, v]

        for k in range(n):
            for v in range(nvar):
                if iteration == 0:
                    rim[v, pl.ds(k, 1), :] = bufs[k][pl.ds(v * rows, 1), :]
                    rim[v, pl.ds(n + k, 1), :] = bufs[k][pl.ds(v * rows + rows - 1, 1), :]
                else:
                    rim[v, pl.ds(k, 1), :] = flow[iteration - 1, k, v, pl.ds(0, 1), :]
                    rim[v, pl.ds(n + k, 1), :] = flow[iteration - 1, k, v, pl.ds(rows - 1, 1), :]
        edge_rows = [rim[v] for v in range(nvar)]
        lower = crossed(pick(is_below, inner, edge_rows), False)
        upper = pick(is_below, edge_rows, inner)
        inner_face = [halo[2 * nvar + 5], halo[2 * nvar + 6]]
        flux_inner = flux(inner_face, lower, transformed(lower), upper, transformed(upper))
        flux_back = crossed(flux_inner, True)
        if not final:
            outer = [halo[v] for v in range(nvar)]
            low, high = pick(is_below, outer, inner), pick(is_below, inner, outer)
            outer_face = [halo[2 * nvar + 1], halo[2 * nvar + 2]]
            flux_outer = flux(outer_face, low, transformed(low), high, transformed(high))
            change = [
                jnp.where(is_below, flux_back[v] - flux_outer[v], flux_outer[v] - flux_inner[v])
                for v in range(nvar)
            ]
            inner_col = [halo[2 * nvar + 3], halo[2 * nvar + 4]]
            beside = col_change(inner_col, inner, transformed(inner))
            volume = halo[2 * nvar]
            inverse = 1.0 / volume
            volume_rate = spread_sum(volume)
            inner_next = [
                inner[v]
                - spread_sum(inner[v])
                - inverse * (inner[v] * volume_rate + pseudo_step * (change[v] + beside[v]))
                for v in range(nvar)
            ]
        for k in range(n):
            values = [cells(k, v) for v in range(nvar)]
            values_j = transformed(values)
            shifted = [pltpu.roll(x, 1, 0) for x in values]
            shifted_j = [[pltpu.roll(x, 1, 0) for x in values_j[d]] for d in range(2)]
            row_face = [plane(k, nvar + 1), plane(k, nvar + 2)]
            col_face = [plane(k, nvar + 3), plane(k, nvar + 4)]
            row_flux = flux(row_face, shifted, shifted_j, values, values_j)
            row_flux = [
                jnp.where(row_index == 0, flux_inner[v][k : k + 1], row_flux[v]) for v in range(nvar)
            ]
            row_above = [
                jnp.where(
                    row_index == rows - 1,
                    flux_back[v][n + k : n + k + 1],
                    pltpu.roll(row_flux[v], rows - 1, 0),
                )
                for v in range(nvar)
            ]
            beside = col_change(col_face, values, values_j)
            inverse = 1.0 / plane(k, nvar)
            volume_rate = sum(weights[k][j] * plane(j, nvar) for j in range(n))
            for v in range(nvar):
                time_rate = sum(weights[k][j] * cells(j, v) for j in range(n))
                change = pseudo_step * ((row_above[v] - row_flux[v]) + beside[v])
                moved = values[v] - time_rate - inverse * (values[v] * volume_rate + change)
                if final:
                    outs[k][v] = moved
                else:
                    flow[iteration, k, v] = moved
        if not final:
            inner = inner_next


def unpack_kernel(n, rows, *refs):
    blocks, out = refs[:n], refs[n]
    me = lax.axis_index("inst")
    for k in range(n):
        block = jnp.bitwise_xor(me, k)
        lo = pl.multiple_of(block * rows, rows)
        step = row_step(rows)
        for v in range(out.shape[1]):
            for r in range(0, rows, step):
                out[0, v, pl.ds(lo + r, step), :] = blocks[k][v, pl.ds(r, step), :]


def body(states, volumes, row_normals, col_normals, face_links, jacobians):
    n = lax.axis_size("inst")
    slabs = lax.axis_size("slab")
    _, nvar, depth, columns = states.shape
    rows = depth // n
    buffer_rows = (nvar + 5) * rows + 4 * nvar + 12
    edge_rows = -(-(2 * nvar + 8) // 8) * 8

    def f32(*shape):
        return jax.ShapeDtypeStruct(shape, jnp.float32)

    vmem = pl.BlockSpec(memory_space=pltpu.VMEM)
    smem = pl.BlockSpec(memory_space=pltpu.SMEM)

    packed = pl.pallas_call(
        functools.partial(pack_kernel, n, rows),
        out_shape=[f32(buffer_rows, columns)] * n + [f32(edge_rows, columns)] * n,
        in_specs=[vmem] * 5,
        out_specs=[vmem] * (2 * n),
        name="pack",
    )(states, volumes, row_normals, col_normals, face_links)
    sent, sent_edges = packed[:n], packed[n:]

    def swapped(x, k):
        return lax.ppermute(x, "inst", [(i, i ^ k) for i in range(n)])

    received = [sent[0]] + [swapped(sent[k], k) for k in range(1, n)]

    def to_edge(x, k):
        pairs = []
        for s in range(slabs):
            pairs.append((k * slabs + s, (s + 1) % slabs))
            pairs.append(((n - 1 - k) * slabs + s, (n - 1) * slabs + (s - 1) % slabs))
        return lax.ppermute(x, ("inst", "slab"), pairs)

    edges = [to_edge(sent_edges[k], k) for k in range(n)]

    results = pl.pallas_call(
        functools.partial(compute_kernel, n, rows, nvar, ITERS),
        out_shape=[f32(nvar, rows, columns)] * n,
        in_specs=[smem, smem, vmem] + [vmem] * (2 * n),
        out_specs=[vmem] * n,
        scratch_shapes=[
            pltpu.VMEM((2 * nvar + 7, 2 * n, columns), jnp.float32),
            pltpu.VMEM((nvar, 2 * n, columns), jnp.float32),
            pltpu.VMEM((ITERS - 1, n, nvar, rows, columns), jnp.float32),
        ],
        compiler_params=pltpu.CompilerParams(vmem_limit_bytes=32 * 1024 * 1024),
        name="iterate",
    )(spectral_table(n), jacobians, face_links, *received, *edges)

    returned = [results[0]] + [swapped(results[k], k) for k in range(1, n)]
    return pl.pallas_call(
        functools.partial(unpack_kernel, n, rows),
        out_shape=f32(1, nvar, depth, columns),
        in_specs=[vmem] * n,
        out_specs=vmem,
        name="unpack",
    )(*returned)


def solution(mesh):
    return jax.shard_map(
        body,
        mesh=mesh,
        in_specs=(
            P(("grp", "inst"), None, "slab", None),
            P(("grp", "inst"), "slab", None),
            P(("grp", "inst"), None, "slab", None),
            P(("grp", "inst"), None, "slab", None),
            P("slab", None),
            P(),
        ),
        out_specs=P(("grp", "inst"), None, "slab", None),
        check_vma=False,
    )
```

```python
import functools

import jax
import jax.numpy as jnp
import numpy as np
from jax import lax
from jax.experimental import pallas as pl
from jax.experimental.pallas import tpu as pltpu
from jax.sharding import PartitionSpec as P

frequency = 0.5
pseudo_step = 0.2
nyquist_damping = 0.25


def spectral_table(instances):
    offsets = np.arange(instances)[:, None] - np.arange(instances)[None, :]
    phases = np.pi * offsets / instances
    sine_safe = np.where(offsets == 0, 1.0, np.sin(phases))
    parity = np.where(offsets % 2 == 0, 1.0, -1.0)
    matrix = np.where(offsets == 0, 0.0, 0.5 * frequency * parity * np.cos(phases) / sine_safe)
    matrix = matrix + nyquist_damping * parity
    return jnp.asarray(matrix, jnp.float32)


def row_step(rows):
    return rows if rows % 8 == 0 else 1


def pack_kernel(n, rows, *refs):
    sources, bufs, upward, downward, own_links = refs[:5], refs[5 : 5 + n], refs[5 + n], refs[6 + n], refs[7 + n]
    held, sems = refs[8 + n : 13 + n], refs[13 + n]
    copies = [pltpu.make_async_copy(sources[a], held[a], sems.at[a]) for a in range(5)]
    for copy in copies:
        copy.start()
    for copy in copies:
        copy.wait()
    states, volumes, row_normals, col_normals, links = held
    nvar, depth = states.shape[1], states.shape[2]
    me = lax.axis_index("inst")

    def put(ref, at, row_below, row_in, row_outer):
        for v in range(nvar):
            ref[pl.ds(at + v, 1), :] = states[0, v, pl.ds(row_below, 1), :]
            ref[pl.ds(at + nvar + v, 1), :] = states[0, v, pl.ds(row_in, 1), :]
        at = at + 2 * nvar
        ref[pl.ds(at, 1), :] = volumes[0, pl.ds(row_in, 1), :]
        for d in range(2):
            ref[pl.ds(at + 1 + d, 1), :] = row_normals[0, d, pl.ds(row_outer, 1), :]
            ref[pl.ds(at + 3 + d, 1), :] = col_normals[0, d, pl.ds(row_in, 1), :]

    def put_inner(ref, at, row):
        for d in range(2):
            ref[pl.ds(at + d, 1), :] = row_normals[0, d, pl.ds(row, 1), :]

    for k in range(n):
        buf = bufs[k]
        block = jnp.bitwise_xor(me, k)
        lo = pl.multiple_of(block * rows, rows)
        step = row_step(rows)
        for r in range(0, rows, step):
            here = pl.ds(lo + r, step)
            for v in range(nvar):
                buf[pl.ds(v * rows + r, step), :] = states[0, v, here, :]
            buf[pl.ds(nvar * rows + r, step), :] = volumes[0, here, :]
            for d in range(2):
                buf[pl.ds((nvar + 1 + d) * rows + r, step), :] = row_normals[0, d, here, :]
                buf[pl.ds((nvar + 3 + d) * rows + r, step), :] = col_normals[0, d, here, :]
        at = (nvar + 5) * rows
        below_1, below_2 = jnp.maximum(lo - 1, 0), jnp.maximum(lo - 2, 0)
        above_1, above_2 = jnp.minimum(lo + rows, depth - 1), jnp.minimum(lo + rows + 1, depth - 1)
        put(buf, at, below_2, below_1, below_1)
        at += 2 * nvar + 5
        put(buf, at, above_2, above_1, above_2)
        put_inner(buf, at + 2 * nvar + 5, above_1)
    own_links[...] = links[...]
    put(upward, 0, depth - 2, depth - 1, depth - 1)
    put(downward, 0, 1, 0, 1)
    put_inner(downward, 2 * nvar + 5, 0)
    downward[pl.ds(2 * nvar + 7, 1), :] = links[...].astype(jnp.float32)


def edge_kernel(n, below, above, *outs):
    me = lax.axis_index("inst")
    for k in range(n):
        outs[k][...] = jnp.where(jnp.bitwise_xor(me, k) == 0, below[...], above[...])


def split_dot(x, onehot, transposed):
    high = x.astype(jnp.bfloat16)
    rest = x - high.astype(jnp.float32)
    middle = rest.astype(jnp.bfloat16)
    low = (rest - middle.astype(jnp.float32)).astype(jnp.bfloat16)
    count = x.shape[0]
    stacked = jnp.concatenate([high, middle, low], axis=0)
    out = lax.dot_general(
        stacked,
        onehot,
        (((1,), (1 if transposed else 0,)), ((), ())),
        preferred_element_type=jnp.float32,
    )
    return out[:count] + (out[count : 2 * count] + out[2 * count :])


def half_jacobians(jacobians, nvar):
    return [[[0.5 * jacobians[d, v, w] for w in range(nvar)] for v in range(nvar)] for d in range(2)]


def step_weights(table, n):
    me = lax.axis_index("inst")
    return [
        [pseudo_step * table[jnp.bitwise_xor(me, k), jnp.bitwise_xor(me, j)] for j in range(n)]
        for k in range(n)
    ]


def transformed(half, values):
    count = len(values)
    return [
        [sum(half[d][v][w] * values[w] for w in range(count)) for v in range(count)] for d in range(2)
    ]


def face_flux(normal, lower, lower_j, upper, upper_j):
    spread = 0.5 * (jnp.abs(normal[0]) + jnp.abs(normal[1]))
    return [
        normal[0] * (lower_j[0][v] + upper_j[0][v])
        + normal[1] * (lower_j[1][v] + upper_j[1][v])
        - spread * (upper[v] - lower[v])
        for v in range(len(lower))
    ]


def col_change(normal, values, values_j):
    columns = values[0].shape[1]
    left = [pltpu.roll(x, 1, 1) for x in values]
    left_j = [[pltpu.roll(x, 1, 1) for x in values_j[d]] for d in range(2)]
    across = face_flux(normal, left, left_j, values, values_j)
    return [pltpu.roll(x, columns - 1, 1) - x for x in across]


def advance_main(k, rows, half, weights, bufs, cells, first_flux, last_flux, store):
    n, nvar = len(bufs), len(half[0])
    columns = bufs[0].shape[1]
    row_index = lax.broadcasted_iota(jnp.int32, (rows, columns), 0)

    def plane(j, p):
        return bufs[j][pl.ds(p * rows, rows), :]

    values = [cells(k, v) for v in range(nvar)]
    values_j = transformed(half, values)
    shifted = [pltpu.roll(x, 1, 0) for x in values]
    shifted_j = [[pltpu.roll(x, 1, 0) for x in values_j[d]] for d in range(2)]
    row_flux = face_flux([plane(k, nvar + 1), plane(k, nvar + 2)], shifted, shifted_j, values, values_j)
    row_flux = [jnp.where(row_index == 0, first_flux(v), row_flux[v]) for v in range(nvar)]
    row_above = [
        jnp.where(row_index == rows - 1, last_flux(v), pltpu.roll(row_flux[v], rows - 1, 0))
        for v in range(nvar)
    ]
    beside = col_change([plane(k, nvar + 3), plane(k, nvar + 4)], values, values_j)
    inverse = 1.0 / plane(k, nvar)
    volume_rate = sum(weights[k][j] * plane(j, nvar) for j in range(n))
    for v in range(nvar):
        time_rate = sum(weights[k][j] * cells(j, v) for j in range(n))
        change = pseudo_step * ((row_above[v] - row_flux[v]) + beside[v])
        store(v, values[v] - time_rate - inverse * (values[v] * volume_rate + change))


def first_kernel(n, rows, nvar, table, jacobians, *refs):
    bufs, outs = refs[:n], refs[n:]
    half, weights = half_jacobians(jacobians, nvar), step_weights(table, n)

    def cells(k, v):
        return bufs[k][pl.ds(v * rows, rows), :]

    for k in range(n):

        def store(v, value):
            outs[k][v] = value

        advance_main(k, rows, half, weights, bufs, cells, lambda v: 0.0, lambda v: 0.0, store)


def second_kernel(n, rows, nvar, table, jacobians, links, *refs):
    bufs, edges, stepped, outs = refs[:n], refs[n : 2 * n], refs[2 * n : 3 * n], refs[3 * n : 4 * n]
    halo, rim, flow = refs[4 * n :]
    columns = links.shape[1]
    main = (nvar + 5) * rows
    below_at, above_at = main, main + 2 * nvar + 5
    me = lax.axis_index("inst")
    first, last = me == 0, me == n - 1
    half, weights = half_jacobians(jacobians, nvar), step_weights(table, n)

    for k in range(n):
        for t in range(2 * nvar + 5):
            halo[t, pl.ds(k, 1), :] = jnp.where(
                first, edges[k][pl.ds(t, 1), :], bufs[k][pl.ds(below_at + t, 1), :]
            )
        for t in range(2 * nvar + 7):
            halo[t, pl.ds(n + k, 1), :] = jnp.where(
                last, edges[k][pl.ds(t, 1), :], bufs[k][pl.ds(above_at + t, 1), :]
            )
        for d in range(2):
            halo[2 * nvar + 5 + d, pl.ds(k, 1), :] = bufs[k][pl.ds((nvar + 1 + d) * rows, 1), :]
        for v in range(nvar + 1):
            rim[v, pl.ds(k, 1), :] = bufs[k][pl.ds(v * rows, 1), :]
            rim[v, pl.ds(n + k, 1), :] = bufs[k][pl.ds(v * rows + rows - 1, 1), :]
        for v in range(nvar):
            flow[k, v] = stepped[k][v]

    own = lax.broadcasted_iota(jnp.int32, (1, columns), 1)
    cell = lax.broadcasted_iota(jnp.int32, (columns, columns), 0)
    links_above = edges[0][pl.ds(2 * nvar + 7, 1), :].astype(jnp.int32)
    onehot_below = (cell == jnp.where(first, links[...], own)).astype(jnp.float32).astype(jnp.bfloat16)
    onehot_above = (cell == jnp.where(last, links_above, own)).astype(jnp.float32).astype(jnp.bfloat16)
    side = lax.broadcasted_iota(jnp.int32, (2 * n, columns), 0)
    is_below = side < n
    place = jnp.where(is_below, side, side - n)

    def crossed(values, back):
        stacked = jnp.concatenate(values, axis=0)
        through_below = split_dot(stacked, onehot_below, back)
        through_above = split_dot(stacked, onehot_above, back)
        return [
            jnp.where(
                is_below,
                through_below[2 * n * v : 2 * n * (v + 1)],
                through_above[2 * n * v : 2 * n * (v + 1)],
            )
            for v in range(nvar)
        ]

    def pick(mask, a, b):
        return [jnp.where(mask, x, y) for x, y in zip(a, b)]

    factors = []
    for j in range(n):
        factor = jnp.zeros((2 * n, columns), jnp.float32)
        for k in range(n):
            factor = jnp.where(place == k, weights[k][j], factor)
        factors.append(factor)

    def spread_sum(x):
        return sum(
            factors[j] * jnp.where(is_below, x[j : j + 1], x[n + j : n + j + 1]) for j in range(n)
        )

    inner_face = [halo[2 * nvar + 5], halo[2 * nvar + 6]]

    def through_inner(inner, edge):
        lower = crossed(pick(is_below, inner, edge), False)
        upper = pick(is_below, edge, inner)
        across = face_flux(inner_face, lower, transformed(half, lower), upper, transformed(half, upper))
        return across, crossed(across, True)

    inner = [halo[nvar + v] for v in range(nvar)]
    flux_inner, flux_back = through_inner(inner, [rim[v] for v in range(nvar)])

    rim_inverse = pseudo_step / rim[nvar]
    for v in range(nvar):
        rim[v] = rim_inverse * jnp.where(is_below, flux_inner[v], -flux_back[v])
        for k in range(n):
            flow[k, v, pl.ds(0, 1), :] += rim[v, pl.ds(k, 1), :]
            flow[k, v, pl.ds(rows - 1, 1), :] += rim[v, pl.ds(n + k, 1), :]
            rim[v, pl.ds(k, 1), :] = flow[k, v, pl.ds(0, 1), :]
            rim[v, pl.ds(n + k, 1), :] = flow[k, v, pl.ds(rows - 1, 1), :]

    outer = [halo[v] for v in range(nvar)]
    low, high = pick(is_below, outer, inner), pick(is_below, inner, outer)
    outer_face = [halo[2 * nvar + 1], halo[2 * nvar + 2]]
    flux_outer = face_flux(outer_face, low, transformed(half, low), high, transformed(half, high))
    inner_col = [halo[2 * nvar + 3], halo[2 * nvar + 4]]
    beside = col_change(inner_col, inner, transformed(half, inner))
    volume = halo[2 * nvar]
    inverse = 1.0 / volume
    volume_rate = spread_sum(volume)
    stepped_inner = []
    for v in range(nvar):
        change = jnp.where(is_below, flux_back[v] - flux_outer[v], flux_outer[v] - flux_inner[v]) + beside[v]
        stepped_inner.append(
            inner[v] - spread_sum(inner[v]) - inverse * (inner[v] * volume_rate + pseudo_step * change)
        )
    flux_inner, flux_back = through_inner(stepped_inner, [rim[v] for v in range(nvar)])

    def cells(k, v):
        return flow[k, v]

    for k in range(n):

        def store(v, value):
            outs[k][v] = value

        advance_main(
            k,
            rows,
            half,
            weights,
            bufs,
            cells,
            lambda v: flux_inner[v][k : k + 1],
            lambda v: flux_back[v][n + k : n + k + 1],
            store,
        )


def unpack_kernel(n, rows, *refs):
    blocks, out = refs[:n], refs[n]
    me = lax.axis_index("inst")
    for k in range(n):
        block = jnp.bitwise_xor(me, k)
        lo = pl.multiple_of(block * rows, rows)
        step = row_step(rows)
        for v in range(out.shape[1]):
            for r in range(0, rows, step):
                out[0, v, pl.ds(lo + r, step), :] = blocks[k][v, pl.ds(r, step), :]


def body(states, volumes, row_normals, col_normals, face_links, jacobians):
    n = lax.axis_size("inst")
    slabs = lax.axis_size("slab")
    _, nvar, depth, columns = states.shape
    rows = depth // n
    buffer_rows = (nvar + 5) * rows + 4 * nvar + 12
    edge_rows = -(-(2 * nvar + 8) // 8) * 8

    def f32(*shape):
        return jax.ShapeDtypeStruct(shape, jnp.float32)

    params = pltpu.CompilerParams(vmem_limit_bytes=24 * 1024 * 1024)
    vmem = pl.BlockSpec(memory_space=pltpu.VMEM)
    smem = pl.BlockSpec(memory_space=pltpu.SMEM)

    inputs = [
        pltpu.with_memory_space_constraint(x, pltpu.HBM)
        for x in (states, volumes, row_normals, col_normals, face_links)
    ]
    packed = pl.pallas_call(
        functools.partial(pack_kernel, n, rows),
        out_shape=[f32(buffer_rows, columns)] * n + [f32(edge_rows, columns)] * 2
        + [jax.ShapeDtypeStruct(face_links.shape, face_links.dtype)],
        in_specs=[pl.BlockSpec(memory_space=pltpu.HBM)] * 5,
        out_specs=[vmem] * (n + 3),
        scratch_shapes=[pltpu.VMEM(x.shape, x.dtype) for x in inputs] + [pltpu.SemaphoreType.DMA((5,))],
        compiler_params=params,
        name="pack",
    )(*inputs)
    sent, (upward, downward, own_links) = packed[:n], packed[n:]

    def swapped(x, k):
        return lax.ppermute(x, "inst", [(i, i ^ k) for i in range(n)])

    received = [sent[0]] + [swapped(sent[k], k) for k in range(1, n)]
    from_below = lax.ppermute(upward, "slab", [(i, (i + 1) % slabs) for i in range(slabs)])
    from_above = lax.ppermute(downward, "slab", [(i, (i - 1) % slabs) for i in range(slabs)])
    edges = pl.pallas_call(
        functools.partial(edge_kernel, n),
        out_shape=[f32(edge_rows, columns)] * n,
        in_specs=[vmem] * 2,
        out_specs=[vmem] * n,
        compiler_params=params,
        name="edges",
    )(from_below, from_above)
    edges = [edges[0]] + [swapped(edges[k], k) for k in range(1, n)]

    table = spectral_table(n)
    stepped = pl.pallas_call(
        functools.partial(first_kernel, n, rows, nvar),
        out_shape=[f32(nvar, rows, columns)] * n,
        in_specs=[smem, smem] + [vmem] * n,
        out_specs=[vmem] * n,
        compiler_params=params,
        name="first",
    )(table, jacobians, *received)
    results = pl.pallas_call(
        functools.partial(second_kernel, n, rows, nvar),
        out_shape=[f32(nvar, rows, columns)] * n,
        in_specs=[smem, smem, vmem] + [vmem] * (3 * n),
        out_specs=[vmem] * n,
        scratch_shapes=[
            pltpu.VMEM((2 * nvar + 7, 2 * n, columns), jnp.float32),
            pltpu.VMEM((nvar + 1, 2 * n, columns), jnp.float32),
            pltpu.VMEM((n, nvar, rows, columns), jnp.float32),
        ],
        compiler_params=params,
        name="second",
    )(table, jacobians, own_links, *received, *edges, *stepped)

    returned = [results[0]] + [swapped(results[k], k) for k in range(1, n)]
    return pl.pallas_call(
        functools.partial(unpack_kernel, n, rows),
        out_shape=f32(1, nvar, depth, columns),
        in_specs=[vmem] * n,
        out_specs=vmem,
        compiler_params=params,
        name="unpack",
    )(*returned)


def solution(mesh):
    return jax.shard_map(
        body,
        mesh=mesh,
        in_specs=(
            P(("grp", "inst"), None, "slab", None),
            P(("grp", "inst"), "slab", None),
            P(("grp", "inst"), None, "slab", None),
            P(("grp", "inst"), None, "slab", None),
            P("slab", None),
            P(),
        ),
        out_specs=P(("grp", "inst"), None, "slab", None),
        check_vma=False,
    )
```

```python
import functools

import jax
import jax.numpy as jnp
import numpy as np
from jax import lax
from jax.experimental import pallas as pl
from jax.experimental.pallas import tpu as pltpu
from jax.sharding import PartitionSpec as P

frequency = 0.5
pseudo_step = 0.2
nyquist_damping = 0.25

STRIP = 8


def spectral_table(instances):
    offsets = np.arange(instances)[:, None] - np.arange(instances)[None, :]
    phases = np.pi * offsets / instances
    sine_safe = np.where(offsets == 0, 1.0, np.sin(phases))
    parity = np.where(offsets % 2 == 0, 1.0, -1.0)
    matrix = np.where(offsets == 0, 0.0, 0.5 * frequency * parity * np.cos(phases) / sine_safe)
    matrix = matrix + nyquist_damping * parity
    return jnp.asarray(matrix, jnp.float32)


def pack_kernel(states, volumes, row_normals, col_normals, links, near, cell, rows, own_links, upward, downward, sems):
    nvar, depth = states.shape[1], states.shape[2]
    pairs = [
        (states.at[0], near.at[pl.ds(0, nvar)]),
        (volumes, near.at[pl.ds(nvar, 1)]),
        (volumes, cell.at[pl.ds(0, 1)]),
        (col_normals.at[0], cell.at[pl.ds(1, 2)]),
        (row_normals.at[0], rows),
        (links, own_links),
    ]
    copies = [pltpu.make_async_copy(a, b, sems.at[t]) for t, (a, b) in enumerate(pairs)]
    for copy in copies:
        copy.start()
    for copy in copies:
        copy.wait()

    def put(ref, second, edge, face):
        for v in range(nvar):
            ref[pl.ds(v, 1), :] = near[v, pl.ds(second, 1), :]
            ref[pl.ds(nvar + v, 1), :] = near[v, pl.ds(edge, 1), :]
        ref[pl.ds(2 * nvar, 1), :] = near[nvar, pl.ds(edge, 1), :]
        for d in range(2):
            ref[pl.ds(2 * nvar + 1 + d, 1), :] = rows[d, pl.ds(face, 1), :]
            ref[pl.ds(2 * nvar + 3 + d, 1), :] = cell[1 + d, pl.ds(edge, 1), :]

    put(upward, depth - 2, depth - 1, depth - 1)
    put(downward, 1, 0, 1)
    for d in range(2):
        downward[pl.ds(2 * nvar + 5 + d, 1), :] = rows[d, pl.ds(0, 1), :]
    downward[pl.ds(2 * nvar + 7, 1), :] = own_links[...].astype(jnp.float32)


def half_jacobians(jacobians, nvar):
    return [[[0.5 * jacobians[d, v, w] for w in range(nvar)] for v in range(nvar)] for d in range(2)]


def step_weight(table, row, col):
    me = lax.axis_index("inst")
    return pseudo_step * table[jnp.bitwise_xor(me, row), jnp.bitwise_xor(me, col)]


def weighted(weights, values):
    total = weights[0] * values[0]
    for weight, value in zip(weights[1:], values[1:]):
        total = total + weight * value
    return total


def transformed(half, values):
    return [[weighted(half[d][v], values) for v in range(len(values))] for d in range(2)]


def spread_of(normal):
    return 0.5 * (jnp.abs(normal[0]) + jnp.abs(normal[1]))


def own_side(normal, values, values_j):
    spread = spread_of(normal)
    return [
        normal[0] * values_j[0][v] + normal[1] * values_j[1][v] - spread * values[v]
        for v in range(len(values))
    ]


def other_side(normal, values, values_j):
    spread = spread_of(normal)
    return [
        normal[0] * values_j[0][v] + normal[1] * values_j[1][v] + spread * values[v]
        for v in range(len(values))
    ]


def col_change(normal, values, values_j):
    columns = values[0].shape[1]
    upper_normal = [pltpu.roll(x, columns - 1, 1) for x in normal]
    own = own_side(normal, values, values_j)
    other = other_side(upper_normal, values, values_j)
    flux = [a + pltpu.roll(b, 1, 1) for a, b in zip(own, other)]
    return [pltpu.roll(x, columns - 1, 1) - x for x in flux]


def row_changes(count, at, first_flux, last_flux):
    last = None
    ahead = at(0)
    for s in range(count):
        faces, cells, cells_j = ahead
        nvar = len(cells)
        row = lax.broadcasted_iota(jnp.int32, cells[0].shape, 0)
        top, bottom = row == 0, row == STRIP - 1
        rolled_faces = [pltpu.roll(x, STRIP - 1, 0) for x in faces]
        if s + 1 < count:
            ahead = at(s + 1)
            rolled_faces = [
                jnp.where(bottom, pltpu.roll(x, STRIP - 1, 0), y) for x, y in zip(ahead[0], rolled_faces)
            ]
        own = own_side(faces, cells, cells_j)
        rolled = [pltpu.roll(x, 1, 0) for x in other_side(rolled_faces, cells, cells_j)]
        if s == 0:
            flux = [jnp.where(top, first_flux(v), own[v] + rolled[v]) for v in range(nvar)]
        else:
            flux = [own[v] + jnp.where(top, before[v], rolled[v]) for v in range(nvar)]
        lifted = [pltpu.roll(x, STRIP - 1, 0) for x in flux]
        if last is not None:
            yield (
                s - 1,
                last[0],
                last[1],
                [jnp.where(bottom, lifted[v], last[3][v]) - last[2][v] for v in range(nvar)],
            )
        before, last = rolled, (cells, cells_j, flux, lifted)
    yield (
        count - 1,
        last[0],
        last[1],
        [jnp.where(bottom, last_flux(v), last[3][v]) - last[2][v] for v in range(nvar)],
    )


def strip(s):
    return pl.ds(s * STRIP, STRIP)


def face_flux(normal, lower, lower_j, upper, upper_j):
    spread = spread_of(normal)
    return [
        normal[0] * (lower_j[0][v] + upper_j[0][v])
        + normal[1] * (lower_j[1][v] + upper_j[1][v])
        - spread * (upper[v] - lower[v])
        for v in range(len(lower))
    ]


def split_dot(x, onehot, transposed):
    high = x.astype(jnp.bfloat16)
    rest = x - high.astype(jnp.float32)
    middle = rest.astype(jnp.bfloat16)
    low = (rest - middle.astype(jnp.float32)).astype(jnp.bfloat16)
    count = x.shape[0]
    stacked = jnp.concatenate([high, middle, low], axis=0)
    out = lax.dot_general(
        stacked,
        onehot,
        (((1,), (1 if transposed else 0,)), ((), ())),
        preferred_element_type=jnp.float32,
    )
    return out[:count] + (out[count : 2 * count] + out[2 * count :])


def pair(below, above):
    return jnp.concatenate([below, above], axis=0)


def pick(mask, a, b):
    return [jnp.where(mask, x, y) for x, y in zip(a, b)]


def pick_both(mask, a, b):
    return pick(mask, a[0], b[0]), [pick(mask, x, y) for x, y in zip(a[1], b[1])]


def behind(below, above, t):
    return pair(below[pl.ds(t, 1), :], above[pl.ds(t, 1), :])


def crossed(rows, links_below, links_above, stack):
    stack[...] = jnp.zeros(stack.shape, jnp.float32)
    for t, x in enumerate(rows):
        stack[pl.ds(2 * t, 2), :] = x
    columns = stack.shape[1]
    cell = lax.broadcasted_iota(jnp.int32, (columns, columns), 0)
    onehots = [(cell == x).astype(jnp.float32).astype(jnp.bfloat16) for x in (links_below, links_above)]
    stacked = stack[...]
    side = lax.broadcasted_iota(jnp.int32, stacked.shape, 0) % 2
    stack[...] = jnp.where(
        side == 0, split_dot(stacked, onehots[0], False), split_dot(stacked, onehots[1], True)
    )
    return [stack[pl.ds(2 * t, 2), :] for t in range(len(rows))]


def edge_kernel(nvar, jacobians, below, above, near, row_normals, links, early, out, kept, stack):
    depth, columns = near.shape[1], near.shape[2]
    half = half_jacobians(jacobians, nvar)
    is_below = lax.broadcasted_iota(jnp.int32, (2, columns), 0) == 0
    inner_face = [
        pair(row_normals[d, pl.ds(0, 1), :], above[pl.ds(2 * nvar + 5 + d, 1), :]) for d in range(2)
    ]
    rows = [behind(below, above, nvar + v) for v in range(nvar + 1)] + inner_face
    links_above = above[pl.ds(2 * nvar + 7, 1), :].astype(jnp.int32)
    rows = crossed(rows, links[...], links_above, stack)
    rim, volume, face = rows[:nvar], rows[nvar], pick(is_below, inner_face, rows[nvar + 1 :])
    inside = [pair(near[v, pl.ds(0, 1), :], near[v, pl.ds(depth - 1, 1), :]) for v in range(nvar)]
    low, high = pick(is_below, rim, inside), pick(is_below, inside, rim)
    summed = transformed(half, [x + y for x, y in zip(low, high)])
    spread = spread_of(face)
    across = [
        face[0] * summed[0][v] + face[1] * summed[1][v] - spread * (high[v] - low[v]) for v in range(nvar)
    ]
    at = 2 * nvar
    for v in range(nvar):
        out[pl.ds(v, 1), :] = across[v][0:1]
        out[pl.ds(nvar + v, 1), :] = across[v][1:2]
        kept[v] = rim[v]
        kept[nvar + v] = jnp.where(is_below, across[v], -across[v])
    for v, x in enumerate(rim + [volume]):
        out[pl.ds(at + v, 1), :] = x[0:1]
        out[pl.ds(at + nvar + 1 + v, 1), :] = x[1:2]
    kept[2 * nvar] = volume
    for d in range(2):
        kept[2 * nvar + 1 + d] = face[d]
    head = out.shape[0] - 2 * depth
    for d in range(2):
        out[pl.ds(head + d * depth, depth), :] = row_normals[d]


def behind_kernel(nvar, jacobians, below, above, links, out, stack):
    half = half_jacobians(jacobians, nvar)
    is_below = lax.broadcasted_iota(jnp.int32, (2, links.shape[1]), 0) == 0

    def with_j(values):
        return values, transformed(half, values)

    outer, rim = [with_j([behind(below, above, t + v) for v in range(nvar)]) for t in (0, nvar)]
    low, high = pick_both(is_below, outer, rim), pick_both(is_below, rim, outer)
    at = 2 * nvar + 1
    far_flux = face_flux([behind(below, above, at + d) for d in range(2)], *low, *high)
    beside = col_change([behind(below, above, at + 2 + d) for d in range(2)], *rim)
    rows = [jnp.where(is_below, -x, x) + y for x, y in zip(far_flux, beside)]
    links_above = above[pl.ds(2 * nvar + 7, 1), :].astype(jnp.int32)
    for v, x in enumerate(crossed(rows, links[...], links_above, stack)):
        out[v] = x


def state_kernel(states, before, *outs):
    at = 0
    for out in outs:
        out[...] = states[0, pl.ds(at, out.shape[0])]
        at += out.shape[0]


def volume_kernel(cells, before, out):
    out[...] = cells[pl.ds(0, 1)]


def own_flux_kernel(nvar, jacobians, near, cell, row_normals, out):
    strips = out.shape[1] // STRIP
    half = half_jacobians(jacobians, nvar)

    def at(s):
        cells = [near[v, strip(s), :] for v in range(nvar)]
        return [row_normals[d, strip(s), :] for d in range(2)], cells, transformed(half, cells)

    for s, cells, cells_j, along in row_changes(strips, at, lambda v: 0.0, lambda v: 0.0):
        beside = col_change([cell[1 + d, strip(s), :] for d in range(2)], cells, cells_j)
        factor = pseudo_step / cell[0, strip(s), :]
        for v in range(nvar):
            out[v, strip(s), :] = cells[v] - factor * (along[v] + beside[v])


def far_col_kernel(nvar, jacobians, states, cell, out, out_j):
    strips = out.shape[1] // STRIP
    half = half_jacobians(jacobians, nvar)
    for s in range(strips):
        cells = [states[0, v, strip(s), :] for v in range(nvar)]
        cells_j = transformed(half, cells)
        beside = col_change([cell[1 + d, strip(s), :] for d in range(2)], cells, cells_j)
        factor = pseudo_step / cell[0, strip(s), :]
        for v in range(nvar):
            out[v, strip(s), :] = cells[v] - factor * beside[v]
            for d in range(2):
                out_j[d, v, strip(s), :] = cells_j[d][v]


def time_kernel(n, nvar, table, near, beyond, edge, *refs):
    far = n // 2 - 1
    states, cells, *pieces, beyond_volumes = [refs[far * t : far * (t + 1)] for t in range(5)]
    parts, outs = refs[5 * far : 6 * far + 1], refs[6 * far + 1 :]
    beyond_states = [[x.at[v] for x in piece for v in range(x.shape[0])] for piece in zip(*pieces)]
    count = far + 1
    weights = [
        [step_weight(table, 2 * a, 2 * b) for b in range(count)]
        + [step_weight(table, 2 * a, 2 * b + 1) for b in range(count)]
        for a in range(count)
    ]
    strips = outs[0].shape[1] // STRIP
    row = lax.broadcasted_iota(jnp.int32, (STRIP, near.shape[2]), 0)
    for s in range(strips):
        here = [near[nvar, strip(s), :]] + [x[0, strip(s), :] for x in cells]
        sizes = here + [beyond[nvar, strip(s), :]] + [x[0, strip(s), :] for x in beyond_volumes]
        factors = [weighted(weights[a], sizes) / here[a] for a in range(count)]
        for v in range(nvar):
            values = [near[v, strip(s), :]] + [x[0, v, strip(s), :] for x in states]
            values = values + [beyond[v, strip(s), :]] + [x[v][strip(s), :] for x in beyond_states]
            moved = [
                parts[a][v, strip(s), :] - weighted(weights[a], values) - factors[a] * values[a]
                for a in range(count)
            ]
            if s == 0:
                moved[0] = moved[0] + jnp.where(row == 0, pseudo_step * edge[pl.ds(v, 1), :], 0.0) / here[0]
            if s == strips - 1:
                lacking = jnp.where(row == STRIP - 1, pseudo_step * edge[pl.ds(nvar + v, 1), :], 0.0)
                moved[0] = moved[0] - lacking / here[0]
            for a in range(count):
                outs[a][v, strip(s), :] = moved[a]


def base_kernel(n, nvar, table, jacobians, stepped, near, beyond, cell, row_normals, *refs):
    far = n // 2 - 1
    cells_of, beyond_volumes, out = refs[:far], refs[far : 2 * far], refs[2 * far]
    strips = out.shape[1] // STRIP
    half = half_jacobians(jacobians, nvar)
    weights = [step_weight(table, 0, 2 * b) for b in range(far + 1)]
    weights = weights + [step_weight(table, 0, 2 * b + 1) for b in range(far + 1)]

    def at(s):
        cells = [stepped[v, strip(s), :] for v in range(nvar)]
        return [row_normals[d, strip(s), :] for d in range(2)], cells, transformed(half, cells)

    for s, cells, cells_j, along in row_changes(strips, at, lambda v: 0.0, lambda v: 0.0):
        beside = col_change([cell[1 + d, strip(s), :] for d in range(2)], cells, cells_j)
        sizes = [near[nvar, strip(s), :]] + [x[0, strip(s), :] for x in cells_of]
        sizes = sizes + [beyond[nvar, strip(s), :]] + [x[0, strip(s), :] for x in beyond_volumes]
        inverse = 1.0 / sizes[0]
        kept = (1.0 - weights[0]) - inverse * weighted(weights, sizes)
        for v in range(nvar):
            out[v, strip(s), :] = kept * cells[v] - (pseudo_step * inverse) * (along[v] + beside[v])


def far_step_kernel(n, nvar, table, stepped, base, edge, *refs):
    far = n // 2 - 1
    edges, states, cells_of, parts, transforms = [refs[far * t : far * (t + 1)] for t in range(5)]
    shared, out = refs[5 * far :]
    depth = stepped.shape[1]
    strips = depth // STRIP
    mine = [step_weight(table, 0, 2 * b) for b in range(far + 1)]
    other = [step_weight(table, 1, 2 * b) for b in range(far + 1)]
    head = edge.shape[0] - 2 * depth

    def changes(a):
        def at(s):
            faces = [edges[a][pl.ds(head + d * depth + s * STRIP, STRIP), :] for d in range(2)]
            cells = [states[a][0, v, strip(s), :] for v in range(nvar)]
            return faces, cells, [[transforms[a][d, v, strip(s), :] for v in range(nvar)] for d in range(2)]

        return row_changes(
            strips, at, lambda v: edges[a][pl.ds(v, 1), :], lambda v: edges[a][pl.ds(nvar + v, 1), :]
        )

    for moves in zip(*[changes(a) for a in range(far)]):
        s = moves[0][0]
        factors = [pseudo_step / cells_of[a][0, strip(s), :] for a in range(far)]
        for v in range(nvar):
            given = other[0] * stepped[v, strip(s), :]
            taken = base[v, strip(s), :]
            for a in range(far):
                value = parts[a][v, strip(s), :] - factors[a] * moves[a][3][v]
                given = given + other[1 + a] * value
                taken = taken - mine[1 + a] * value
            shared[pl.ds(v * depth + s * STRIP, STRIP), :] = given
            out[v, strip(s), :] = taken
    rims = pl.ds(2 * nvar, 2 * nvar + 2)
    shared[pl.ds(nvar * depth, 2 * nvar + 2), :] = weighted(
        other, [edge[rims, :]] + [edges[a][rims, :] for a in range(far)]
    )


def rim_kernel(n, nvar, table, jacobians, edge, kept, others, near, stepped, *refs):
    far = n // 2 - 1
    edges, out = refs[:far], refs[far]
    depth, columns = stepped.shape[1], stepped.shape[2]
    half = half_jacobians(jacobians, nvar)
    weights = [step_weight(table, 0, 2 * b) for b in range(far + 1)]
    is_below = lax.broadcasted_iota(jnp.int32, (2, columns), 0) == 0
    at = 2 * nvar

    def rim(v):
        return weighted(
            weights,
            [
                pair(ref[pl.ds(at + v, 1), :], ref[pl.ds(at + nvar + 1 + v, 1), :])
                for ref in [edge] + list(edges)
            ],
        )

    inverse = 1.0 / kept[2 * nvar]
    volume_rate = rim(nvar)
    face = [kept[2 * nvar + 1], kept[2 * nvar + 2]]
    spread = spread_of(face)
    inside = [pair(stepped[v, pl.ds(0, 1), :], stepped[v, pl.ds(depth - 1, 1), :]) for v in range(nvar)]
    inside_j = transformed(half, inside)
    for v in range(nvar):
        change = pseudo_step * (kept[nvar + v] + others[v])
        out[v] = kept[v] - rim(v) - inverse * (kept[v] * volume_rate + change)
        out[nvar + v] = inverse * kept[v]
        out[2 * nvar + v] = (
            face[0] * inside_j[0][v]
            + face[1] * inside_j[1][v]
            + jnp.where(is_below, -spread, spread) * inside[v]
        )
    volume = pair(near[nvar, pl.ds(0, 1), :], near[nvar, pl.ds(depth - 1, 1), :])
    factor = pseudo_step / volume
    out[3 * nvar] = jnp.where(is_below, factor, -factor)


def final_kernel(nvar, jacobians, rims, kept, base, shared, out, held, sems):
    depth, columns = base.shape[1], base.shape[2]
    strips = depth // STRIP
    half = half_jacobians(jacobians, nvar)
    is_below = lax.broadcasted_iota(jnp.int32, (2, columns), 0) == 0

    def summed(v):
        return pair(shared[pl.ds(nvar * depth + v, 1), :], shared[pl.ds(nvar * depth + nvar + 1 + v, 1), :])

    def value(v, s):
        return base[v, strip(s), :] - shared[pl.ds(v * depth + s * STRIP, STRIP), :]

    copies = []

    def send(t, first, count):
        where = pl.ds(first * STRIP, count * STRIP)
        copies.append(pltpu.make_async_copy(held.at[:, where], out.at[0, :, where], sems.at[t]))
        copies[-1].start()

    for s in range(1, strips - 1):
        for v in range(nvar):
            held[v, strip(s), :] = value(v, s)
    send(0, 1, strips - 2)
    volume_rate = summed(nvar)
    outside = [rims[v] - summed(v) - rims[nvar + v] * volume_rate for v in range(nvar)]
    outside_j = transformed(half, outside)
    face = [kept[2 * nvar + 1], kept[2 * nvar + 2]]
    spread = spread_of(face)
    signed = jnp.where(is_below, spread, -spread)
    row = lax.broadcasted_iota(jnp.int32, (STRIP, columns), 0)
    for v in range(nvar):
        across = face[0] * outside_j[0][v] + face[1] * outside_j[1][v] + signed * outside[v]
        lacking = rims[3 * nvar] * (across + rims[2 * nvar + v])
        held[v, strip(0), :] = value(v, 0) + jnp.where(row == 0, lacking[0:1], 0.0)
        held[v, strip(strips - 1), :] = value(v, strips - 1) + jnp.where(
            row == STRIP - 1, lacking[1:2], 0.0
        )
    send(1, 0, 1)
    send(2, strips - 1, 1)
    for copy in copies:
        copy.wait()


def body(states, volumes, row_normals, col_normals, face_links, jacobians):
    n = lax.axis_size("inst")
    slabs = lax.axis_size("slab")
    _, nvar, depth, columns = states.shape
    far = list(range(2, n, 2))
    down_rows = -(-(2 * nvar + 8) // 8) * 8
    up_rows = down_rows + 8
    head = -(-(4 * nvar + 2) // 8) * 8

    def f32(*shape):
        return jax.ShapeDtypeStruct(shape, jnp.float32)

    vmem = pl.BlockSpec(memory_space=pltpu.VMEM)
    smem = pl.BlockSpec(memory_space=pltpu.SMEM)
    hbm = pl.BlockSpec(memory_space=pltpu.HBM)
    params = pltpu.CompilerParams(vmem_limit_bytes=24 * 1024 * 1024)
    table = spectral_table(n)

    def call(kernel, name, shapes, *operands, scratch=(), out_spec=vmem):
        single = not isinstance(shapes, list)
        return pl.pallas_call(
            kernel,
            out_shape=shapes,
            in_specs=[smem if x is table or x is jacobians else vmem for x in operands],
            out_specs=out_spec if single else [out_spec] * len(shapes),
            scratch_shapes=list(scratch),
            compiler_params=params,
            name=name,
        )(*operands)

    def swapped(x, k):
        return lax.ppermute(x, "inst", [(i, i ^ k) for i in range(n)])

    state_of = {k: swapped(states, k) for k in far}
    inputs = [
        pltpu.with_memory_space_constraint(x, pltpu.HBM)
        for x in (states, volumes, row_normals, col_normals, face_links)
    ]
    near, own_cell, own_rows, own_links, upward, downward = pl.pallas_call(
        pack_kernel,
        out_shape=[
            f32(nvar + 1, depth, columns),
            f32(3, depth, columns),
            f32(2, depth, columns),
            jax.ShapeDtypeStruct(face_links.shape, face_links.dtype),
            f32(up_rows, columns),
            f32(down_rows, columns),
        ],
        in_specs=[hbm] * 5,
        out_specs=[vmem] * 6,
        scratch_shapes=[pltpu.SemaphoreType.DMA((6,))],
        compiler_params=params,
        name="pack",
    )(*inputs)
    cell_of = {k: swapped(own_cell, k) for k in far}
    below = lax.ppermute(upward, "slab", [(i, (i + 1) % slabs) for i in range(slabs)])
    above = lax.ppermute(downward, "slab", [(i, (i - 1) % slabs) for i in range(slabs)])
    field = f32(nvar, depth, columns)
    parts = [
        call(functools.partial(own_flux_kernel, nvar), "own_flux", field, jacobians, near, own_cell, own_rows)
    ]
    edge, kept = call(
        functools.partial(edge_kernel, nvar),
        "edges",
        [f32(head + 2 * depth, columns), f32(2 * nvar + 3, 2, columns)],
        jacobians,
        below,
        above,
        near,
        own_rows,
        own_links,
        parts[0],
        scratch=[pltpu.VMEM((-(-(2 * nvar + 6) // 8) * 8, columns), jnp.float32)],
    )
    others = call(
        functools.partial(behind_kernel, nvar),
        "behind",
        f32(nvar, 2, columns),
        jacobians,
        below,
        above,
        own_links,
        scratch=[pltpu.VMEM((-(-2 * nvar // 8) * 8, columns), jnp.float32)],
    )
    edge_of = {k: swapped(edge, k) for k in far}
    beyond = swapped(near, 1)
    pieces = [f32(count, depth, columns) for count in (nvar - nvar // 2, nvar // 2)]
    beyond_states = []
    for k in far:
        beyond_states.append([swapped(x, 1) for x in call(state_kernel, "states", pieces, state_of[k], edge)])
    beyond_volumes = {
        k: swapped(call(volume_kernel, "volumes", f32(1, depth, columns), cell_of[k], others), 1) for k in far
    }

    transforms = {}
    for k in far:
        part, transforms[k] = call(
            functools.partial(far_col_kernel, nvar),
            "far_col",
            [field, f32(2, nvar, depth, columns)],
            jacobians,
            state_of[k],
            cell_of[k],
        )
        parts.append(part)
    stepped, *parts = call(
        functools.partial(time_kernel, n, nvar),
        "time",
        [field] * (len(far) + 1),
        table,
        near,
        beyond,
        edge,
        *[state_of[k] for k in far],
        *[cell_of[k] for k in far],
        *[x[0] for x in beyond_states],
        *[x[1] for x in beyond_states],
        *[beyond_volumes[k] for k in far],
        *parts,
    )
    base = call(
        functools.partial(base_kernel, n, nvar),
        "base",
        field,
        table,
        jacobians,
        stepped,
        near,
        beyond,
        own_cell,
        own_rows,
        *[cell_of[k] for k in far],
        *[beyond_volumes[k] for k in far],
    )
    shared, base = call(
        functools.partial(far_step_kernel, n, nvar),
        "far_step",
        [f32(nvar * depth + 16, columns), field],
        table,
        stepped,
        base,
        edge,
        *[edge_of[k] for k in far],
        *[state_of[k] for k in far],
        *[cell_of[k] for k in far],
        *parts,
        *[transforms[k] for k in far],
    )
    rims = call(
        functools.partial(rim_kernel, n, nvar),
        "rims",
        f32(3 * nvar + 1, 2, columns),
        table,
        jacobians,
        edge,
        kept,
        others,
        near,
        stepped,
        *[edge_of[k] for k in far],
    )
    return call(
        functools.partial(final_kernel, nvar),
        "final",
        f32(1, nvar, depth, columns),
        jacobians,
        rims,
        kept,
        base,
        swapped(shared, 1),
        scratch=[pltpu.VMEM((nvar, depth, columns), jnp.float32), pltpu.SemaphoreType.DMA((3,))],
        out_spec=hbm,
    )


def solution(mesh):
    return jax.shard_map(
        body,
        mesh=mesh,
        in_specs=(
            P(("grp", "inst"), None, "slab", None),
            P(("grp", "inst"), "slab", None),
            P(("grp", "inst"), None, "slab", None),
            P(("grp", "inst"), None, "slab", None),
            P("slab", None),
            P(),
        ),
        out_specs=P(("grp", "inst"), None, "slab", None),
        check_vma=False,
    )
```

```python
import functools

import jax
import jax.numpy as jnp
import numpy as np
from jax import lax
from jax.experimental import pallas as pl
from jax.experimental.pallas import tpu as pltpu
from jax.sharding import PartitionSpec as P

frequency = 0.5
pseudo_step = 0.2
nyquist_damping = 0.25

STRIP = 8


def spectral_table(instances):
    offsets = np.arange(instances)[:, None] - np.arange(instances)[None, :]
    phases = np.pi * offsets / instances
    sine_safe = np.where(offsets == 0, 1.0, np.sin(phases))
    parity = np.where(offsets % 2 == 0, 1.0, -1.0)
    matrix = np.where(offsets == 0, 0.0, 0.5 * frequency * parity * np.cos(phases) / sine_safe)
    matrix = matrix + nyquist_damping * parity
    return matrix.astype(np.float32)


def pack_kernel(states, volumes, row_normals, col_normals, links, near, cell, rows, own_links, upward, downward, sems):
    nvar, depth = states.shape[1], states.shape[2]
    pairs = [
        (states.at[0], near.at[pl.ds(0, nvar)]),
        (volumes, near.at[pl.ds(nvar, 1)]),
        (volumes, cell.at[pl.ds(0, 1)]),
        (col_normals.at[0], cell.at[pl.ds(1, 2)]),
        (row_normals.at[0], rows),
        (links, own_links),
    ]
    copies = [pltpu.make_async_copy(a, b, sems.at[t]) for t, (a, b) in enumerate(pairs)]
    for copy in copies:
        copy.start()
    for copy in copies:
        copy.wait()

    def put(ref, second, edge, face):
        for v in range(nvar):
            ref[pl.ds(v, 1), :] = near[v, pl.ds(second, 1), :]
            ref[pl.ds(nvar + v, 1), :] = near[v, pl.ds(edge, 1), :]
        ref[pl.ds(2 * nvar, 1), :] = near[nvar, pl.ds(edge, 1), :]
        for d in range(2):
            ref[pl.ds(2 * nvar + 1 + d, 1), :] = rows[d, pl.ds(face, 1), :]
            ref[pl.ds(2 * nvar + 3 + d, 1), :] = cell[1 + d, pl.ds(edge, 1), :]

    put(upward, depth - 2, depth - 1, depth - 1)
    put(downward, 1, 0, 1)
    for d in range(2):
        downward[pl.ds(2 * nvar + 5 + d, 1), :] = rows[d, pl.ds(0, 1), :]
    downward[pl.ds(2 * nvar + 7, 1), :] = own_links[...].astype(jnp.float32)


def half_jacobians(coefs, nvar):
    return [
        [[coefs[pl.ds((d * nvar + v) * nvar + w, 1), :] for w in range(nvar)] for v in range(nvar)]
        for d in range(2)
    ]


def step_weight(n, row, col):
    me = lax.axis_index("inst")
    values = [np.float32(pseudo_step) * spectral_table(n)[i ^ row, i ^ col] for i in range(n)]
    weight = values[0]
    for i in range(1, n):
        weight = jnp.where(me == i, values[i], weight)
    return weight


def weighted(weights, values):
    total = weights[0] * values[0]
    for weight, value in zip(weights[1:], values[1:]):
        total = total + weight * value
    return total


def transformed(half, values):
    return [[weighted(half[d][v], values) for v in range(len(values))] for d in range(2)]


def spread_of(normal):
    return 0.5 * (jnp.abs(normal[0]) + jnp.abs(normal[1]))


def own_side(normal, values, values_j):
    spread = spread_of(normal)
    return [
        normal[0] * values_j[0][v] + normal[1] * values_j[1][v] - spread * values[v]
        for v in range(len(values))
    ]


def other_side(normal, values, values_j):
    spread = spread_of(normal)
    return [
        normal[0] * values_j[0][v] + normal[1] * values_j[1][v] + spread * values[v]
        for v in range(len(values))
    ]


def col_change(normal, values, values_j):
    columns = values[0].shape[1]
    upper_normal = [pltpu.roll(x, columns - 1, 1) for x in normal]
    own = own_side(normal, values, values_j)
    other = other_side(upper_normal, values, values_j)
    flux = [a + pltpu.roll(b, 1, 1) for a, b in zip(own, other)]
    return [pltpu.roll(x, columns - 1, 1) - x for x in flux]


def row_changes(count, at, first_flux, last_flux):
    last = None
    ahead = at(0)
    for s in range(count):
        faces, cells, cells_j = ahead
        nvar = len(cells)
        row = lax.broadcasted_iota(jnp.int32, cells[0].shape, 0)
        top, bottom = row == 0, row == STRIP - 1
        rolled_faces = [pltpu.roll(x, STRIP - 1, 0) for x in faces]
        if s + 1 < count:
            ahead = at(s + 1)
            rolled_faces = [
                jnp.where(bottom, pltpu.roll(x, STRIP - 1, 0), y) for x, y in zip(ahead[0], rolled_faces)
            ]
        own = own_side(faces, cells, cells_j)
        rolled = [pltpu.roll(x, 1, 0) for x in other_side(rolled_faces, cells, cells_j)]
        if s == 0:
            flux = [jnp.where(top, first_flux(v), own[v] + rolled[v]) for v in range(nvar)]
        else:
            flux = [own[v] + jnp.where(top, before[v], rolled[v]) for v in range(nvar)]
        lifted = [pltpu.roll(x, STRIP - 1, 0) for x in flux]
        if last is not None:
            yield (
                s - 1,
                last[0],
                last[1],
                [jnp.where(bottom, lifted[v], last[3][v]) - last[2][v] for v in range(nvar)],
            )
        before, last = rolled, (cells, cells_j, flux, lifted)
    yield (
        count - 1,
        last[0],
        last[1],
        [jnp.where(bottom, last_flux(v), last[3][v]) - last[2][v] for v in range(nvar)],
    )


def strip(s):
    return pl.ds(s * STRIP, STRIP)


def face_flux(normal, lower, lower_j, upper, upper_j):
    spread = spread_of(normal)
    return [
        normal[0] * (lower_j[0][v] + upper_j[0][v])
        + normal[1] * (lower_j[1][v] + upper_j[1][v])
        - spread * (upper[v] - lower[v])
        for v in range(len(lower))
    ]


def split_dot(x, onehot, transposed):
    high = x.astype(jnp.bfloat16)
    rest = x - high.astype(jnp.float32)
    middle = rest.astype(jnp.bfloat16)
    low = (rest - middle.astype(jnp.float32)).astype(jnp.bfloat16)
    count = x.shape[0]
    stacked = jnp.concatenate([high, middle, low], axis=0)
    out = lax.dot_general(
        stacked,
        onehot,
        (((1,), (1 if transposed else 0,)), ((), ())),
        preferred_element_type=jnp.float32,
    )
    return out[:count] + (out[count : 2 * count] + out[2 * count :])


def pair(below, above):
    return jnp.concatenate([below, above], axis=0)


def pick(mask, a, b):
    return [jnp.where(mask, x, y) for x, y in zip(a, b)]


def pick_both(mask, a, b):
    return pick(mask, a[0], b[0]), [pick(mask, x, y) for x, y in zip(a[1], b[1])]


def behind(below, above, t):
    return pair(below[pl.ds(t, 1), :], above[pl.ds(t, 1), :])


def crossed(rows, links_below, links_above, stack):
    stack[...] = jnp.zeros(stack.shape, jnp.float32)
    for t, x in enumerate(rows):
        stack[pl.ds(2 * t, 2), :] = x
    columns = stack.shape[1]
    cell = lax.broadcasted_iota(jnp.int32, (columns, columns), 0)
    onehots = [(cell == x).astype(jnp.float32).astype(jnp.bfloat16) for x in (links_below, links_above)]
    stacked = stack[...]
    side = lax.broadcasted_iota(jnp.int32, stacked.shape, 0) % 2
    stack[...] = jnp.where(
        side == 0, split_dot(stacked, onehots[0], False), split_dot(stacked, onehots[1], True)
    )
    return [stack[pl.ds(2 * t, 2), :] for t in range(len(rows))]


def edge_kernel(nvar, coefs, below, above, near, row_normals, links, early, out, kept, stack):
    depth, columns = near.shape[1], near.shape[2]
    half = half_jacobians(coefs, nvar)
    is_below = lax.broadcasted_iota(jnp.int32, (2, columns), 0) == 0
    inner_face = [
        pair(row_normals[d, pl.ds(0, 1), :], above[pl.ds(2 * nvar + 5 + d, 1), :]) for d in range(2)
    ]
    rows = [behind(below, above, nvar + v) for v in range(nvar + 1)] + inner_face
    links_above = above[pl.ds(2 * nvar + 7, 1), :].astype(jnp.int32)
    rows = crossed(rows, links[...], links_above, stack)
    rim, volume, face = rows[:nvar], rows[nvar], pick(is_below, inner_face, rows[nvar + 1 :])
    inside = [pair(near[v, pl.ds(0, 1), :], near[v, pl.ds(depth - 1, 1), :]) for v in range(nvar)]
    low, high = pick(is_below, rim, inside), pick(is_below, inside, rim)
    summed = transformed(half, [x + y for x, y in zip(low, high)])
    spread = spread_of(face)
    across = [
        face[0] * summed[0][v] + face[1] * summed[1][v] - spread * (high[v] - low[v]) for v in range(nvar)
    ]
    at = 2 * nvar
    for v in range(nvar):
        out[pl.ds(v, 1), :] = across[v][0:1]
        out[pl.ds(nvar + v, 1), :] = across[v][1:2]
        kept[v] = rim[v]
        kept[nvar + v] = jnp.where(is_below, across[v], -across[v])
    for v, x in enumerate(rim + [volume]):
        out[pl.ds(at + v, 1), :] = x[0:1]
        out[pl.ds(at + nvar + 1 + v, 1), :] = x[1:2]
    kept[2 * nvar] = volume
    for d in range(2):
        kept[2 * nvar + 1 + d] = face[d]
    head = out.shape[0] - 2 * depth
    for d in range(2):
        out[pl.ds(head + d * depth, depth), :] = row_normals[d]


def behind_kernel(nvar, coefs, below, above, links, out, stack):
    half = half_jacobians(coefs, nvar)
    is_below = lax.broadcasted_iota(jnp.int32, (2, links.shape[1]), 0) == 0

    def with_j(values):
        return values, transformed(half, values)

    outer, rim = [with_j([behind(below, above, t + v) for v in range(nvar)]) for t in (0, nvar)]
    low, high = pick_both(is_below, outer, rim), pick_both(is_below, rim, outer)
    at = 2 * nvar + 1
    far_flux = face_flux([behind(below, above, at + d) for d in range(2)], *low, *high)
    beside = col_change([behind(below, above, at + 2 + d) for d in range(2)], *rim)
    rows = [jnp.where(is_below, -x, x) + y for x, y in zip(far_flux, beside)]
    links_above = above[pl.ds(2 * nvar + 7, 1), :].astype(jnp.int32)
    for v, x in enumerate(crossed(rows, links[...], links_above, stack)):
        out[v] = x


def state_kernel(states, before, *outs):
    at = 0
    for out in outs:
        out[...] = states[0, pl.ds(at, out.shape[0])]
        at += out.shape[0]


def volume_kernel(cells, before, also, out):
    out[...] = cells[pl.ds(0, 1)]


def own_flux_kernel(nvar, jacobians, near, cell, row_normals, out, coefs):
    strips = out.shape[1] // STRIP
    for d in range(2):
        for v in range(nvar):
            for w in range(nvar):
                coefs[pl.ds((d * nvar + v) * nvar + w, 1), :] = jnp.full(
                    (1, coefs.shape[1]), 0.5 * jacobians[d, v, w], jnp.float32
                )
    half = half_jacobians(coefs, nvar)

    def at(s):
        cells = [near[v, strip(s), :] for v in range(nvar)]
        return [row_normals[d, strip(s), :] for d in range(2)], cells, transformed(half, cells)

    for s, cells, cells_j, along in row_changes(strips, at, lambda v: 0.0, lambda v: 0.0):
        beside = col_change([cell[1 + d, strip(s), :] for d in range(2)], cells, cells_j)
        factor = pseudo_step / cell[0, strip(s), :]
        for v in range(nvar):
            out[v, strip(s), :] = cells[v] - factor * (along[v] + beside[v])


def far_col_kernel(nvar, coefs, states, cell, out, out_j):
    strips = out.shape[1] // STRIP
    half = half_jacobians(coefs, nvar)
    for s in range(strips):
        cells = [states[0, v, strip(s), :] for v in range(nvar)]
        cells_j = transformed(half, cells)
        beside = col_change([cell[1 + d, strip(s), :] for d in range(2)], cells, cells_j)
        factor = pseudo_step / cell[0, strip(s), :]
        for v in range(nvar):
            out[v, strip(s), :] = cells[v] - factor * beside[v]
            for d in range(2):
                out_j[d, v, strip(s), :] = cells_j[d][v]


def time_kernel(n, nvar, near, beyond, edge, *refs):
    far = n // 2 - 1
    states, cells, *pieces, beyond_volumes = [refs[far * t : far * (t + 1)] for t in range(6)]
    parts, outs = refs[6 * far : 7 * far + 1], refs[7 * far + 1 :]
    beyond_states = [[x.at[v] for x in piece for v in range(x.shape[0])] for piece in zip(*pieces)]
    count = far + 1
    weights = [
        [step_weight(n, 2 * a, 2 * b) for b in range(count)]
        + [step_weight(n, 2 * a, 2 * b + 1) for b in range(count)]
        for a in range(count)
    ]
    strips = outs[0].shape[1] // STRIP
    row = lax.broadcasted_iota(jnp.int32, (STRIP, near.shape[2]), 0)
    for s in range(strips):
        here = [near[nvar, strip(s), :]] + [x[0, strip(s), :] for x in cells]
        sizes = here + [beyond[nvar, strip(s), :]] + [x[0, strip(s), :] for x in beyond_volumes]
        factors = [weighted(weights[a], sizes) / here[a] for a in range(count)]
        for v in range(nvar):
            values = [near[v, strip(s), :]] + [x[0, v, strip(s), :] for x in states]
            values = values + [beyond[v, strip(s), :]] + [x[v][strip(s), :] for x in beyond_states]
            moved = [
                parts[a][v, strip(s), :] - weighted(weights[a], values) - factors[a] * values[a]
                for a in range(count)
            ]
            if s == 0:
                moved[0] = moved[0] + jnp.where(row == 0, pseudo_step * edge[pl.ds(v, 1), :], 0.0) / here[0]
            if s == strips - 1:
                lacking = jnp.where(row == STRIP - 1, pseudo_step * edge[pl.ds(nvar + v, 1), :], 0.0)
                moved[0] = moved[0] - lacking / here[0]
            for a in range(count):
                outs[a][v, strip(s), :] = moved[a]


def base_kernel(n, nvar, coefs, stepped, near, beyond, cell, row_normals, *refs):
    far = n // 2 - 1
    cells_of, beyond_volumes, out = refs[:far], refs[far : 2 * far], refs[2 * far]
    strips = out.shape[1] // STRIP
    half = half_jacobians(coefs, nvar)
    weights = [step_weight(n, 0, 2 * b) for b in range(far + 1)]
    weights = weights + [step_weight(n, 0, 2 * b + 1) for b in range(far + 1)]

    def at(s):
        cells = [stepped[v, strip(s), :] for v in range(nvar)]
        return [row_normals[d, strip(s), :] for d in range(2)], cells, transformed(half, cells)

    for s, cells, cells_j, along in row_changes(strips, at, lambda v: 0.0, lambda v: 0.0):
        beside = col_change([cell[1 + d, strip(s), :] for d in range(2)], cells, cells_j)
        sizes = [near[nvar, strip(s), :]] + [x[0, strip(s), :] for x in cells_of]
        sizes = sizes + [beyond[nvar, strip(s), :]] + [x[0, strip(s), :] for x in beyond_volumes]
        inverse = 1.0 / sizes[0]
        kept = (1.0 - weights[0]) - inverse * weighted(weights, sizes)
        for v in range(nvar):
            out[v, strip(s), :] = kept * cells[v] - (pseudo_step * inverse) * (along[v] + beside[v])


def far_step_kernel(n, nvar, stepped, edge, *refs):
    far = n // 2 - 1
    edges, states, cells_of, parts, transforms = [refs[far * t : far * (t + 1)] for t in range(5)]
    shared, out = refs[5 * far :]
    depth = stepped.shape[1]
    strips = depth // STRIP
    mine = [step_weight(n, 0, 2 * b) for b in range(far + 1)]
    other = [step_weight(n, 1, 2 * b) for b in range(far + 1)]
    head = edge.shape[0] - 2 * depth

    def changes(a):
        def at(s):
            faces = [edges[a][pl.ds(head + d * depth + s * STRIP, STRIP), :] for d in range(2)]
            cells = [states[a][0, v, strip(s), :] for v in range(nvar)]
            return faces, cells, [[transforms[a][d, v, strip(s), :] for v in range(nvar)] for d in range(2)]

        return row_changes(
            strips, at, lambda v: edges[a][pl.ds(v, 1), :], lambda v: edges[a][pl.ds(nvar + v, 1), :]
        )

    for moves in zip(*[changes(a) for a in range(far)]):
        s = moves[0][0]
        factors = [pseudo_step / cells_of[a][0, strip(s), :] for a in range(far)]
        for v in range(nvar):
            given = other[0] * stepped[v, strip(s), :]
            taken = None
            for a in range(far):
                value = parts[a][v, strip(s), :] - factors[a] * moves[a][3][v]
                given = given + other[1 + a] * value
                taken = mine[1 + a] * value if taken is None else taken + mine[1 + a] * value
            shared[pl.ds(v * depth + s * STRIP, STRIP), :] = given
            out[v, strip(s), :] = taken
    rims = pl.ds(2 * nvar, 2 * nvar + 2)
    shared[pl.ds(nvar * depth, 2 * nvar + 2), :] = weighted(
        other, [edge[rims, :]] + [edges[a][rims, :] for a in range(far)]
    )


def rim_kernel(n, nvar, coefs, edge, kept, others, near, stepped, *refs):
    far = n // 2 - 1
    edges, out = refs[:far], refs[far]
    depth, columns = stepped.shape[1], stepped.shape[2]
    half = half_jacobians(coefs, nvar)
    weights = [step_weight(n, 0, 2 * b) for b in range(far + 1)]
    is_below = lax.broadcasted_iota(jnp.int32, (2, columns), 0) == 0
    at = 2 * nvar

    def rim(v):
        return weighted(
            weights,
            [
                pair(ref[pl.ds(at + v, 1), :], ref[pl.ds(at + nvar + 1 + v, 1), :])
                for ref in [edge] + list(edges)
            ],
        )

    inverse = 1.0 / kept[2 * nvar]
    volume_rate = rim(nvar)
    face = [kept[2 * nvar + 1], kept[2 * nvar + 2]]
    spread = spread_of(face)
    inside = [pair(stepped[v, pl.ds(0, 1), :], stepped[v, pl.ds(depth - 1, 1), :]) for v in range(nvar)]
    inside_j = transformed(half, inside)
    for v in range(nvar):
        change = pseudo_step * (kept[nvar + v] + others[v])
        out[v] = kept[v] - rim(v) - inverse * (kept[v] * volume_rate + change)
        out[nvar + v] = inverse * kept[v]
        out[2 * nvar + v] = (
            face[0] * inside_j[0][v]
            + face[1] * inside_j[1][v]
            + jnp.where(is_below, -spread, spread) * inside[v]
        )
    volume = pair(near[nvar, pl.ds(0, 1), :], near[nvar, pl.ds(depth - 1, 1), :])
    factor = pseudo_step / volume
    out[3 * nvar] = jnp.where(is_below, factor, -factor)


def final_kernel(nvar, coefs, rims, kept, base, taken, shared, out, held, sems):
    depth, columns = base.shape[1], base.shape[2]
    strips = depth // STRIP
    half = half_jacobians(coefs, nvar)
    is_below = lax.broadcasted_iota(jnp.int32, (2, columns), 0) == 0

    def summed(v):
        return pair(shared[pl.ds(nvar * depth + v, 1), :], shared[pl.ds(nvar * depth + nvar + 1 + v, 1), :])

    def value(v, s):
        other = taken[v, strip(s), :] + shared[pl.ds(v * depth + s * STRIP, STRIP), :]
        return base[v, strip(s), :] - other

    copies = []

    def send(t, first, count):
        where = pl.ds(first * STRIP, count * STRIP)
        copies.append(pltpu.make_async_copy(held.at[:, where], out.at[0, :, where], sems.at[t]))
        copies[-1].start()

    for s in range(1, strips - 1):
        for v in range(nvar):
            held[v, strip(s), :] = value(v, s)
    send(0, 1, strips - 2)
    volume_rate = summed(nvar)
    outside = [rims[v] - summed(v) - rims[nvar + v] * volume_rate for v in range(nvar)]
    outside_j = transformed(half, outside)
    face = [kept[2 * nvar + 1], kept[2 * nvar + 2]]
    spread = spread_of(face)
    signed = jnp.where(is_below, spread, -spread)
    row = lax.broadcasted_iota(jnp.int32, (STRIP, columns), 0)
    for v in range(nvar):
        across = face[0] * outside_j[0][v] + face[1] * outside_j[1][v] + signed * outside[v]
        lacking = rims[3 * nvar] * (across + rims[2 * nvar + v])
        held[v, strip(0), :] = value(v, 0) + jnp.where(row == 0, lacking[0:1], 0.0)
        held[v, strip(strips - 1), :] = value(v, strips - 1) + jnp.where(
            row == STRIP - 1, lacking[1:2], 0.0
        )
    send(1, 0, 1)
    send(2, strips - 1, 1)
    for copy in copies:
        copy.wait()


def body(states, volumes, row_normals, col_normals, face_links, jacobians):
    n = lax.axis_size("inst")
    slabs = lax.axis_size("slab")
    _, nvar, depth, columns = states.shape
    far = list(range(2, n, 2))
    down_rows = -(-(2 * nvar + 8) // 8) * 8
    up_rows = down_rows + 8
    head = -(-(4 * nvar + 2) // 8) * 8

    def f32(*shape):
        return jax.ShapeDtypeStruct(shape, jnp.float32)

    vmem = pl.BlockSpec(memory_space=pltpu.VMEM)
    smem = pl.BlockSpec(memory_space=pltpu.SMEM)
    hbm = pl.BlockSpec(memory_space=pltpu.HBM)
    params = pltpu.CompilerParams(vmem_limit_bytes=24 * 1024 * 1024)

    def call(kernel, name, shapes, *operands, scratch=(), out_spec=vmem):
        single = not isinstance(shapes, list)
        return pl.pallas_call(
            kernel,
            out_shape=shapes,
            in_specs=[smem if x is jacobians else vmem for x in operands],
            out_specs=out_spec if single else [out_spec] * len(shapes),
            scratch_shapes=list(scratch),
            compiler_params=params,
            name=name,
        )(*operands)

    def swapped(x, k):
        return lax.ppermute(x, "inst", [(i, i ^ k) for i in range(n)])

    state_of = {k: swapped(states, k) for k in far}
    inputs = [
        pltpu.with_memory_space_constraint(x, pltpu.HBM)
        for x in (states, volumes, row_normals, col_normals, face_links)
    ]
    near, own_cell, own_rows, own_links, upward, downward = pl.pallas_call(
        pack_kernel,
        out_shape=[
            f32(nvar + 1, depth, columns),
            f32(3, depth, columns),
            f32(2, depth, columns),
            jax.ShapeDtypeStruct(face_links.shape, face_links.dtype),
            f32(up_rows, columns),
            f32(down_rows, columns),
        ],
        in_specs=[hbm] * 5,
        out_specs=[vmem] * 6,
        scratch_shapes=[pltpu.SemaphoreType.DMA((6,))],
        compiler_params=params,
        name="pack",
    )(*inputs)
    cell_of = {k: swapped(own_cell, k) for k in far}
    below = lax.ppermute(upward, "slab", [(i, (i + 1) % slabs) for i in range(slabs)])
    above = lax.ppermute(downward, "slab", [(i, (i - 1) % slabs) for i in range(slabs)])
    field = f32(nvar, depth, columns)
    own_part, coefs = call(
        functools.partial(own_flux_kernel, nvar),
        "own_flux",
        [field, f32(-(-2 * nvar * nvar // 8) * 8, columns)],
        jacobians,
        near,
        own_cell,
        own_rows,
    )
    parts = [own_part]
    edge, kept = call(
        functools.partial(edge_kernel, nvar),
        "edges",
        [f32(head + 2 * depth, columns), f32(2 * nvar + 3, 2, columns)],
        coefs,
        below,
        above,
        near,
        own_rows,
        own_links,
        own_part,
        scratch=[pltpu.VMEM((-(-(2 * nvar + 6) // 8) * 8, columns), jnp.float32)],
    )
    others = call(
        functools.partial(behind_kernel, nvar),
        "behind",
        f32(nvar, 2, columns),
        coefs,
        below,
        above,
        own_links,
        scratch=[pltpu.VMEM((-(-2 * nvar // 8) * 8, columns), jnp.float32)],
    )
    edge_of = {k: swapped(edge, k) for k in far}
    beyond = swapped(near, 1)
    pieces = [f32(count, depth, columns) for count in (2, 2, nvar - 4)]
    beyond_states, beyond_volumes = [], dict()
    for k in far:
        copies = call(state_kernel, "states", pieces, state_of[k], edge)
        beyond_states.append([swapped(x, 1) for x in copies])
        held = call(volume_kernel, "volumes", f32(1, depth, columns), cell_of[k], others, copies[-1])
        beyond_volumes[k] = swapped(held, 1)

    transforms = {}
    for k in far:
        part, transforms[k] = call(
            functools.partial(far_col_kernel, nvar),
            "far_col",
            [field, f32(2, nvar, depth, columns)],
            coefs,
            state_of[k],
            cell_of[k],
        )
        parts.append(part)
    stepped, *parts = call(
        functools.partial(time_kernel, n, nvar),
        "time",
        [field] * (len(far) + 1),
        near,
        beyond,
        edge,
        *[state_of[k] for k in far],
        *[cell_of[k] for k in far],
        *[x[0] for x in beyond_states],
        *[x[1] for x in beyond_states],
        *[x[2] for x in beyond_states],
        *[beyond_volumes[k] for k in far],
        *parts,
    )
    base = call(
        functools.partial(base_kernel, n, nvar),
        "base",
        field,
        coefs,
        stepped,
        near,
        beyond,
        own_cell,
        own_rows,
        *[cell_of[k] for k in far],
        *[beyond_volumes[k] for k in far],
    )
    shared, taken = call(
        functools.partial(far_step_kernel, n, nvar),
        "far_step",
        [f32(nvar * depth + 16, columns), field],
        stepped,
        edge,
        *[edge_of[k] for k in far],
        *[state_of[k] for k in far],
        *[cell_of[k] for k in far],
        *parts,
        *[transforms[k] for k in far],
    )
    rims = call(
        functools.partial(rim_kernel, n, nvar),
        "rims",
        f32(3 * nvar + 1, 2, columns),
        coefs,
        edge,
        kept,
        others,
        near,
        stepped,
        *[edge_of[k] for k in far],
    )
    return call(
        functools.partial(final_kernel, nvar),
        "final",
        f32(1, nvar, depth, columns),
        coefs,
        rims,
        kept,
        base,
        taken,
        swapped(shared, 1),
        scratch=[pltpu.VMEM((nvar, depth, columns), jnp.float32), pltpu.SemaphoreType.DMA((3,))],
        out_spec=hbm,
    )


def solution(mesh):
    return jax.shard_map(
        body,
        mesh=mesh,
        in_specs=(
            P(("grp", "inst"), None, "slab", None),
            P(("grp", "inst"), "slab", None),
            P(("grp", "inst"), None, "slab", None),
            P(("grp", "inst"), None, "slab", None),
            P("slab", None),
            P(),
        ),
        out_specs=P(("grp", "inst"), None, "slab", None),
        check_vma=False,
    )
```

```python
import functools

import jax
import jax.numpy as jnp
import numpy as np
from jax import lax
from jax.experimental import pallas as pl
from jax.experimental.pallas import tpu as pltpu
from jax.sharding import PartitionSpec as P

frequency = 0.5
pseudo_step = 0.2
nyquist_damping = 0.25

STRIP = 8
PIECES = (2, 2, 1)


def spectral_table(instances):
    offsets = np.arange(instances)[:, None] - np.arange(instances)[None, :]
    phases = np.pi * offsets / instances
    sine_safe = np.where(offsets == 0, 1.0, np.sin(phases))
    parity = np.where(offsets % 2 == 0, 1.0, -1.0)
    matrix = np.where(offsets == 0, 0.0, 0.5 * frequency * parity * np.cos(phases) / sine_safe)
    matrix = matrix + nyquist_damping * parity
    return matrix.astype(np.float32)


def pack_kernel(states, volumes, row_normals, col_normals, links, near, cell, rows, own_links, upward, downward, sems):
    nvar, depth = states.shape[1], states.shape[2]
    pairs = [
        (states.at[0], near),
        (volumes, cell.at[pl.ds(0, 1)]),
        (col_normals.at[0], cell.at[pl.ds(1, 2)]),
        (row_normals.at[0], rows),
        (links, own_links),
    ]
    copies = [pltpu.make_async_copy(a, b, sems.at[t]) for t, (a, b) in enumerate(pairs)]
    for copy in copies:
        copy.start()
    for copy in copies:
        copy.wait()

    def put(ref, second, edge, face):
        for v in range(nvar):
            ref[pl.ds(v, 1), :] = near[v, pl.ds(second, 1), :]
            ref[pl.ds(nvar + v, 1), :] = near[v, pl.ds(edge, 1), :]
        ref[pl.ds(2 * nvar, 1), :] = cell[0, pl.ds(edge, 1), :]
        for d in range(2):
            ref[pl.ds(2 * nvar + 1 + d, 1), :] = rows[d, pl.ds(face, 1), :]
            ref[pl.ds(2 * nvar + 3 + d, 1), :] = cell[1 + d, pl.ds(edge, 1), :]

    put(upward, depth - 2, depth - 1, depth - 1)
    put(downward, 1, 0, 1)
    for d in range(2):
        downward[pl.ds(2 * nvar + 5 + d, 1), :] = rows[d, pl.ds(0, 1), :]
    downward[pl.ds(2 * nvar + 7, 1), :] = own_links[...].astype(jnp.float32)


def half_jacobians(coefs, nvar):
    return [
        [[coefs[pl.ds((d * nvar + v) * nvar + w, 1), :] for w in range(nvar)] for v in range(nvar)]
        for d in range(2)
    ]


def step_weight(n, row, col):
    me = lax.axis_index("inst")
    values = [np.float32(pseudo_step) * spectral_table(n)[i ^ row, i ^ col] for i in range(n)]
    weight = values[0]
    for i in range(1, n):
        weight = jnp.where(me == i, values[i], weight)
    return weight


def weighted(weights, values):
    total = weights[0] * values[0]
    for weight, value in zip(weights[1:], values[1:]):
        total = total + weight * value
    return total


def transformed(half, values):
    return [[weighted(half[d][v], values) for v in range(len(values))] for d in range(2)]


def spread_of(normal):
    return 0.5 * (jnp.abs(normal[0]) + jnp.abs(normal[1]))


def own_side(normal, values, values_j):
    spread = spread_of(normal)
    return [
        normal[0] * values_j[0][v] + normal[1] * values_j[1][v] - spread * values[v]
        for v in range(len(values))
    ]


def other_side(normal, values, values_j):
    spread = spread_of(normal)
    return [
        normal[0] * values_j[0][v] + normal[1] * values_j[1][v] + spread * values[v]
        for v in range(len(values))
    ]


def col_change(normal, values, values_j):
    columns = values[0].shape[1]
    upper_normal = [pltpu.roll(x, columns - 1, 1) for x in normal]
    own = own_side(normal, values, values_j)
    other = other_side(upper_normal, values, values_j)
    flux = [a + pltpu.roll(b, 1, 1) for a, b in zip(own, other)]
    return [pltpu.roll(x, columns - 1, 1) - x for x in flux]


def row_changes(count, at, first_flux, last_flux):
    last = None
    ahead = at(0)
    for s in range(count):
        faces, cells, cells_j = ahead
        nvar = len(cells)
        row = lax.broadcasted_iota(jnp.int32, cells[0].shape, 0)
        top, bottom = row == 0, row == STRIP - 1
        rolled_faces = [pltpu.roll(x, STRIP - 1, 0) for x in faces]
        if s + 1 < count:
            ahead = at(s + 1)
            rolled_faces = [
                jnp.where(bottom, pltpu.roll(x, STRIP - 1, 0), y) for x, y in zip(ahead[0], rolled_faces)
            ]
        own = own_side(faces, cells, cells_j)
        rolled = [pltpu.roll(x, 1, 0) for x in other_side(rolled_faces, cells, cells_j)]
        if s == 0:
            flux = [jnp.where(top, first_flux(v), own[v] + rolled[v]) for v in range(nvar)]
        else:
            flux = [own[v] + jnp.where(top, before[v], rolled[v]) for v in range(nvar)]
        lifted = [pltpu.roll(x, STRIP - 1, 0) for x in flux]
        if last is not None:
            yield (
                s - 1,
                last[0],
                last[1],
                [jnp.where(bottom, lifted[v], last[3][v]) - last[2][v] for v in range(nvar)],
            )
        before, last = rolled, (cells, cells_j, flux, lifted)
    yield (
        count - 1,
        last[0],
        last[1],
        [jnp.where(bottom, last_flux(v), last[3][v]) - last[2][v] for v in range(nvar)],
    )


def strip(s):
    return pl.ds(s * STRIP, STRIP)


def face_flux(normal, lower, lower_j, upper, upper_j):
    spread = spread_of(normal)
    return [
        normal[0] * (lower_j[0][v] + upper_j[0][v])
        + normal[1] * (lower_j[1][v] + upper_j[1][v])
        - spread * (upper[v] - lower[v])
        for v in range(len(lower))
    ]


def split_dot(x, onehot, transposed):
    high = x.astype(jnp.bfloat16)
    rest = x - high.astype(jnp.float32)
    middle = rest.astype(jnp.bfloat16)
    low = (rest - middle.astype(jnp.float32)).astype(jnp.bfloat16)
    count = x.shape[0]
    stacked = jnp.concatenate([high, middle, low], axis=0)
    out = lax.dot_general(
        stacked,
        onehot,
        (((1,), (1 if transposed else 0,)), ((), ())),
        preferred_element_type=jnp.float32,
    )
    return out[:count] + (out[count : 2 * count] + out[2 * count :])


def pair(below, above):
    return jnp.concatenate([below, above], axis=0)


def pick(mask, a, b):
    return [jnp.where(mask, x, y) for x, y in zip(a, b)]


def pick_both(mask, a, b):
    return pick(mask, a[0], b[0]), [pick(mask, x, y) for x, y in zip(a[1], b[1])]


def behind(below, above, t):
    return pair(below[pl.ds(t, 1), :], above[pl.ds(t, 1), :])


def crossed(rows, links_below, links_above, stack):
    stack[...] = jnp.zeros(stack.shape, jnp.float32)
    for t, x in enumerate(rows):
        stack[pl.ds(2 * t, 2), :] = x
    columns = stack.shape[1]
    cell = lax.broadcasted_iota(jnp.int32, (columns, columns), 0)
    onehots = [(cell == x).astype(jnp.float32).astype(jnp.bfloat16) for x in (links_below, links_above)]
    stacked = stack[...]
    side = lax.broadcasted_iota(jnp.int32, stacked.shape, 0) % 2
    stack[...] = jnp.where(
        side == 0, split_dot(stacked, onehots[0], False), split_dot(stacked, onehots[1], True)
    )
    return [stack[pl.ds(2 * t, 2), :] for t in range(len(rows))]


def edge_kernel(nvar, coefs, below, above, near, row_normals, links, early, out, kept, stack):
    depth, columns = near.shape[1], near.shape[2]
    half = half_jacobians(coefs, nvar)
    is_below = lax.broadcasted_iota(jnp.int32, (2, columns), 0) == 0
    inner_face = [
        pair(row_normals[d, pl.ds(0, 1), :], above[pl.ds(2 * nvar + 5 + d, 1), :]) for d in range(2)
    ]
    rows = [behind(below, above, nvar + v) for v in range(nvar + 1)] + inner_face
    links_above = above[pl.ds(2 * nvar + 7, 1), :].astype(jnp.int32)
    rows = crossed(rows, links[...], links_above, stack)
    rim, volume, face = rows[:nvar], rows[nvar], pick(is_below, inner_face, rows[nvar + 1 :])
    inside = [pair(near[v, pl.ds(0, 1), :], near[v, pl.ds(depth - 1, 1), :]) for v in range(nvar)]
    low, high = pick(is_below, rim, inside), pick(is_below, inside, rim)
    summed = transformed(half, [x + y for x, y in zip(low, high)])
    spread = spread_of(face)
    across = [
        face[0] * summed[0][v] + face[1] * summed[1][v] - spread * (high[v] - low[v]) for v in range(nvar)
    ]
    at = 2 * nvar
    for v in range(nvar):
        out[pl.ds(v, 1), :] = across[v][0:1]
        out[pl.ds(nvar + v, 1), :] = across[v][1:2]
        kept[v] = rim[v]
        kept[nvar + v] = jnp.where(is_below, across[v], -across[v])
    for v, x in enumerate(rim + [volume]):
        out[pl.ds(at + v, 1), :] = x[0:1]
        out[pl.ds(at + nvar + 1 + v, 1), :] = x[1:2]
    kept[2 * nvar] = volume
    for d in range(2):
        kept[2 * nvar + 1 + d] = face[d]
    head = out.shape[0] - 2 * depth
    for d in range(2):
        out[pl.ds(head + d * depth, depth), :] = row_normals[d]


def behind_kernel(nvar, coefs, below, above, links, out, stack):
    half = half_jacobians(coefs, nvar)
    is_below = lax.broadcasted_iota(jnp.int32, (2, links.shape[1]), 0) == 0

    def with_j(values):
        return values, transformed(half, values)

    outer, rim = [with_j([behind(below, above, t + v) for v in range(nvar)]) for t in (0, nvar)]
    low, high = pick_both(is_below, outer, rim), pick_both(is_below, rim, outer)
    at = 2 * nvar + 1
    far_flux = face_flux([behind(below, above, at + d) for d in range(2)], *low, *high)
    beside = col_change([behind(below, above, at + 2 + d) for d in range(2)], *rim)
    rows = [jnp.where(is_below, -x, x) + y for x, y in zip(far_flux, beside)]
    links_above = above[pl.ds(2 * nvar + 7, 1), :].astype(jnp.int32)
    for v, x in enumerate(crossed(rows, links[...], links_above, stack)):
        out[v] = x


def state_kernel(at, states, before, out):
    out[...] = states[0, pl.ds(at, out.shape[0])]


def volume_kernel(cells, before, out):
    out[...] = cells[pl.ds(0, 1)]


def own_flux_kernel(nvar, jacobians, near, cell, row_normals, out, coefs):
    strips = out.shape[1] // STRIP
    for d in range(2):
        for v in range(nvar):
            for w in range(nvar):
                coefs[pl.ds((d * nvar + v) * nvar + w, 1), :] = jnp.full(
                    (1, coefs.shape[1]), 0.5 * jacobians[d, v, w], jnp.float32
                )
    half = half_jacobians(coefs, nvar)

    def at(s):
        cells = [near[v, strip(s), :] for v in range(nvar)]
        return [row_normals[d, strip(s), :] for d in range(2)], cells, transformed(half, cells)

    for s, cells, cells_j, along in row_changes(strips, at, lambda v: 0.0, lambda v: 0.0):
        beside = col_change([cell[1 + d, strip(s), :] for d in range(2)], cells, cells_j)
        factor = pseudo_step / cell[0, strip(s), :]
        for v in range(nvar):
            out[v, strip(s), :] = cells[v] - factor * (along[v] + beside[v])


def planes(pieces):
    return [x.at[v] for x in pieces for v in range(x.shape[0])]


def families(n):
    return [0] + list(range(3, n, 2)), [1] + list(range(2, n, 2))


def far_col_kernel(nvar, coefs, cell, *refs):
    states, (out, out_j) = planes(refs[:-2]), refs[-2:]
    strips = out.shape[1] // STRIP
    half = half_jacobians(coefs, nvar)
    for s in range(strips):
        cells = [states[v][strip(s), :] for v in range(nvar)]
        cells_j = transformed(half, cells)
        beside = col_change([cell[1 + d, strip(s), :] for d in range(2)], cells, cells_j)
        factor = pseudo_step / cell[0, strip(s), :]
        for v in range(nvar):
            out[v, strip(s), :] = cells[v] - factor * beside[v]
            for d in range(2):
                out_j[d, v, strip(s), :] = cells_j[d][v]


def near_kernel(n, nvar, near, beyond, cell, volumes, part, sizes, *outs):
    here, _ = families(n)
    weights = [[step_weight(n, a, b) for b in (0, 1)] for a in here]
    for s in range(part.shape[1] // STRIP):
        for a in range(len(here)):
            sizes[a, strip(s), :] = weighted(weights[a], [cell[0, strip(s), :], volumes[0, strip(s), :]])
        for v in range(nvar):
            values = [near[v, strip(s), :], beyond[v, strip(s), :]]
            outs[0][v, strip(s), :] = part[v, strip(s), :] - weighted(weights[0], values)
            for a in range(1, len(here)):
                outs[a][v, strip(s), :] = -weighted(weights[a], values)


def time_kernel(n, nvar, near, own, sums, edge, *refs):
    far = n // 2 - 1
    beyond_states, cells, beyond_volumes, *pieces = [refs[far * t : far * (t + 1)] for t in range(3 + len(PIECES))]
    refs = refs[far * (3 + len(PIECES)) :]
    begun, parts = refs[: far + 1], refs[far + 1 : 2 * far + 1]
    rate, outs = refs[2 * far + 1], refs[2 * far + 2 :]
    states = [planes(x) for x in zip(*pieces)]
    here, there = families(n)
    rest = [[step_weight(n, a, b) for b in here[1:] + there[1:]] for a in here]
    strips = outs[0].shape[1] // STRIP
    row = lax.broadcasted_iota(jnp.int32, (STRIP, near.shape[2]), 0)
    for s in range(strips):
        sizes = [x[0, strip(s), :] for x in (own, *cells)]
        far_sizes = sizes[1:] + [x[0, strip(s), :] for x in beyond_volumes]
        rates = [sums[a, strip(s), :] + weighted(rest[a], far_sizes) for a in range(far + 1)]
        factors = [rates[a] / sizes[a] for a in range(far + 1)]
        rate[strip(s), :] = factors[0]
        for v in range(nvar):
            values = [near[v, strip(s), :]] + [x[v][strip(s), :] for x in states]
            others = values[1:] + [x[0, v, strip(s), :] for x in beyond_states]
            moved = [
                begun[a][v, strip(s), :] - weighted(rest[a], others) - factors[a] * values[a]
                for a in range(far + 1)
            ]
            moved = moved[:1] + [moved[a] + parts[a - 1][v, strip(s), :] for a in range(1, far + 1)]
            if s == 0:
                moved[0] = moved[0] + jnp.where(row == 0, pseudo_step * edge[pl.ds(v, 1), :], 0.0) / sizes[0]
            if s == strips - 1:
                lacking = jnp.where(row == STRIP - 1, pseudo_step * edge[pl.ds(nvar + v, 1), :], 0.0)
                moved[0] = moved[0] - lacking / sizes[0]
            for a in range(far + 1):
                outs[a][v, strip(s), :] = moved[a]


def base_kernel(n, nvar, coefs, stepped, cell, row_normals, rate, out):
    strips = out.shape[1] // STRIP
    half = half_jacobians(coefs, nvar)
    weight = step_weight(n, 0, 0)

    def at(s):
        cells = [stepped[v, strip(s), :] for v in range(nvar)]
        return [row_normals[d, strip(s), :] for d in range(2)], cells, transformed(half, cells)

    for s, cells, cells_j, along in row_changes(strips, at, lambda v: 0.0, lambda v: 0.0):
        beside = col_change([cell[1 + d, strip(s), :] for d in range(2)], cells, cells_j)
        inverse = 1.0 / cell[0, strip(s), :]
        kept = (1.0 - weight) - rate[strip(s), :]
        for v in range(nvar):
            out[v, strip(s), :] = kept * cells[v] - (pseudo_step * inverse) * (along[v] + beside[v])


def far_step_kernel(n, nvar, stepped, edge, *refs):
    far = n // 2 - 1
    edges, cells_of, parts, transforms, *pieces = [refs[far * t : far * (t + 1)] for t in range(4 + len(PIECES))]
    states = [planes(x) for x in zip(*pieces)]
    shared, out = refs[(4 + len(PIECES)) * far :]
    depth = stepped.shape[1]
    strips = depth // STRIP
    mine = [step_weight(n, 0, b) for b in families(n)[0]]
    other = [step_weight(n, 1, b) for b in families(n)[0]]
    head = edge.shape[0] - 2 * depth

    def changes(a):
        def at(s):
            faces = [edges[a][pl.ds(head + d * depth + s * STRIP, STRIP), :] for d in range(2)]
            cells = [states[a][v][strip(s), :] for v in range(nvar)]
            return faces, cells, [[transforms[a][d, v, strip(s), :] for v in range(nvar)] for d in range(2)]

        return row_changes(
            strips, at, lambda v: edges[a][pl.ds(v, 1), :], lambda v: edges[a][pl.ds(nvar + v, 1), :]
        )

    for moves in zip(*[changes(a) for a in range(far)]):
        s = moves[0][0]
        factors = [pseudo_step / cells_of[a][0, strip(s), :] for a in range(far)]
        for v in range(nvar):
            given = other[0] * stepped[v, strip(s), :]
            taken = None
            for a in range(far):
                value = parts[a][v, strip(s), :] - factors[a] * moves[a][3][v]
                given = given + other[1 + a] * value
                taken = mine[1 + a] * value if taken is None else taken + mine[1 + a] * value
            shared[pl.ds(v * depth + s * STRIP, STRIP), :] = given
            out[v, strip(s), :] = taken
    rims = pl.ds(2 * nvar, 2 * nvar + 2)
    shared[pl.ds(nvar * depth, 2 * nvar + 2), :] = weighted(
        other, [edge[rims, :]] + [edges[a][rims, :] for a in range(far)]
    )


def rim_kernel(n, nvar, coefs, edge, kept, others, cell, stepped, *refs):
    far = n // 2 - 1
    edges, out = refs[:far], refs[far]
    depth, columns = stepped.shape[1], stepped.shape[2]
    half = half_jacobians(coefs, nvar)
    weights = [step_weight(n, 0, b) for b in families(n)[0]]
    is_below = lax.broadcasted_iota(jnp.int32, (2, columns), 0) == 0
    at = 2 * nvar

    def rim(v):
        return weighted(
            weights,
            [
                pair(ref[pl.ds(at + v, 1), :], ref[pl.ds(at + nvar + 1 + v, 1), :])
                for ref in [edge] + list(edges)
            ],
        )

    inverse = 1.0 / kept[2 * nvar]
    volume_rate = rim(nvar)
    face = [kept[2 * nvar + 1], kept[2 * nvar + 2]]
    spread = spread_of(face)
    inside = [pair(stepped[v, pl.ds(0, 1), :], stepped[v, pl.ds(depth - 1, 1), :]) for v in range(nvar)]
    inside_j = transformed(half, inside)
    for v in range(nvar):
        change = pseudo_step * (kept[nvar + v] + others[v])
        out[v] = kept[v] - rim(v) - inverse * (kept[v] * volume_rate + change)
        out[nvar + v] = inverse * kept[v]
        out[2 * nvar + v] = (
            face[0] * inside_j[0][v]
            + face[1] * inside_j[1][v]
            + jnp.where(is_below, -spread, spread) * inside[v]
        )
    volume = pair(cell[0, pl.ds(0, 1), :], cell[0, pl.ds(depth - 1, 1), :])
    factor = pseudo_step / volume
    out[3 * nvar] = jnp.where(is_below, factor, -factor)


def final_kernel(nvar, coefs, rims, kept, base, taken, shared, out, held, sems):
    depth, columns = base.shape[1], base.shape[2]
    strips = depth // STRIP
    half = half_jacobians(coefs, nvar)
    is_below = lax.broadcasted_iota(jnp.int32, (2, columns), 0) == 0

    def summed(v):
        return pair(shared[pl.ds(nvar * depth + v, 1), :], shared[pl.ds(nvar * depth + nvar + 1 + v, 1), :])

    def value(v, s):
        other = taken[v, strip(s), :] + shared[pl.ds(v * depth + s * STRIP, STRIP), :]
        return base[v, strip(s), :] - other

    copies = []

    def send(t, first, count):
        where = pl.ds(first * STRIP, count * STRIP)
        copies.append(pltpu.make_async_copy(held.at[:, where], out.at[0, :, where], sems.at[t]))
        copies[-1].start()

    for s in range(1, strips - 1):
        for v in range(nvar):
            held[v, strip(s), :] = value(v, s)
    send(0, 1, strips - 2)
    volume_rate = summed(nvar)
    outside = [rims[v] - summed(v) - rims[nvar + v] * volume_rate for v in range(nvar)]
    outside_j = transformed(half, outside)
    face = [kept[2 * nvar + 1], kept[2 * nvar + 2]]
    spread = spread_of(face)
    signed = jnp.where(is_below, spread, -spread)
    row = lax.broadcasted_iota(jnp.int32, (STRIP, columns), 0)
    for v in range(nvar):
        across = face[0] * outside_j[0][v] + face[1] * outside_j[1][v] + signed * outside[v]
        lacking = rims[3 * nvar] * (across + rims[2 * nvar + v])
        held[v, strip(0), :] = value(v, 0) + jnp.where(row == 0, lacking[0:1], 0.0)
        held[v, strip(strips - 1), :] = value(v, strips - 1) + jnp.where(
            row == STRIP - 1, lacking[1:2], 0.0
        )
    send(1, 0, 1)
    send(2, strips - 1, 1)
    for copy in copies:
        copy.wait()


def body(states, volumes, row_normals, col_normals, face_links, jacobians):
    n = lax.axis_size("inst")
    slabs = lax.axis_size("slab")
    _, nvar, depth, columns = states.shape
    far = list(range(2, n, 2))
    down_rows = -(-(2 * nvar + 8) // 8) * 8
    up_rows = down_rows + 8
    head = -(-(4 * nvar + 2) // 8) * 8

    def f32(*shape):
        return jax.ShapeDtypeStruct(shape, jnp.float32)

    vmem = pl.BlockSpec(memory_space=pltpu.VMEM)
    smem = pl.BlockSpec(memory_space=pltpu.SMEM)
    hbm = pl.BlockSpec(memory_space=pltpu.HBM)
    params = pltpu.CompilerParams(vmem_limit_bytes=24 * 1024 * 1024)

    def call(kernel, name, shapes, *operands, scratch=(), out_spec=vmem):
        single = not isinstance(shapes, list)
        return pl.pallas_call(
            kernel,
            out_shape=shapes,
            in_specs=[smem if x is jacobians else vmem for x in operands],
            out_specs=out_spec if single else [out_spec] * len(shapes),
            scratch_shapes=list(scratch),
            compiler_params=params,
            name=name,
        )(*operands)

    def swapped(x, k):
        return lax.ppermute(x, "inst", [(i, i ^ k) for i in range(n)])

    state_of = {k: swapped(states, k) for k in far}
    inputs = [
        pltpu.with_memory_space_constraint(x, pltpu.HBM)
        for x in (states, volumes, row_normals, col_normals, face_links)
    ]
    near, own_cell, own_rows, own_links, upward, downward = pl.pallas_call(
        pack_kernel,
        out_shape=[
            f32(nvar, depth, columns),
            f32(3, depth, columns),
            f32(2, depth, columns),
            jax.ShapeDtypeStruct(face_links.shape, face_links.dtype),
            f32(up_rows, columns),
            f32(down_rows, columns),
        ],
        in_specs=[hbm] * 5,
        out_specs=[vmem] * 6,
        scratch_shapes=[pltpu.SemaphoreType.DMA((5,))],
        compiler_params=params,
        name="pack",
    )(*inputs)
    cell_of = {k: swapped(own_cell, k + 1) for k in far}
    below = lax.ppermute(upward, "slab", [(i, (i + 1) % slabs) for i in range(slabs)])
    above = lax.ppermute(downward, "slab", [(i, (i - 1) % slabs) for i in range(slabs)])
    field = f32(nvar, depth, columns)
    own_part, coefs = call(
        functools.partial(own_flux_kernel, nvar),
        "own_flux",
        [field, f32(-(-2 * nvar * nvar // 8) * 8, columns)],
        jacobians,
        near,
        own_cell,
        own_rows,
    )
    parts = []
    edge, kept = call(
        functools.partial(edge_kernel, nvar),
        "edges",
        [f32(head + 2 * depth, columns), f32(2 * nvar + 3, 2, columns)],
        coefs,
        below,
        above,
        near,
        own_rows,
        own_links,
        own_part,
        scratch=[pltpu.VMEM((-(-(2 * nvar + 6) // 8) * 8, columns), jnp.float32)],
    )
    others = call(
        functools.partial(behind_kernel, nvar),
        "behind",
        f32(nvar, 2, columns),
        coefs,
        below,
        above,
        own_links,
        scratch=[pltpu.VMEM((-(-2 * nvar // 8) * 8, columns), jnp.float32)],
    )
    edge_of = {k: swapped(edge, k + 1) for k in far}
    beyond = swapped(near, 1)
    sums, *begun = call(
        functools.partial(near_kernel, n, nvar),
        "near",
        [f32(len(far) + 1, depth, columns)] + [field] * (len(far) + 1),
        near,
        beyond,
        own_cell,
        swapped(call(volume_kernel, "volumes", f32(1, depth, columns), own_cell, edge), 1),
        own_part,
    )
    pieces_of, beyond_volumes = dict(), dict()
    for k in far:
        pieces, at = [], 0
        for t, count in enumerate(PIECES):
            before = begun[0] if t + 1 == len(PIECES) else edge
            shape = f32(count, depth, columns)
            kernel = functools.partial(state_kernel, at)
            held = call(kernel, "states", shape, state_of[k], before)
            pieces.append(swapped(held, 1))
            at += count
        pieces_of[k] = pieces
        held = call(volume_kernel, "volumes", f32(1, depth, columns), cell_of[k], begun[0])
        beyond_volumes[k] = swapped(held, 1)

    transforms = {}
    for k in far:
        part, transforms[k] = call(
            functools.partial(far_col_kernel, nvar),
            "far_col",
            [field, f32(2, nvar, depth, columns)],
            coefs,
            cell_of[k],
            *pieces_of[k],
        )
        parts.append(part)
    rate, stepped, *parts = call(
        functools.partial(time_kernel, n, nvar),
        "time",
        [f32(depth, columns)] + [field] * (len(far) + 1),
        near,
        own_cell,
        sums,
        edge,
        *[state_of[k] for k in far],
        *[cell_of[k] for k in far],
        *[beyond_volumes[k] for k in far],
        *[pieces_of[k][t] for t in range(len(PIECES)) for k in far],
        *begun,
        *parts,
    )
    base = call(
        functools.partial(base_kernel, n, nvar),
        "base",
        field,
        coefs,
        stepped,
        own_cell,
        own_rows,
        rate,
    )
    shared, taken = call(
        functools.partial(far_step_kernel, n, nvar),
        "far_step",
        [f32(nvar * depth + 16, columns), field],
        stepped,
        edge,
        *[edge_of[k] for k in far],
        *[cell_of[k] for k in far],
        *parts,
        *[transforms[k] for k in far],
        *[pieces_of[k][t] for t in range(len(PIECES)) for k in far],
    )
    rims = call(
        functools.partial(rim_kernel, n, nvar),
        "rims",
        f32(3 * nvar + 1, 2, columns),
        coefs,
        edge,
        kept,
        others,
        own_cell,
        stepped,
        *[edge_of[k] for k in far],
    )
    return call(
        functools.partial(final_kernel, nvar),
        "final",
        f32(1, nvar, depth, columns),
        coefs,
        rims,
        kept,
        base,
        taken,
        swapped(shared, 1),
        scratch=[pltpu.VMEM((nvar, depth, columns), jnp.float32), pltpu.SemaphoreType.DMA((3,))],
        out_spec=hbm,
    )


def solution(mesh):
    return jax.shard_map(
        body,
        mesh=mesh,
        in_specs=(
            P(("grp", "inst"), None, "slab", None),
            P(("grp", "inst"), "slab", None),
            P(("grp", "inst"), None, "slab", None),
            P(("grp", "inst"), None, "slab", None),
            P("slab", None),
            P(),
        ),
        out_specs=P(("grp", "inst"), None, "slab", None),
        check_vma=False,
    )
```

```python
import functools

import jax
import jax.numpy as jnp
import numpy as np
from jax import lax
from jax.experimental import pallas as pl
from jax.experimental.pallas import tpu as pltpu
from jax.sharding import PartitionSpec as P

frequency = 0.5
pseudo_step = 0.2
nyquist_damping = 0.25

STRIP = 8
PIECES = (2, 2, 1)


def spectral_table(instances):
    offsets = np.arange(instances)[:, None] - np.arange(instances)[None, :]
    phases = np.pi * offsets / instances
    sine_safe = np.where(offsets == 0, 1.0, np.sin(phases))
    parity = np.where(offsets % 2 == 0, 1.0, -1.0)
    matrix = np.where(offsets == 0, 0.0, 0.5 * frequency * parity * np.cos(phases) / sine_safe)
    matrix = matrix + nyquist_damping * parity
    return matrix.astype(np.float32)


def pack_kernel(states, volumes, row_normals, col_normals, links, near, cell, rows, own_links, upward, downward, sems):
    nvar, depth = states.shape[1], states.shape[2]
    pairs = [
        (states.at[0], near),
        (volumes, cell.at[pl.ds(0, 1)]),
        (col_normals.at[0], cell.at[pl.ds(1, 2)]),
        (row_normals.at[0], rows),
        (links, own_links),
    ]
    copies = [pltpu.make_async_copy(a, b, sems.at[t]) for t, (a, b) in enumerate(pairs)]
    for copy in copies:
        copy.start()
    for copy in copies:
        copy.wait()

    def put(ref, second, edge, face):
        for v in range(nvar):
            ref[pl.ds(v, 1), :] = near[v, pl.ds(second, 1), :]
            ref[pl.ds(nvar + v, 1), :] = near[v, pl.ds(edge, 1), :]
        ref[pl.ds(2 * nvar, 1), :] = cell[0, pl.ds(edge, 1), :]
        for d in range(2):
            ref[pl.ds(2 * nvar + 1 + d, 1), :] = rows[d, pl.ds(face, 1), :]
            ref[pl.ds(2 * nvar + 3 + d, 1), :] = cell[1 + d, pl.ds(edge, 1), :]

    put(upward, depth - 2, depth - 1, depth - 1)
    put(downward, 1, 0, 1)
    for d in range(2):
        downward[pl.ds(2 * nvar + 5 + d, 1), :] = rows[d, pl.ds(0, 1), :]
    downward[pl.ds(2 * nvar + 7, 1), :] = own_links[...].astype(jnp.float32)


def half_jacobians(coefs, nvar):
    return [
        [[coefs[pl.ds((d * nvar + v) * nvar + w, 1), :] for w in range(nvar)] for v in range(nvar)]
        for d in range(2)
    ]


def step_weight(n, row, col):
    me = lax.axis_index("inst")
    values = [np.float32(pseudo_step) * spectral_table(n)[i ^ row, i ^ col] for i in range(n)]
    weight = values[0]
    for i in range(1, n):
        weight = jnp.where(me == i, values[i], weight)
    return weight


def weighted(weights, values):
    total = weights[0] * values[0]
    for weight, value in zip(weights[1:], values[1:]):
        total = total + weight * value
    return total


def transformed(half, values):
    return [[weighted(half[d][v], values) for v in range(len(values))] for d in range(2)]


def spread_of(normal):
    return 0.5 * (jnp.abs(normal[0]) + jnp.abs(normal[1]))


def own_side(normal, values, values_j):
    spread = spread_of(normal)
    return [
        normal[0] * values_j[0][v] + normal[1] * values_j[1][v] - spread * values[v]
        for v in range(len(values))
    ]


def other_side(normal, values, values_j):
    spread = spread_of(normal)
    return [
        normal[0] * values_j[0][v] + normal[1] * values_j[1][v] + spread * values[v]
        for v in range(len(values))
    ]


def col_change(normal, values, values_j):
    columns = values[0].shape[1]
    upper_normal = [pltpu.roll(x, columns - 1, 1) for x in normal]
    own = own_side(normal, values, values_j)
    other = other_side(upper_normal, values, values_j)
    flux = [a + pltpu.roll(b, 1, 1) for a, b in zip(own, other)]
    return [pltpu.roll(x, columns - 1, 1) - x for x in flux]


def row_changes(count, at, first_flux, last_flux):
    last = None
    ahead = at(0)
    for s in range(count):
        faces, cells, cells_j = ahead
        nvar = len(cells)
        row = lax.broadcasted_iota(jnp.int32, cells[0].shape, 0)
        top, bottom = row == 0, row == STRIP - 1
        rolled_faces = [pltpu.roll(x, STRIP - 1, 0) for x in faces]
        if s + 1 < count:
            ahead = at(s + 1)
            rolled_faces = [
                jnp.where(bottom, pltpu.roll(x, STRIP - 1, 0), y) for x, y in zip(ahead[0], rolled_faces)
            ]
        own = own_side(faces, cells, cells_j)
        rolled = [pltpu.roll(x, 1, 0) for x in other_side(rolled_faces, cells, cells_j)]
        if s == 0:
            flux = [jnp.where(top, first_flux(v), own[v] + rolled[v]) for v in range(nvar)]
        else:
            flux = [own[v] + jnp.where(top, before[v], rolled[v]) for v in range(nvar)]
        lifted = [pltpu.roll(x, STRIP - 1, 0) for x in flux]
        if last is not None:
            yield (
                s - 1,
                last[0],
                last[1],
                [jnp.where(bottom, lifted[v], last[3][v]) - last[2][v] for v in range(nvar)],
            )
        before, last = rolled, (cells, cells_j, flux, lifted)
    yield (
        count - 1,
        last[0],
        last[1],
        [jnp.where(bottom, last_flux(v), last[3][v]) - last[2][v] for v in range(nvar)],
    )


def strip(s):
    return pl.ds(s * STRIP, STRIP)


def face_flux(normal, lower, lower_j, upper, upper_j):
    spread = spread_of(normal)
    return [
        normal[0] * (lower_j[0][v] + upper_j[0][v])
        + normal[1] * (lower_j[1][v] + upper_j[1][v])
        - spread * (upper[v] - lower[v])
        for v in range(len(lower))
    ]


def split_dot(x, onehot, transposed):
    high = x.astype(jnp.bfloat16)
    rest = x - high.astype(jnp.float32)
    middle = rest.astype(jnp.bfloat16)
    low = (rest - middle.astype(jnp.float32)).astype(jnp.bfloat16)
    count = x.shape[0]
    stacked = jnp.concatenate([high, middle, low], axis=0)
    out = lax.dot_general(
        stacked,
        onehot,
        (((1,), (1 if transposed else 0,)), ((), ())),
        preferred_element_type=jnp.float32,
    )
    return out[:count] + (out[count : 2 * count] + out[2 * count :])


def pair(below, above):
    return jnp.concatenate([below, above], axis=0)


def pick(mask, a, b):
    return [jnp.where(mask, x, y) for x, y in zip(a, b)]


def pick_both(mask, a, b):
    return pick(mask, a[0], b[0]), [pick(mask, x, y) for x, y in zip(a[1], b[1])]


def behind(below, above, t):
    return pair(below[pl.ds(t, 1), :], above[pl.ds(t, 1), :])


def crossed(rows, links_below, links_above, stack):
    stack[...] = jnp.zeros(stack.shape, jnp.float32)
    for t, x in enumerate(rows):
        stack[pl.ds(2 * t, 2), :] = x
    columns = stack.shape[1]
    cell = lax.broadcasted_iota(jnp.int32, (columns, columns), 0)
    onehots = [(cell == x).astype(jnp.float32).astype(jnp.bfloat16) for x in (links_below, links_above)]
    stacked = stack[...]
    side = lax.broadcasted_iota(jnp.int32, stacked.shape, 0) % 2
    stack[...] = jnp.where(
        side == 0, split_dot(stacked, onehots[0], False), split_dot(stacked, onehots[1], True)
    )
    return [stack[pl.ds(2 * t, 2), :] for t in range(len(rows))]


def edge_kernel(nvar, coefs, below, above, near, row_normals, links, early, out, kept, stack):
    depth, columns = near.shape[1], near.shape[2]
    half = half_jacobians(coefs, nvar)
    is_below = lax.broadcasted_iota(jnp.int32, (2, columns), 0) == 0
    inner_face = [
        pair(row_normals[d, pl.ds(0, 1), :], above[pl.ds(2 * nvar + 5 + d, 1), :]) for d in range(2)
    ]
    rows = [behind(below, above, nvar + v) for v in range(nvar + 1)] + inner_face
    links_above = above[pl.ds(2 * nvar + 7, 1), :].astype(jnp.int32)
    rows = crossed(rows, links[...], links_above, stack)
    rim, volume, face = rows[:nvar], rows[nvar], pick(is_below, inner_face, rows[nvar + 1 :])
    inside = [pair(near[v, pl.ds(0, 1), :], near[v, pl.ds(depth - 1, 1), :]) for v in range(nvar)]
    low, high = pick(is_below, rim, inside), pick(is_below, inside, rim)
    summed = transformed(half, [x + y for x, y in zip(low, high)])
    spread = spread_of(face)
    across = [
        face[0] * summed[0][v] + face[1] * summed[1][v] - spread * (high[v] - low[v]) for v in range(nvar)
    ]
    for v in range(nvar):
        kept[v] = rim[v]
        kept[nvar + v] = jnp.where(is_below, across[v], -across[v])
    for v, x in enumerate(rim + [volume]):
        out[pl.ds(v, 1), :] = x[0:1]
        out[pl.ds(nvar + 1 + v, 1), :] = x[1:2]
    kept[2 * nvar] = volume
    for d in range(2):
        out[pl.ds(2 * nvar + 2 + d, 1), :] = face[d][1:2]
        kept[2 * nvar + 1 + d] = face[d]
    head = out.shape[0] - 2 * depth
    for d in range(2):
        out[pl.ds(head + d * depth, depth), :] = row_normals[d]


def behind_kernel(nvar, coefs, below, above, links, out, stack):
    half = half_jacobians(coefs, nvar)
    is_below = lax.broadcasted_iota(jnp.int32, (2, links.shape[1]), 0) == 0

    def with_j(values):
        return values, transformed(half, values)

    outer, rim = [with_j([behind(below, above, t + v) for v in range(nvar)]) for t in (0, nvar)]
    low, high = pick_both(is_below, outer, rim), pick_both(is_below, rim, outer)
    at = 2 * nvar + 1
    far_flux = face_flux([behind(below, above, at + d) for d in range(2)], *low, *high)
    beside = col_change([behind(below, above, at + 2 + d) for d in range(2)], *rim)
    rows = [jnp.where(is_below, -x, x) + y for x, y in zip(far_flux, beside)]
    links_above = above[pl.ds(2 * nvar + 7, 1), :].astype(jnp.int32)
    for v, x in enumerate(crossed(rows, links[...], links_above, stack)):
        out[v] = x


def state_kernel(at, states, before, out):
    out[...] = states[0, pl.ds(at, out.shape[0])]


def volume_kernel(cells, before, out):
    out[...] = cells[pl.ds(0, 1)]


def own_flux_kernel(nvar, jacobians, near, cell, row_normals, out, coefs):
    strips = out.shape[1] // STRIP
    for d in range(2):
        for v in range(nvar):
            for w in range(nvar):
                coefs[pl.ds((d * nvar + v) * nvar + w, 1), :] = jnp.full(
                    (1, coefs.shape[1]), 0.5 * jacobians[d, v, w], jnp.float32
                )
    half = half_jacobians(coefs, nvar)

    def at(s):
        cells = [near[v, strip(s), :] for v in range(nvar)]
        return [row_normals[d, strip(s), :] for d in range(2)], cells, transformed(half, cells)

    for s, cells, cells_j, along in row_changes(strips, at, lambda v: 0.0, lambda v: 0.0):
        beside = col_change([cell[1 + d, strip(s), :] for d in range(2)], cells, cells_j)
        factor = pseudo_step / cell[0, strip(s), :]
        for v in range(nvar):
            out[v, strip(s), :] = cells[v] - factor * (along[v] + beside[v])


def planes(pieces):
    return [x.at[v] for x in pieces for v in range(x.shape[0])]


def families(n):
    return [0] + list(range(3, n, 2)), [1] + list(range(2, n, 2))


def far_col_kernel(nvar, coefs, cell, *refs):
    states, out = planes(refs[:-1]), refs[-1]
    half = half_jacobians(coefs, nvar)
    for s in range(out.shape[1] // STRIP):
        cells = [states[v][strip(s), :] for v in range(nvar)]
        beside = col_change([cell[1 + d, strip(s), :] for d in range(2)], cells, transformed(half, cells))
        factor = pseudo_step / cell[0, strip(s), :]
        for v in range(nvar):
            out[v, strip(s), :] = cells[v] - factor * beside[v]


def far_face_kernel(nvar, coefs, *refs):
    states, out = planes(refs[:-1]), refs[-1]
    half = half_jacobians(coefs, nvar)
    row = lax.broadcasted_iota(jnp.int32, (STRIP, out.shape[3]), 0)
    before = None
    for s in range(out.shape[2] // STRIP):
        cells = [states[v][strip(s), :] for v in range(nvar)]
        rolled = [pltpu.roll(x, 1, 0) for x in cells]
        lower = rolled if s == 0 else [jnp.where(row == 0, x, y) for x, y in zip(before, rolled)]
        summed = transformed(half, [x + y for x, y in zip(lower, cells)])
        for v in range(nvar):
            out[0, v, strip(s), :] = summed[0][v]
            out[1, v, strip(s), :] = summed[1][v]
            out[2, v, strip(s), :] = cells[v] - lower[v]
        before = rolled


def near_kernel(n, nvar, near, beyond, cell, volumes, part, sizes, *outs):
    here, _ = families(n)
    weights = [[step_weight(n, a, b) for b in (0, 1)] for a in here]
    for s in range(part.shape[1] // STRIP):
        for a in range(len(here)):
            sizes[a, strip(s), :] = weighted(weights[a], [cell[0, strip(s), :], volumes[0, strip(s), :]])
        for v in range(nvar):
            values = [near[v, strip(s), :], beyond[v, strip(s), :]]
            outs[0][v, strip(s), :] = part[v, strip(s), :] - weighted(weights[0], values)
            for a in range(1, len(here)):
                outs[a][v, strip(s), :] = -weighted(weights[a], values)


def time_kernel(n, nvar, near, own, sums, kept, *refs):
    far = n // 2 - 1
    beyond_states, cells, beyond_volumes, *pieces = [refs[far * t : far * (t + 1)] for t in range(3 + len(PIECES))]
    refs = refs[far * (3 + len(PIECES)) :]
    begun, parts = refs[: far + 1], refs[far + 1 : 2 * far + 1]
    rate, outs = refs[2 * far + 1], refs[2 * far + 2 :]
    states = [planes(x) for x in zip(*pieces)]
    here, there = families(n)
    rest = [[step_weight(n, a, b) for b in here[1:] + there[1:]] for a in here]
    strips = outs[0].shape[1] // STRIP
    row = lax.broadcasted_iota(jnp.int32, (STRIP, near.shape[2]), 0)
    for s in range(strips):
        sizes = [x[0, strip(s), :] for x in (own, *cells)]
        far_sizes = sizes[1:] + [x[0, strip(s), :] for x in beyond_volumes]
        rates = [sums[a, strip(s), :] + weighted(rest[a], far_sizes) for a in range(far + 1)]
        factors = [rates[a] / sizes[a] for a in range(far + 1)]
        rate[strip(s), :] = factors[0]
        for v in range(nvar):
            values = [near[v, strip(s), :]] + [x[v][strip(s), :] for x in states]
            others = values[1:] + [x[0, v, strip(s), :] for x in beyond_states]
            moved = [
                begun[a][v, strip(s), :] - weighted(rest[a], others) - factors[a] * values[a]
                for a in range(far + 1)
            ]
            moved = moved[:1] + [moved[a] + parts[a - 1][v, strip(s), :] for a in range(1, far + 1)]
            if s == 0:
                moved[0] = moved[0] + jnp.where(row == 0, pseudo_step * kept[nvar + v][0:1], 0.0) / sizes[0]
            if s == strips - 1:
                lacking = jnp.where(row == STRIP - 1, pseudo_step * kept[nvar + v][1:2], 0.0)
                moved[0] = moved[0] + lacking / sizes[0]
            for a in range(far + 1):
                outs[a][v, strip(s), :] = moved[a]


def base_kernel(n, nvar, coefs, stepped, cell, row_normals, rate, out):
    strips = out.shape[1] // STRIP
    half = half_jacobians(coefs, nvar)
    weight = step_weight(n, 0, 0)

    def at(s):
        cells = [stepped[v, strip(s), :] for v in range(nvar)]
        return [row_normals[d, strip(s), :] for d in range(2)], cells, transformed(half, cells)

    for s, cells, cells_j, along in row_changes(strips, at, lambda v: 0.0, lambda v: 0.0):
        beside = col_change([cell[1 + d, strip(s), :] for d in range(2)], cells, cells_j)
        inverse = 1.0 / cell[0, strip(s), :]
        kept = (1.0 - weight) - rate[strip(s), :]
        for v in range(nvar):
            out[v, strip(s), :] = kept * cells[v] - (pseudo_step * inverse) * (along[v] + beside[v])


def far_step_kernel(n, nvar, coefs, stepped, edge, *refs):
    far = n // 2 - 1
    edges, cells_of, parts, beside, *pieces = [refs[far * t : far * (t + 1)] for t in range(4 + len(PIECES))]
    states = [planes(x) for x in zip(*pieces)]
    shared, out = refs[(4 + len(PIECES)) * far :]
    depth = stepped.shape[1]
    strips = depth // STRIP
    mine = [step_weight(n, 0, b) for b in families(n)[0]]
    other = [step_weight(n, 1, b) for b in families(n)[0]]
    head = edge.shape[0] - 2 * depth
    half = half_jacobians(coefs, nvar)
    is_below = lax.broadcasted_iota(jnp.int32, (2, stepped.shape[2]), 0) == 0
    row = lax.broadcasted_iota(jnp.int32, (STRIP, stepped.shape[2]), 0)

    def changes(a):
        def behind_rows(v):
            return pair(edges[a][pl.ds(v, 1), :], edges[a][pl.ds(nvar + 1 + v, 1), :])

        ends = [pair(states[a][v][pl.ds(0, 1), :], states[a][v][pl.ds(depth - 1, 1), :]) for v in range(nvar)]
        rims = [behind_rows(v) for v in range(nvar)]
        face = [
            pair(edges[a][pl.ds(head + d * depth, 1), :], edges[a][pl.ds(2 * nvar + 2 + d, 1), :])
            for d in range(2)
        ]
        ends_j = transformed(half, [x + y for x, y in zip(ends, rims)])
        spread = jnp.where(is_below, spread_of(face), -spread_of(face))
        across = [
            face[0] * ends_j[0][v] + face[1] * ends_j[1][v] - spread * (ends[v] - rims[v])
            for v in range(nvar)
        ]
        last = None
        for s in range(strips + 1):
            if s < strips:
                normal = [edges[a][pl.ds(head + d * depth + s * STRIP, STRIP), :] for d in range(2)]
                spread = spread_of(normal)
                flux = []
                for v in range(nvar):
                    sums, difference = [beside[a][d, v, strip(s), :] for d in range(2)], beside[a][2, v, strip(s), :]
                    flux.append(normal[0] * sums[0] + normal[1] * sums[1] - spread * difference)
                if s == 0:
                    flux = [jnp.where(row == 0, across[v][0:1], flux[v]) for v in range(nvar)]
                lifted = [pltpu.roll(x, STRIP - 1, 0) for x in flux]
            else:
                lifted = [across[v][1:2] for v in range(nvar)]
            if s > 0:
                yield (
                    s - 1,
                    [jnp.where(row == STRIP - 1, lifted[v], last[1][v]) - last[0][v] for v in range(nvar)],
                )
            last = (flux, lifted)

    for moves in zip(*[changes(a) for a in range(far)]):
        s = moves[0][0]
        factors = [pseudo_step / cells_of[a][0, strip(s), :] for a in range(far)]
        for v in range(nvar):
            given = other[0] * stepped[v, strip(s), :]
            taken = None
            for a in range(far):
                value = parts[a][v, strip(s), :] - factors[a] * moves[a][1][v]
                given = given + other[1 + a] * value
                taken = mine[1 + a] * value if taken is None else taken + mine[1 + a] * value
            shared[pl.ds(v * depth + s * STRIP, STRIP), :] = given
            out[v, strip(s), :] = taken
    rims = pl.ds(0, 2 * nvar + 2)
    shared[pl.ds(nvar * depth, 2 * nvar + 2), :] = weighted(
        other, [edge[rims, :]] + [edges[a][rims, :] for a in range(far)]
    )


def rim_kernel(n, nvar, coefs, edge, kept, others, cell, stepped, *refs):
    far = n // 2 - 1
    edges, out = refs[:far], refs[far]
    depth, columns = stepped.shape[1], stepped.shape[2]
    half = half_jacobians(coefs, nvar)
    weights = [step_weight(n, 0, b) for b in families(n)[0]]
    is_below = lax.broadcasted_iota(jnp.int32, (2, columns), 0) == 0

    def rim(v):
        return weighted(
            weights,
            [
                pair(ref[pl.ds(v, 1), :], ref[pl.ds(nvar + 1 + v, 1), :])
                for ref in [edge] + list(edges)
            ],
        )

    inverse = 1.0 / kept[2 * nvar]
    volume_rate = rim(nvar)
    face = [kept[2 * nvar + 1], kept[2 * nvar + 2]]
    spread = spread_of(face)
    inside = [pair(stepped[v, pl.ds(0, 1), :], stepped[v, pl.ds(depth - 1, 1), :]) for v in range(nvar)]
    inside_j = transformed(half, inside)
    for v in range(nvar):
        change = pseudo_step * (kept[nvar + v] + others[v])
        out[v] = kept[v] - rim(v) - inverse * (kept[v] * volume_rate + change)
        out[nvar + v] = inverse * kept[v]
        out[2 * nvar + v] = (
            face[0] * inside_j[0][v]
            + face[1] * inside_j[1][v]
            + jnp.where(is_below, -spread, spread) * inside[v]
        )
    volume = pair(cell[0, pl.ds(0, 1), :], cell[0, pl.ds(depth - 1, 1), :])
    factor = pseudo_step / volume
    out[3 * nvar] = jnp.where(is_below, factor, -factor)


def final_kernel(nvar, coefs, rims, kept, base, taken, shared, out, held, sems):
    depth, columns = base.shape[1], base.shape[2]
    strips = depth // STRIP
    half = half_jacobians(coefs, nvar)
    is_below = lax.broadcasted_iota(jnp.int32, (2, columns), 0) == 0

    def summed(v):
        return pair(shared[pl.ds(nvar * depth + v, 1), :], shared[pl.ds(nvar * depth + nvar + 1 + v, 1), :])

    def value(v, s):
        other = taken[v, strip(s), :] + shared[pl.ds(v * depth + s * STRIP, STRIP), :]
        return base[v, strip(s), :] - other

    copies = []

    def send(t, first, count):
        where = pl.ds(first * STRIP, count * STRIP)
        copies.append(pltpu.make_async_copy(held.at[:, where], out.at[0, :, where], sems.at[t]))
        copies[-1].start()

    for s in range(1, strips - 1):
        for v in range(nvar):
            held[v, strip(s), :] = value(v, s)
    send(0, 1, strips - 2)
    volume_rate = summed(nvar)
    outside = [rims[v] - summed(v) - rims[nvar + v] * volume_rate for v in range(nvar)]
    outside_j = transformed(half, outside)
    face = [kept[2 * nvar + 1], kept[2 * nvar + 2]]
    spread = spread_of(face)
    signed = jnp.where(is_below, spread, -spread)
    row = lax.broadcasted_iota(jnp.int32, (STRIP, columns), 0)
    for v in range(nvar):
        across = face[0] * outside_j[0][v] + face[1] * outside_j[1][v] + signed * outside[v]
        lacking = rims[3 * nvar] * (across + rims[2 * nvar + v])
        held[v, strip(0), :] = value(v, 0) + jnp.where(row == 0, lacking[0:1], 0.0)
        held[v, strip(strips - 1), :] = value(v, strips - 1) + jnp.where(
            row == STRIP - 1, lacking[1:2], 0.0
        )
    send(1, 0, 1)
    send(2, strips - 1, 1)
    for copy in copies:
        copy.wait()


def body(states, volumes, row_normals, col_normals, face_links, jacobians):
    n = lax.axis_size("inst")
    slabs = lax.axis_size("slab")
    _, nvar, depth, columns = states.shape
    far = list(range(2, n, 2))
    down_rows = -(-(2 * nvar + 8) // 8) * 8
    up_rows = down_rows + 8
    head = -(-(2 * nvar + 4) // 8) * 8

    def f32(*shape):
        return jax.ShapeDtypeStruct(shape, jnp.float32)

    vmem = pl.BlockSpec(memory_space=pltpu.VMEM)
    smem = pl.BlockSpec(memory_space=pltpu.SMEM)
    hbm = pl.BlockSpec(memory_space=pltpu.HBM)
    params = pltpu.CompilerParams(vmem_limit_bytes=24 * 1024 * 1024)

    def call(kernel, name, shapes, *operands, scratch=(), out_spec=vmem):
        single = not isinstance(shapes, list)
        return pl.pallas_call(
            kernel,
            out_shape=shapes,
            in_specs=[smem if x is jacobians else vmem for x in operands],
            out_specs=out_spec if single else [out_spec] * len(shapes),
            scratch_shapes=list(scratch),
            compiler_params=params,
            name=name,
        )(*operands)

    def swapped(x, k):
        return lax.ppermute(x, "inst", [(i, i ^ k) for i in range(n)])

    state_of = {k: swapped(states, k) for k in far}
    inputs = [
        pltpu.with_memory_space_constraint(x, pltpu.HBM)
        for x in (states, volumes, row_normals, col_normals, face_links)
    ]
    near, own_cell, own_rows, own_links, upward, downward = pl.pallas_call(
        pack_kernel,
        out_shape=[
            f32(nvar, depth, columns),
            f32(3, depth, columns),
            f32(2, depth, columns),
            jax.ShapeDtypeStruct(face_links.shape, face_links.dtype),
            f32(up_rows, columns),
            f32(down_rows, columns),
        ],
        in_specs=[hbm] * 5,
        out_specs=[vmem] * 6,
        scratch_shapes=[pltpu.SemaphoreType.DMA((5,))],
        compiler_params=params,
        name="pack",
    )(*inputs)
    cell_of = {k: swapped(own_cell, k + 1) for k in far}
    below = lax.ppermute(upward, "slab", [(i, (i + 1) % slabs) for i in range(slabs)])
    above = lax.ppermute(downward, "slab", [(i, (i - 1) % slabs) for i in range(slabs)])
    field = f32(nvar, depth, columns)
    own_part, coefs = call(
        functools.partial(own_flux_kernel, nvar),
        "own_flux",
        [field, f32(-(-2 * nvar * nvar // 8) * 8, columns)],
        jacobians,
        near,
        own_cell,
        own_rows,
    )
    parts = []
    edge, kept = call(
        functools.partial(edge_kernel, nvar),
        "edges",
        [f32(head + 2 * depth, columns), f32(2 * nvar + 3, 2, columns)],
        coefs,
        below,
        above,
        near,
        own_rows,
        own_links,
        own_part,
        scratch=[pltpu.VMEM((-(-(2 * nvar + 6) // 8) * 8, columns), jnp.float32)],
    )
    others = call(
        functools.partial(behind_kernel, nvar),
        "behind",
        f32(nvar, 2, columns),
        coefs,
        below,
        above,
        own_links,
        scratch=[pltpu.VMEM((-(-2 * nvar // 8) * 8, columns), jnp.float32)],
    )
    edge_of = {k: swapped(edge, k + 1) for k in far}
    beyond = swapped(near, 1)
    sums, *begun = call(
        functools.partial(near_kernel, n, nvar),
        "near",
        [f32(len(far) + 1, depth, columns)] + [field] * (len(far) + 1),
        near,
        beyond,
        own_cell,
        swapped(call(volume_kernel, "volumes", f32(1, depth, columns), own_cell, edge), 1),
        own_part,
    )
    pieces_of, beyond_volumes = dict(), dict()
    for k in far:
        pieces, at = [], 0
        for t, count in enumerate(PIECES):
            before = begun[0] if t + 1 == len(PIECES) else edge
            shape = f32(count, depth, columns)
            kernel = functools.partial(state_kernel, at)
            held = call(kernel, "states", shape, state_of[k], before)
            pieces.append(swapped(held, 1))
            at += count
        pieces_of[k] = pieces
        held = call(volume_kernel, "volumes", f32(1, depth, columns), cell_of[k], begun[0])
        beyond_volumes[k] = swapped(held, 1)

    faces = {}
    for k in far:
        shape = f32(3, nvar, depth, columns)
        faces[k] = call(functools.partial(far_face_kernel, nvar), "far_faces", shape, coefs, *pieces_of[k])
        parts.append(
            call(functools.partial(far_col_kernel, nvar), "far_col", field, coefs, cell_of[k], *pieces_of[k])
        )
    rate, stepped, *parts = call(
        functools.partial(time_kernel, n, nvar),
        "time",
        [f32(depth, columns)] + [field] * (len(far) + 1),
        near,
        own_cell,
        sums,
        kept,
        *[state_of[k] for k in far],
        *[cell_of[k] for k in far],
        *[beyond_volumes[k] for k in far],
        *[pieces_of[k][t] for t in range(len(PIECES)) for k in far],
        *begun,
        *parts,
    )
    base = call(
        functools.partial(base_kernel, n, nvar),
        "base",
        field,
        coefs,
        stepped,
        own_cell,
        own_rows,
        rate,
    )
    shared, taken = call(
        functools.partial(far_step_kernel, n, nvar),
        "far_step",
        [f32(nvar * depth + 16, columns), field],
        coefs,
        stepped,
        edge,
        *[edge_of[k] for k in far],
        *[cell_of[k] for k in far],
        *parts,
        *[faces[k] for k in far],
        *[pieces_of[k][t] for t in range(len(PIECES)) for k in far],
    )
    rims = call(
        functools.partial(rim_kernel, n, nvar),
        "rims",
        f32(3 * nvar + 1, 2, columns),
        coefs,
        edge,
        kept,
        others,
        own_cell,
        stepped,
        *[edge_of[k] for k in far],
    )
    return call(
        functools.partial(final_kernel, nvar),
        "final",
        f32(1, nvar, depth, columns),
        coefs,
        rims,
        kept,
        base,
        taken,
        swapped(shared, 1),
        scratch=[pltpu.VMEM((nvar, depth, columns), jnp.float32), pltpu.SemaphoreType.DMA((3,))],
        out_spec=hbm,
    )


def solution(mesh):
    return jax.shard_map(
        body,
        mesh=mesh,
        in_specs=(
            P(("grp", "inst"), None, "slab", None),
            P(("grp", "inst"), "slab", None),
            P(("grp", "inst"), None, "slab", None),
            P(("grp", "inst"), None, "slab", None),
            P("slab", None),
            P(),
        ),
        out_specs=P(("grp", "inst"), None, "slab", None),
        check_vma=False,
    )
```

```python
import functools

import jax
import jax.numpy as jnp
import numpy as np
from jax import lax
from jax.experimental import pallas as pl
from jax.experimental.pallas import tpu as pltpu
from jax.sharding import PartitionSpec as P

frequency = 0.5
pseudo_step = 0.2
nyquist_damping = 0.25

STRIP = 8
PIECES = (2, 2, 1)


def spectral_table(instances):
    offsets = np.arange(instances)[:, None] - np.arange(instances)[None, :]
    phases = np.pi * offsets / instances
    sine_safe = np.where(offsets == 0, 1.0, np.sin(phases))
    parity = np.where(offsets % 2 == 0, 1.0, -1.0)
    matrix = np.where(offsets == 0, 0.0, 0.5 * frequency * parity * np.cos(phases) / sine_safe)
    matrix = matrix + nyquist_damping * parity
    return matrix.astype(np.float32)


def pack_kernel(states, volumes, row_normals, col_normals, links, near, cell, rows, own_links, upward, downward, sems):
    nvar, depth = states.shape[1], states.shape[2]
    pairs = [
        (states.at[0], near),
        (volumes, cell.at[pl.ds(0, 1)]),
        (col_normals.at[0], cell.at[pl.ds(1, 2)]),
        (row_normals.at[0], rows),
        (links, own_links),
    ]
    copies = [pltpu.make_async_copy(a, b, sems.at[t]) for t, (a, b) in enumerate(pairs)]
    for copy in copies:
        copy.start()
    for copy in copies:
        copy.wait()

    def put(ref, second, edge, face):
        for v in range(nvar):
            ref[pl.ds(v, 1), :] = near[v, pl.ds(second, 1), :]
            ref[pl.ds(nvar + v, 1), :] = near[v, pl.ds(edge, 1), :]
        ref[pl.ds(2 * nvar, 1), :] = cell[0, pl.ds(edge, 1), :]
        for d in range(2):
            ref[pl.ds(2 * nvar + 1 + d, 1), :] = rows[d, pl.ds(face, 1), :]
            ref[pl.ds(2 * nvar + 3 + d, 1), :] = cell[1 + d, pl.ds(edge, 1), :]

    put(upward, depth - 2, depth - 1, depth - 1)
    put(downward, 1, 0, 1)
    for d in range(2):
        downward[pl.ds(2 * nvar + 5 + d, 1), :] = rows[d, pl.ds(0, 1), :]
    downward[pl.ds(2 * nvar + 7, 1), :] = own_links[...].astype(jnp.float32)


def half_jacobians(coefs, nvar):
    return [
        [[coefs[pl.ds((d * nvar + v) * nvar + w, 1), :] for w in range(nvar)] for v in range(nvar)]
        for d in range(2)
    ]


def step_weight(n, row, col):
    me = lax.axis_index("inst")
    values = [np.float32(pseudo_step) * spectral_table(n)[i ^ row, i ^ col] for i in range(n)]
    weight = values[0]
    for i in range(1, n):
        weight = jnp.where(me == i, values[i], weight)
    return weight


def weighted(weights, values):
    total = weights[0] * values[0]
    for weight, value in zip(weights[1:], values[1:]):
        total = total + weight * value
    return total


def transformed(half, values):
    return [[weighted(half[d][v], values) for v in range(len(values))] for d in range(2)]


def spread_of(normal):
    return 0.5 * (jnp.abs(normal[0]) + jnp.abs(normal[1]))


def own_side(normal, values, values_j):
    spread = spread_of(normal)
    return [
        normal[0] * values_j[0][v] + normal[1] * values_j[1][v] - spread * values[v]
        for v in range(len(values))
    ]


def other_side(normal, values, values_j):
    spread = spread_of(normal)
    return [
        normal[0] * values_j[0][v] + normal[1] * values_j[1][v] + spread * values[v]
        for v in range(len(values))
    ]


def col_change(normal, values, values_j):
    columns = values[0].shape[1]
    upper_normal = [pltpu.roll(x, columns - 1, 1) for x in normal]
    own = own_side(normal, values, values_j)
    other = other_side(upper_normal, values, values_j)
    flux = [a + pltpu.roll(b, 1, 1) for a, b in zip(own, other)]
    return [pltpu.roll(x, columns - 1, 1) - x for x in flux]


def row_changes(count, at, first_flux, last_flux):
    last = None
    ahead = at(0)
    for s in range(count):
        faces, cells, cells_j = ahead
        nvar = len(cells)
        row = lax.broadcasted_iota(jnp.int32, cells[0].shape, 0)
        top, bottom = row == 0, row == STRIP - 1
        rolled_faces = [pltpu.roll(x, STRIP - 1, 0) for x in faces]
        if s + 1 < count:
            ahead = at(s + 1)
            rolled_faces = [
                jnp.where(bottom, pltpu.roll(x, STRIP - 1, 0), y) for x, y in zip(ahead[0], rolled_faces)
            ]
        own = own_side(faces, cells, cells_j)
        rolled = [pltpu.roll(x, 1, 0) for x in other_side(rolled_faces, cells, cells_j)]
        if s == 0:
            flux = [jnp.where(top, first_flux(v), own[v] + rolled[v]) for v in range(nvar)]
        else:
            flux = [own[v] + jnp.where(top, before[v], rolled[v]) for v in range(nvar)]
        lifted = [pltpu.roll(x, STRIP - 1, 0) for x in flux]
        if last is not None:
            yield (
                s - 1,
                last[0],
                last[1],
                [jnp.where(bottom, lifted[v], last[3][v]) - last[2][v] for v in range(nvar)],
            )
        before, last = rolled, (cells, cells_j, flux, lifted)
    yield (
        count - 1,
        last[0],
        last[1],
        [jnp.where(bottom, last_flux(v), last[3][v]) - last[2][v] for v in range(nvar)],
    )


def strip(s):
    return pl.ds(s * STRIP, STRIP)


def face_flux(normal, lower, lower_j, upper, upper_j):
    spread = spread_of(normal)
    return [
        normal[0] * (lower_j[0][v] + upper_j[0][v])
        + normal[1] * (lower_j[1][v] + upper_j[1][v])
        - spread * (upper[v] - lower[v])
        for v in range(len(lower))
    ]


def split_dot(x, onehot, transposed):
    high = x.astype(jnp.bfloat16)
    rest = x - high.astype(jnp.float32)
    middle = rest.astype(jnp.bfloat16)
    low = (rest - middle.astype(jnp.float32)).astype(jnp.bfloat16)
    count = x.shape[0]
    stacked = jnp.concatenate([high, middle, low], axis=0)
    out = lax.dot_general(
        stacked,
        onehot,
        (((1,), (1 if transposed else 0,)), ((), ())),
        preferred_element_type=jnp.float32,
    )
    return out[:count] + (out[count : 2 * count] + out[2 * count :])


def pair(below, above):
    return jnp.concatenate([below, above], axis=0)


def pick(mask, a, b):
    return [jnp.where(mask, x, y) for x, y in zip(a, b)]


def pick_both(mask, a, b):
    return pick(mask, a[0], b[0]), [pick(mask, x, y) for x, y in zip(a[1], b[1])]


def behind(below, above, t):
    return pair(below[pl.ds(t, 1), :], above[pl.ds(t, 1), :])


def crossed(rows, links_below, links_above, stack):
    stack[...] = jnp.zeros(stack.shape, jnp.float32)
    for t, x in enumerate(rows):
        stack[pl.ds(2 * t, 2), :] = x
    columns = stack.shape[1]
    cell = lax.broadcasted_iota(jnp.int32, (columns, columns), 0)
    onehots = [(cell == x).astype(jnp.float32).astype(jnp.bfloat16) for x in (links_below, links_above)]
    stacked = stack[...]
    side = lax.broadcasted_iota(jnp.int32, stacked.shape, 0) % 2
    stack[...] = jnp.where(
        side == 0, split_dot(stacked, onehots[0], False), split_dot(stacked, onehots[1], True)
    )
    return [stack[pl.ds(2 * t, 2), :] for t in range(len(rows))]


def edge_kernel(nvar, coefs, below, above, near, row_normals, links, early, out, kept, stack):
    depth, columns = near.shape[1], near.shape[2]
    half = half_jacobians(coefs, nvar)
    is_below = lax.broadcasted_iota(jnp.int32, (2, columns), 0) == 0
    inner_face = [
        pair(row_normals[d, pl.ds(0, 1), :], above[pl.ds(2 * nvar + 5 + d, 1), :]) for d in range(2)
    ]
    rows = [behind(below, above, nvar + v) for v in range(nvar + 1)] + inner_face
    links_above = above[pl.ds(2 * nvar + 7, 1), :].astype(jnp.int32)
    rows = crossed(rows, links[...], links_above, stack)
    rim, volume, face = rows[:nvar], rows[nvar], pick(is_below, inner_face, rows[nvar + 1 :])
    inside = [pair(near[v, pl.ds(0, 1), :], near[v, pl.ds(depth - 1, 1), :]) for v in range(nvar)]
    low, high = pick(is_below, rim, inside), pick(is_below, inside, rim)
    summed = transformed(half, [x + y for x, y in zip(low, high)])
    spread = spread_of(face)
    across = [
        face[0] * summed[0][v] + face[1] * summed[1][v] - spread * (high[v] - low[v]) for v in range(nvar)
    ]
    for v in range(nvar):
        kept[v] = rim[v]
        kept[nvar + v] = jnp.where(is_below, across[v], -across[v])
    for v, x in enumerate(rim + [volume]):
        out[pl.ds(v, 1), :] = x[0:1]
        out[pl.ds(nvar + 1 + v, 1), :] = x[1:2]
    kept[2 * nvar] = volume
    for d in range(2):
        out[pl.ds(2 * nvar + 2 + d, 1), :] = face[d][1:2]
        kept[2 * nvar + 1 + d] = face[d]
    head = out.shape[0] - 2 * depth
    for d in range(2):
        out[pl.ds(head + d * depth, depth), :] = row_normals[d]


def behind_kernel(nvar, coefs, below, above, links, out, stack):
    half = half_jacobians(coefs, nvar)
    is_below = lax.broadcasted_iota(jnp.int32, (2, links.shape[1]), 0) == 0

    def with_j(values):
        return values, transformed(half, values)

    outer, rim = [with_j([behind(below, above, t + v) for v in range(nvar)]) for t in (0, nvar)]
    low, high = pick_both(is_below, outer, rim), pick_both(is_below, rim, outer)
    at = 2 * nvar + 1
    far_flux = face_flux([behind(below, above, at + d) for d in range(2)], *low, *high)
    beside = col_change([behind(below, above, at + 2 + d) for d in range(2)], *rim)
    rows = [jnp.where(is_below, -x, x) + y for x, y in zip(far_flux, beside)]
    links_above = above[pl.ds(2 * nvar + 7, 1), :].astype(jnp.int32)
    for v, x in enumerate(crossed(rows, links[...], links_above, stack)):
        out[v] = x


def state_kernel(at, states, before, out):
    out[...] = states[0, pl.ds(at, out.shape[0])]


def volume_kernel(cells, before, out):
    out[...] = cells[pl.ds(0, 1)]


def own_flux_kernel(nvar, jacobians, near, cell, row_normals, out, coefs):
    strips = out.shape[1] // STRIP
    for d in range(2):
        for v in range(nvar):
            for w in range(nvar):
                coefs[pl.ds((d * nvar + v) * nvar + w, 1), :] = jnp.full(
                    (1, coefs.shape[1]), 0.5 * jacobians[d, v, w], jnp.float32
                )
    half = half_jacobians(coefs, nvar)

    def at(s):
        cells = [near[v, strip(s), :] for v in range(nvar)]
        return [row_normals[d, strip(s), :] for d in range(2)], cells, transformed(half, cells)

    for s, cells, cells_j, along in row_changes(strips, at, lambda v: 0.0, lambda v: 0.0):
        beside = col_change([cell[1 + d, strip(s), :] for d in range(2)], cells, cells_j)
        factor = pseudo_step / cell[0, strip(s), :]
        for v in range(nvar):
            out[v, strip(s), :] = cells[v] - factor * (along[v] + beside[v])


def planes(pieces):
    return [x.at[v] for x in pieces for v in range(x.shape[0])]


def families(n):
    return [0] + list(range(3, n, 2)), [1] + list(range(2, n, 2))


def far_col_kernel(nvar, coefs, cell, *refs):
    states, out = planes(refs[:-1]), refs[-1]
    half = half_jacobians(coefs, nvar)
    for s in range(out.shape[1] // STRIP):
        cells = [states[v][strip(s), :] for v in range(nvar)]
        beside = col_change([cell[1 + d, strip(s), :] for d in range(2)], cells, transformed(half, cells))
        factor = pseudo_step / cell[0, strip(s), :]
        for v in range(nvar):
            out[v, strip(s), :] = cells[v] - factor * beside[v]


def far_face_kernel(nvar, coefs, *refs):
    states, out = planes(refs[:-1]), refs[-1]
    half = half_jacobians(coefs, nvar)
    row = lax.broadcasted_iota(jnp.int32, (STRIP, out.shape[3]), 0)
    before = None
    for s in range(out.shape[2] // STRIP):
        cells = [states[v][strip(s), :] for v in range(nvar)]
        rolled = [pltpu.roll(x, 1, 0) for x in cells]
        lower = rolled if s == 0 else [jnp.where(row == 0, x, y) for x, y in zip(before, rolled)]
        summed = transformed(half, [x + y for x, y in zip(lower, cells)])
        for v in range(nvar):
            out[0, v, strip(s), :] = summed[0][v]
            out[1, v, strip(s), :] = summed[1][v]
            out[2, v, strip(s), :] = cells[v] - lower[v]
        before = rolled


def near_kernel(n, nvar, near, beyond, cell, volumes, part, sizes, *outs):
    here, _ = families(n)
    weights = [[step_weight(n, a, b) for b in (0, 1)] for a in here]
    for s in range(part.shape[1] // STRIP):
        for a in range(len(here)):
            sizes[a, strip(s), :] = weighted(weights[a], [cell[0, strip(s), :], volumes[0, strip(s), :]])
        for v in range(nvar):
            values = [near[v, strip(s), :], beyond[v, strip(s), :]]
            outs[0][v, strip(s), :] = part[v, strip(s), :] - weighted(weights[0], values)
            for a in range(1, len(here)):
                outs[a][v, strip(s), :] = -weighted(weights[a], values)


def time_kernel(n, nvar, near, own, sums, kept, *refs):
    far = n // 2 - 1
    beyond_states, cells, beyond_volumes, *pieces = [refs[far * t : far * (t + 1)] for t in range(3 + len(PIECES))]
    refs = refs[far * (3 + len(PIECES)) :]
    begun, parts = refs[: far + 1], refs[far + 1 : 2 * far + 1]
    rate, early, outs = refs[2 * far + 1], refs[2 * far + 2], refs[2 * far + 3 :]
    other = [step_weight(n, 1, b) for b in families(n)[0]]
    states = [planes(x) for x in zip(*pieces)]
    here, there = families(n)
    rest = [[step_weight(n, a, b) for b in here[1:] + there[1:]] for a in here]
    strips = outs[0].shape[1] // STRIP
    row = lax.broadcasted_iota(jnp.int32, (STRIP, near.shape[2]), 0)
    for s in range(strips):
        sizes = [x[0, strip(s), :] for x in (own, *cells)]
        far_sizes = sizes[1:] + [x[0, strip(s), :] for x in beyond_volumes]
        rates = [sums[a, strip(s), :] + weighted(rest[a], far_sizes) for a in range(far + 1)]
        factors = [rates[a] / sizes[a] for a in range(far + 1)]
        rate[strip(s), :] = factors[0]
        for v in range(nvar):
            values = [near[v, strip(s), :]] + [x[v][strip(s), :] for x in states]
            others = values[1:] + [x[0, v, strip(s), :] for x in beyond_states]
            moved = [
                begun[a][v, strip(s), :] - weighted(rest[a], others) - factors[a] * values[a]
                for a in range(far + 1)
            ]
            moved = moved[:1] + [moved[a] + parts[a - 1][v, strip(s), :] for a in range(1, far + 1)]
            if s == 0:
                moved[0] = moved[0] + jnp.where(row == 0, pseudo_step * kept[nvar + v][0:1], 0.0) / sizes[0]
            if s == strips - 1:
                lacking = jnp.where(row == STRIP - 1, pseudo_step * kept[nvar + v][1:2], 0.0)
                moved[0] = moved[0] + lacking / sizes[0]
            for a in range(far + 1):
                outs[a][v, strip(s), :] = moved[a]
            early[v, strip(s), :] = weighted(other, moved)


def base_kernel(n, nvar, coefs, stepped, cell, row_normals, rate, *refs):
    parts, out = refs[:-1], refs[-1]
    strips = out.shape[1] // STRIP
    half = half_jacobians(coefs, nvar)
    weight, *rest = [step_weight(n, 0, b) for b in families(n)[0]]

    def at(s):
        cells = [stepped[v, strip(s), :] for v in range(nvar)]
        return [row_normals[d, strip(s), :] for d in range(2)], cells, transformed(half, cells)

    for s, cells, cells_j, along in row_changes(strips, at, lambda v: 0.0, lambda v: 0.0):
        beside = col_change([cell[1 + d, strip(s), :] for d in range(2)], cells, cells_j)
        inverse = 1.0 / cell[0, strip(s), :]
        kept = (1.0 - weight) - rate[strip(s), :]
        for v in range(nvar):
            value = kept * cells[v] - (pseudo_step * inverse) * (along[v] + beside[v])
            out[v, strip(s), :] = value - weighted(rest, [x[v, strip(s), :] for x in parts])


def far_step_kernel(n, nvar, coefs, early, edge, *refs):
    far = n // 2 - 1
    edges, cells_of, beside, *pieces = [refs[far * t : far * (t + 1)] for t in range(3 + len(PIECES))]
    states = [planes(x) for x in zip(*pieces)]
    shared, outs = refs[far * (3 + len(PIECES))], refs[far * (3 + len(PIECES)) + 1 :]
    depth, columns = early.shape[1], early.shape[2]
    strips = depth // STRIP
    other = [step_weight(n, 1, b) for b in families(n)[0]]
    head = edge.shape[0] - 2 * depth
    half = half_jacobians(coefs, nvar)
    is_below = lax.broadcasted_iota(jnp.int32, (2, columns), 0) == 0
    row = lax.broadcasted_iota(jnp.int32, (STRIP, columns), 0)

    def interface(a):
        ends = [pair(states[a][v][pl.ds(0, 1), :], states[a][v][pl.ds(depth - 1, 1), :]) for v in range(nvar)]
        rims = [pair(edges[a][pl.ds(v, 1), :], edges[a][pl.ds(nvar + 1 + v, 1), :]) for v in range(nvar)]
        face = [
            pair(edges[a][pl.ds(head + d * depth, 1), :], edges[a][pl.ds(2 * nvar + 2 + d, 1), :])
            for d in range(2)
        ]
        ends_j = transformed(half, [x + y for x, y in zip(ends, rims)])
        spread = jnp.where(is_below, spread_of(face), -spread_of(face))
        return [
            face[0] * ends_j[0][v] + face[1] * ends_j[1][v] - spread * (ends[v] - rims[v]) for v in range(nvar)
        ]

    def flux_of(a, s):
        normal = [edges[a][pl.ds(head + d * depth + s * STRIP, STRIP), :] for d in range(2)]
        spread = spread_of(normal)
        flux = []
        for v in range(nvar):
            sums, difference = [beside[a][d, v, strip(s), :] for d in range(2)], beside[a][2, v, strip(s), :]
            flux.append(normal[0] * sums[0] + normal[1] * sums[1] - spread * difference)
        return flux, [pltpu.roll(x, STRIP - 1, 0) for x in flux]

    across = [None] * far
    fluxes = [[None] * (strips + 1) for _ in range(far)]
    for s in list(range(2, strips)) + [1, strips, 0]:
        for a in range(far):
            if s in (strips, 0) and across[a] is None:
                across[a] = interface(a)
            if s == strips:
                fluxes[a][s] = (None, [across[a][v][1:2] for v in range(nvar)])
            else:
                fluxes[a][s] = flux_of(a, s)
            if s == 0:
                flux = [jnp.where(row == 0, across[a][v][0:1], fluxes[a][0][0][v]) for v in range(nvar)]
                fluxes[a][0] = (flux, fluxes[a][0][1])
        for t in {2: [], 1: [1], strips: [strips - 1], 0: [0]}.get(s, [s - 1]):
            factors = [pseudo_step / cells_of[a][0, strip(t), :] for a in range(far)]
            for v in range(nvar):
                total = early[v, strip(t), :]
                for a in range(far):
                    above = jnp.where(row == STRIP - 1, fluxes[a][t + 1][1][v], fluxes[a][t][1][v])
                    value = factors[a] * (above - fluxes[a][t][0][v])
                    outs[a][v, strip(t), :] = value
                    total = total - other[1 + a] * value
                shared[pl.ds(v * depth + t * STRIP, STRIP), :] = total
    rims = pl.ds(0, 2 * nvar + 2)
    shared[pl.ds(nvar * depth, 2 * nvar + 2), :] = weighted(
        other, [edge[rims, :]] + [edges[a][rims, :] for a in range(far)]
    )


def rim_kernel(n, nvar, coefs, edge, kept, others, cell, stepped, *refs):
    far = n // 2 - 1
    edges, out = refs[:far], refs[far]
    depth, columns = stepped.shape[1], stepped.shape[2]
    half = half_jacobians(coefs, nvar)
    weights = [step_weight(n, 0, b) for b in families(n)[0]]
    is_below = lax.broadcasted_iota(jnp.int32, (2, columns), 0) == 0

    def rim(v):
        return weighted(
            weights,
            [
                pair(ref[pl.ds(v, 1), :], ref[pl.ds(nvar + 1 + v, 1), :])
                for ref in [edge] + list(edges)
            ],
        )

    inverse = 1.0 / kept[2 * nvar]
    volume_rate = rim(nvar)
    face = [kept[2 * nvar + 1], kept[2 * nvar + 2]]
    spread = spread_of(face)
    inside = [pair(stepped[v, pl.ds(0, 1), :], stepped[v, pl.ds(depth - 1, 1), :]) for v in range(nvar)]
    inside_j = transformed(half, inside)
    for v in range(nvar):
        change = pseudo_step * (kept[nvar + v] + others[v])
        out[v] = kept[v] - rim(v) - inverse * (kept[v] * volume_rate + change)
        out[nvar + v] = inverse * kept[v]
        out[2 * nvar + v] = (
            face[0] * inside_j[0][v]
            + face[1] * inside_j[1][v]
            + jnp.where(is_below, -spread, spread) * inside[v]
        )
    volume = pair(cell[0, pl.ds(0, 1), :], cell[0, pl.ds(depth - 1, 1), :])
    factor = pseudo_step / volume
    out[3 * nvar] = jnp.where(is_below, factor, -factor)


def final_kernel(n, nvar, coefs, rims, kept, base, shared, *refs):
    rows, (out, held, sems) = refs[:-3], refs[-3:]
    weights = [step_weight(n, 0, b) for b in families(n)[0][1:]]
    depth, columns = base.shape[1], base.shape[2]
    strips = depth // STRIP
    half = half_jacobians(coefs, nvar)
    is_below = lax.broadcasted_iota(jnp.int32, (2, columns), 0) == 0

    def summed(v):
        return pair(shared[pl.ds(nvar * depth + v, 1), :], shared[pl.ds(nvar * depth + nvar + 1 + v, 1), :])

    def value(v, s):
        total = base[v, strip(s), :] - shared[pl.ds(v * depth + s * STRIP, STRIP), :]
        return total + weighted(weights, [x[v, strip(s), :] for x in rows])

    copies = []

    def send(t, first, count):
        where = pl.ds(first * STRIP, count * STRIP)
        copies.append(pltpu.make_async_copy(held.at[:, where], out.at[0, :, where], sems.at[t]))
        copies[-1].start()

    for s in range(1, strips - 1):
        for v in range(nvar):
            held[v, strip(s), :] = value(v, s)
    send(0, 1, strips - 2)
    volume_rate = summed(nvar)
    outside = [rims[v] - summed(v) - rims[nvar + v] * volume_rate for v in range(nvar)]
    outside_j = transformed(half, outside)
    face = [kept[2 * nvar + 1], kept[2 * nvar + 2]]
    spread = spread_of(face)
    signed = jnp.where(is_below, spread, -spread)
    row = lax.broadcasted_iota(jnp.int32, (STRIP, columns), 0)
    for v in range(nvar):
        across = face[0] * outside_j[0][v] + face[1] * outside_j[1][v] + signed * outside[v]
        lacking = rims[3 * nvar] * (across + rims[2 * nvar + v])
        held[v, strip(0), :] = value(v, 0) + jnp.where(row == 0, lacking[0:1], 0.0)
        held[v, strip(strips - 1), :] = value(v, strips - 1) + jnp.where(
            row == STRIP - 1, lacking[1:2], 0.0
        )
    send(1, 0, 1)
    send(2, strips - 1, 1)
    for copy in copies:
        copy.wait()


def body(states, volumes, row_normals, col_normals, face_links, jacobians):
    n = lax.axis_size("inst")
    slabs = lax.axis_size("slab")
    _, nvar, depth, columns = states.shape
    far = list(range(2, n, 2))
    down_rows = -(-(2 * nvar + 8) // 8) * 8
    up_rows = down_rows + 8
    head = -(-(2 * nvar + 4) // 8) * 8

    def f32(*shape):
        return jax.ShapeDtypeStruct(shape, jnp.float32)

    vmem = pl.BlockSpec(memory_space=pltpu.VMEM)
    smem = pl.BlockSpec(memory_space=pltpu.SMEM)
    hbm = pl.BlockSpec(memory_space=pltpu.HBM)
    params = pltpu.CompilerParams(vmem_limit_bytes=24 * 1024 * 1024)

    def call(kernel, name, shapes, *operands, scratch=(), out_spec=vmem):
        single = not isinstance(shapes, list)
        return pl.pallas_call(
            kernel,
            out_shape=shapes,
            in_specs=[smem if x is jacobians else vmem for x in operands],
            out_specs=out_spec if single else [out_spec] * len(shapes),
            scratch_shapes=list(scratch),
            compiler_params=params,
            name=name,
        )(*operands)

    def swapped(x, k):
        return lax.ppermute(x, "inst", [(i, i ^ k) for i in range(n)])

    state_of = {k: swapped(states, k) for k in far}
    inputs = [
        pltpu.with_memory_space_constraint(x, pltpu.HBM)
        for x in (states, volumes, row_normals, col_normals, face_links)
    ]
    near, own_cell, own_rows, own_links, upward, downward = pl.pallas_call(
        pack_kernel,
        out_shape=[
            f32(nvar, depth, columns),
            f32(3, depth, columns),
            f32(2, depth, columns),
            jax.ShapeDtypeStruct(face_links.shape, face_links.dtype),
            f32(up_rows, columns),
            f32(down_rows, columns),
        ],
        in_specs=[hbm] * 5,
        out_specs=[vmem] * 6,
        scratch_shapes=[pltpu.SemaphoreType.DMA((5,))],
        compiler_params=params,
        name="pack",
    )(*inputs)
    cell_of = {k: swapped(own_cell, k + 1) for k in far}
    below = lax.ppermute(upward, "slab", [(i, (i + 1) % slabs) for i in range(slabs)])
    above = lax.ppermute(downward, "slab", [(i, (i - 1) % slabs) for i in range(slabs)])
    field = f32(nvar, depth, columns)
    own_part, coefs = call(
        functools.partial(own_flux_kernel, nvar),
        "own_flux",
        [field, f32(-(-2 * nvar * nvar // 8) * 8, columns)],
        jacobians,
        near,
        own_cell,
        own_rows,
    )
    parts = []
    edge, kept = call(
        functools.partial(edge_kernel, nvar),
        "edges",
        [f32(head + 2 * depth, columns), f32(2 * nvar + 3, 2, columns)],
        coefs,
        below,
        above,
        near,
        own_rows,
        own_links,
        own_part,
        scratch=[pltpu.VMEM((-(-(2 * nvar + 6) // 8) * 8, columns), jnp.float32)],
    )
    others = call(
        functools.partial(behind_kernel, nvar),
        "behind",
        f32(nvar, 2, columns),
        coefs,
        below,
        above,
        own_links,
        scratch=[pltpu.VMEM((-(-2 * nvar // 8) * 8, columns), jnp.float32)],
    )
    edge_of = {k: swapped(edge, k + 1) for k in far}
    beyond = swapped(near, 1)
    sums, *begun = call(
        functools.partial(near_kernel, n, nvar),
        "near",
        [f32(len(far) + 1, depth, columns)] + [field] * (len(far) + 1),
        near,
        beyond,
        own_cell,
        swapped(call(volume_kernel, "volumes", f32(1, depth, columns), own_cell, edge), 1),
        own_part,
    )
    pieces_of, beyond_volumes = dict(), dict()
    for k in far:
        pieces, at = [], 0
        for t, count in enumerate(PIECES):
            before = begun[0] if t + 1 == len(PIECES) else edge
            shape = f32(count, depth, columns)
            kernel = functools.partial(state_kernel, at)
            held = call(kernel, "states", shape, state_of[k], before)
            pieces.append(swapped(held, 1))
            at += count
        pieces_of[k] = pieces
        held = call(volume_kernel, "volumes", f32(1, depth, columns), cell_of[k], begun[0])
        beyond_volumes[k] = swapped(held, 1)

    faces = {}
    for k in far:
        shape = f32(3, nvar, depth, columns)
        faces[k] = call(functools.partial(far_face_kernel, nvar), "far_faces", shape, coefs, *pieces_of[k])
        parts.append(
            call(functools.partial(far_col_kernel, nvar), "far_col", field, coefs, cell_of[k], *pieces_of[k])
        )
    rate, early, stepped, *parts = call(
        functools.partial(time_kernel, n, nvar),
        "time",
        [f32(depth, columns)] + [field] * (len(far) + 2),
        near,
        own_cell,
        sums,
        kept,
        *[state_of[k] for k in far],
        *[cell_of[k] for k in far],
        *[beyond_volumes[k] for k in far],
        *[pieces_of[k][t] for t in range(len(PIECES)) for k in far],
        *begun,
        *parts,
    )
    base = call(
        functools.partial(base_kernel, n, nvar),
        "base",
        field,
        coefs,
        stepped,
        own_cell,
        own_rows,
        rate,
        *parts,
    )
    shared, *rows = call(
        functools.partial(far_step_kernel, n, nvar),
        "far_step",
        [f32(nvar * depth + 16, columns)] + [field] * len(far),
        coefs,
        early,
        edge,
        *[edge_of[k] for k in far],
        *[cell_of[k] for k in far],
        *[faces[k] for k in far],
        *[pieces_of[k][t] for t in range(len(PIECES)) for k in far],
    )
    rims = call(
        functools.partial(rim_kernel, n, nvar),
        "rims",
        f32(3 * nvar + 1, 2, columns),
        coefs,
        edge,
        kept,
        others,
        own_cell,
        stepped,
        *[edge_of[k] for k in far],
    )
    return call(
        functools.partial(final_kernel, n, nvar),
        "final",
        f32(1, nvar, depth, columns),
        coefs,
        rims,
        kept,
        base,
        swapped(shared, 1),
        *rows,
        scratch=[pltpu.VMEM((nvar, depth, columns), jnp.float32), pltpu.SemaphoreType.DMA((3,))],
        out_spec=hbm,
    )


def solution(mesh):
    return jax.shard_map(
        body,
        mesh=mesh,
        in_specs=(
            P(("grp", "inst"), None, "slab", None),
            P(("grp", "inst"), "slab", None),
            P(("grp", "inst"), None, "slab", None),
            P(("grp", "inst"), None, "slab", None),
            P("slab", None),
            P(),
        ),
        out_specs=P(("grp", "inst"), None, "slab", None),
        check_vma=False,
    )
```

```python
import functools

import jax
import jax.numpy as jnp
import numpy as np
from jax import lax
from jax.experimental import pallas as pl
from jax.experimental.pallas import tpu as pltpu
from jax.sharding import PartitionSpec as P

frequency = 0.5
pseudo_step = 0.2
nyquist_damping = 0.25

STRIP = 8
PIECES = (2, 2, 1)


def spectral_table(instances):
    offsets = np.arange(instances)[:, None] - np.arange(instances)[None, :]
    phases = np.pi * offsets / instances
    sine_safe = np.where(offsets == 0, 1.0, np.sin(phases))
    parity = np.where(offsets % 2 == 0, 1.0, -1.0)
    matrix = np.where(offsets == 0, 0.0, 0.5 * frequency * parity * np.cos(phases) / sine_safe)
    matrix = matrix + nyquist_damping * parity
    return matrix.astype(np.float32)


def pack_kernel(states, volumes, row_normals, col_normals, links, near, cell, rows, own_links, upward, downward, sems):
    nvar, depth = states.shape[1], states.shape[2]
    pairs = [
        (states.at[0], near),
        (volumes, cell.at[pl.ds(0, 1)]),
        (col_normals.at[0], cell.at[pl.ds(1, 2)]),
        (row_normals.at[0], rows),
        (links, own_links),
    ]
    copies = [pltpu.make_async_copy(a, b, sems.at[t]) for t, (a, b) in enumerate(pairs)]
    for copy in copies:
        copy.start()
    for copy in copies:
        copy.wait()

    def put(ref, second, edge, face):
        for v in range(nvar):
            ref[pl.ds(v, 1), :] = near[v, pl.ds(second, 1), :]
            ref[pl.ds(nvar + v, 1), :] = near[v, pl.ds(edge, 1), :]
        ref[pl.ds(2 * nvar, 1), :] = cell[0, pl.ds(edge, 1), :]
        for d in range(2):
            ref[pl.ds(2 * nvar + 1 + d, 1), :] = rows[d, pl.ds(face, 1), :]
            ref[pl.ds(2 * nvar + 3 + d, 1), :] = cell[1 + d, pl.ds(edge, 1), :]

    put(upward, depth - 2, depth - 1, depth - 1)
    put(downward, 1, 0, 1)
    for d in range(2):
        downward[pl.ds(2 * nvar + 5 + d, 1), :] = rows[d, pl.ds(0, 1), :]
    downward[pl.ds(2 * nvar + 7, 1), :] = own_links[...].astype(jnp.float32)


def half_jacobians(coefs, nvar):
    return [
        [[coefs[pl.ds((d * nvar + v) * nvar + w, 1), :] for w in range(nvar)] for v in range(nvar)]
        for d in range(2)
    ]


def step_weight(n, row, col):
    me = lax.axis_index("inst")
    values = [np.float32(pseudo_step) * spectral_table(n)[i ^ row, i ^ col] for i in range(n)]
    weight = values[0]
    for i in range(1, n):
        weight = jnp.where(me == i, values[i], weight)
    return weight


def weighted(weights, values):
    total = weights[0] * values[0]
    for weight, value in zip(weights[1:], values[1:]):
        total = total + weight * value
    return total


def transformed(half, values):
    return [[weighted(half[d][v], values) for v in range(len(values))] for d in range(2)]


def spread_of(normal):
    return 0.5 * (jnp.abs(normal[0]) + jnp.abs(normal[1]))


def own_side(normal, values, values_j):
    spread = spread_of(normal)
    return [
        normal[0] * values_j[0][v] + normal[1] * values_j[1][v] - spread * values[v]
        for v in range(len(values))
    ]


def other_side(normal, values, values_j):
    spread = spread_of(normal)
    return [
        normal[0] * values_j[0][v] + normal[1] * values_j[1][v] + spread * values[v]
        for v in range(len(values))
    ]


def col_change(normal, values, values_j):
    columns = values[0].shape[1]
    upper_normal = [pltpu.roll(x, columns - 1, 1) for x in normal]
    own = own_side(normal, values, values_j)
    other = other_side(upper_normal, values, values_j)
    flux = [a + pltpu.roll(b, 1, 1) for a, b in zip(own, other)]
    return [pltpu.roll(x, columns - 1, 1) - x for x in flux]


def row_changes(count, at, first_flux, last_flux):
    last = None
    ahead = at(0)
    for s in range(count):
        faces, cells, cells_j = ahead
        nvar = len(cells)
        row = lax.broadcasted_iota(jnp.int32, cells[0].shape, 0)
        top, bottom = row == 0, row == STRIP - 1
        rolled_faces = [pltpu.roll(x, STRIP - 1, 0) for x in faces]
        if s + 1 < count:
            ahead = at(s + 1)
            rolled_faces = [
                jnp.where(bottom, pltpu.roll(x, STRIP - 1, 0), y) for x, y in zip(ahead[0], rolled_faces)
            ]
        own = own_side(faces, cells, cells_j)
        rolled = [pltpu.roll(x, 1, 0) for x in other_side(rolled_faces, cells, cells_j)]
        if s == 0:
            flux = [jnp.where(top, first_flux(v), own[v] + rolled[v]) for v in range(nvar)]
        else:
            flux = [own[v] + jnp.where(top, before[v], rolled[v]) for v in range(nvar)]
        lifted = [pltpu.roll(x, STRIP - 1, 0) for x in flux]
        if last is not None:
            yield (
                s - 1,
                last[0],
                last[1],
                [jnp.where(bottom, lifted[v], last[3][v]) - last[2][v] for v in range(nvar)],
            )
        before, last = rolled, (cells, cells_j, flux, lifted)
    yield (
        count - 1,
        last[0],
        last[1],
        [jnp.where(bottom, last_flux(v), last[3][v]) - last[2][v] for v in range(nvar)],
    )


def strip(s):
    return pl.ds(s * STRIP, STRIP)


def face_flux(normal, lower, lower_j, upper, upper_j):
    spread = spread_of(normal)
    return [
        normal[0] * (lower_j[0][v] + upper_j[0][v])
        + normal[1] * (lower_j[1][v] + upper_j[1][v])
        - spread * (upper[v] - lower[v])
        for v in range(len(lower))
    ]


def split_dot(x, onehot, transposed):
    high = x.astype(jnp.bfloat16)
    rest = x - high.astype(jnp.float32)
    middle = rest.astype(jnp.bfloat16)
    low = (rest - middle.astype(jnp.float32)).astype(jnp.bfloat16)
    count = x.shape[0]
    stacked = jnp.concatenate([high, middle, low], axis=0)
    out = lax.dot_general(
        stacked,
        onehot,
        (((1,), (1 if transposed else 0,)), ((), ())),
        preferred_element_type=jnp.float32,
    )
    return out[:count] + (out[count : 2 * count] + out[2 * count :])


def pair(below, above):
    return jnp.concatenate([below, above], axis=0)


def pick(mask, a, b):
    return [jnp.where(mask, x, y) for x, y in zip(a, b)]


def pick_both(mask, a, b):
    return pick(mask, a[0], b[0]), [pick(mask, x, y) for x, y in zip(a[1], b[1])]


def behind(below, above, t):
    return pair(below[pl.ds(t, 1), :], above[pl.ds(t, 1), :])


def crossed(rows, links_below, links_above, stack):
    stack[...] = jnp.zeros(stack.shape, jnp.float32)
    for t, x in enumerate(rows):
        stack[pl.ds(2 * t, 2), :] = x
    columns = stack.shape[1]
    cell = lax.broadcasted_iota(jnp.int32, (columns, columns), 0)
    onehots = [(cell == x).astype(jnp.float32).astype(jnp.bfloat16) for x in (links_below, links_above)]
    stacked = stack[...]
    side = lax.broadcasted_iota(jnp.int32, stacked.shape, 0) % 2
    stack[...] = jnp.where(
        side == 0, split_dot(stacked, onehots[0], False), split_dot(stacked, onehots[1], True)
    )
    return [stack[pl.ds(2 * t, 2), :] for t in range(len(rows))]


def edge_kernel(nvar, coefs, below, above, near, row_normals, links, early, out, kept, stack):
    depth, columns = near.shape[1], near.shape[2]
    half = half_jacobians(coefs, nvar)
    is_below = lax.broadcasted_iota(jnp.int32, (2, columns), 0) == 0
    inner_face = [
        pair(row_normals[d, pl.ds(0, 1), :], above[pl.ds(2 * nvar + 5 + d, 1), :]) for d in range(2)
    ]
    rows = [behind(below, above, nvar + v) for v in range(nvar + 1)] + inner_face
    links_above = above[pl.ds(2 * nvar + 7, 1), :].astype(jnp.int32)
    rows = crossed(rows, links[...], links_above, stack)
    rim, volume, face = rows[:nvar], rows[nvar], pick(is_below, inner_face, rows[nvar + 1 :])
    inside = [pair(near[v, pl.ds(0, 1), :], near[v, pl.ds(depth - 1, 1), :]) for v in range(nvar)]
    low, high = pick(is_below, rim, inside), pick(is_below, inside, rim)
    summed = transformed(half, [x + y for x, y in zip(low, high)])
    spread = spread_of(face)
    across = [
        face[0] * summed[0][v] + face[1] * summed[1][v] - spread * (high[v] - low[v]) for v in range(nvar)
    ]
    for v in range(nvar):
        kept[v] = rim[v]
        kept[nvar + v] = jnp.where(is_below, across[v], -across[v])
    for v, x in enumerate(rim + [volume]):
        out[pl.ds(v, 1), :] = x[0:1]
        out[pl.ds(nvar + 1 + v, 1), :] = x[1:2]
    kept[2 * nvar] = volume
    for d in range(2):
        out[pl.ds(2 * nvar + 2 + d, 1), :] = face[d][1:2]
        kept[2 * nvar + 1 + d] = face[d]
    head = out.shape[0] - 2 * depth
    for d in range(2):
        out[pl.ds(head + d * depth, depth), :] = row_normals[d]


def behind_kernel(nvar, coefs, below, above, links, out, stack):
    half = half_jacobians(coefs, nvar)
    is_below = lax.broadcasted_iota(jnp.int32, (2, links.shape[1]), 0) == 0

    def with_j(values):
        return values, transformed(half, values)

    outer, rim = [with_j([behind(below, above, t + v) for v in range(nvar)]) for t in (0, nvar)]
    low, high = pick_both(is_below, outer, rim), pick_both(is_below, rim, outer)
    at = 2 * nvar + 1
    far_flux = face_flux([behind(below, above, at + d) for d in range(2)], *low, *high)
    beside = col_change([behind(below, above, at + 2 + d) for d in range(2)], *rim)
    rows = [jnp.where(is_below, -x, x) + y for x, y in zip(far_flux, beside)]
    links_above = above[pl.ds(2 * nvar + 7, 1), :].astype(jnp.int32)
    for v, x in enumerate(crossed(rows, links[...], links_above, stack)):
        out[v] = x


def state_kernel(at, states, before, out):
    out[...] = states[0, pl.ds(at, out.shape[0])]


def volume_kernel(cells, before, out):
    out[...] = cells[pl.ds(0, 1)]


def own_flux_kernel(nvar, jacobians, near, cell, row_normals, out, coefs):
    strips = out.shape[1] // STRIP
    for d in range(2):
        for v in range(nvar):
            for w in range(nvar):
                coefs[pl.ds((d * nvar + v) * nvar + w, 1), :] = jnp.full(
                    (1, coefs.shape[1]), 0.5 * jacobians[d, v, w], jnp.float32
                )
    half = half_jacobians(coefs, nvar)

    def at(s):
        cells = [near[v, strip(s), :] for v in range(nvar)]
        return [row_normals[d, strip(s), :] for d in range(2)], cells, transformed(half, cells)

    for s, cells, cells_j, along in row_changes(strips, at, lambda v: 0.0, lambda v: 0.0):
        beside = col_change([cell[1 + d, strip(s), :] for d in range(2)], cells, cells_j)
        factor = pseudo_step / cell[0, strip(s), :]
        for v in range(nvar):
            out[v, strip(s), :] = cells[v] - factor * (along[v] + beside[v])


def planes(pieces):
    return [x.at[v] for x in pieces for v in range(x.shape[0])]


def families(n):
    return [0] + list(range(3, n, 2)), [1] + list(range(2, n, 2))


def far_col_kernel(nvar, coefs, cell, *refs):
    states, out = planes(refs[:-1]), refs[-1]
    half = half_jacobians(coefs, nvar)
    for s in range(out.shape[1] // STRIP):
        cells = [states[v][strip(s), :] for v in range(nvar)]
        beside = col_change([cell[1 + d, strip(s), :] for d in range(2)], cells, transformed(half, cells))
        factor = pseudo_step / cell[0, strip(s), :]
        for v in range(nvar):
            out[v, strip(s), :] = cells[v] - factor * beside[v]


def far_face_kernel(nvar, coefs, *refs):
    states, out = planes(refs[:-1]), refs[-1]
    half = half_jacobians(coefs, nvar)
    row = lax.broadcasted_iota(jnp.int32, (STRIP, out.shape[3]), 0)
    before = None
    for s in range(out.shape[2] // STRIP):
        cells = [states[v][strip(s), :] for v in range(nvar)]
        rolled = [pltpu.roll(x, 1, 0) for x in cells]
        lower = rolled if s == 0 else [jnp.where(row == 0, x, y) for x, y in zip(before, rolled)]
        summed = transformed(half, [x + y for x, y in zip(lower, cells)])
        for v in range(nvar):
            out[0, v, strip(s), :] = summed[0][v]
            out[1, v, strip(s), :] = summed[1][v]
            out[2, v, strip(s), :] = cells[v] - lower[v]
        before = rolled


def near_kernel(n, nvar, near, beyond, cell, volumes, part, sizes, *outs):
    here, _ = families(n)
    weights = [[step_weight(n, a, b) for b in (0, 1)] for a in here]
    for s in range(part.shape[1] // STRIP):
        for a in range(len(here)):
            sizes[a, strip(s), :] = weighted(weights[a], [cell[0, strip(s), :], volumes[0, strip(s), :]])
        for v in range(nvar):
            values = [near[v, strip(s), :], beyond[v, strip(s), :]]
            outs[0][v, strip(s), :] = part[v, strip(s), :] - weighted(weights[0], values)
            for a in range(1, len(here)):
                outs[a][v, strip(s), :] = -weighted(weights[a], values)


def time_kernel(n, nvar, near, own, sums, kept, *refs):
    far = n // 2 - 1
    beyond_states, cells, beyond_volumes, *pieces = [refs[far * t : far * (t + 1)] for t in range(3 + len(PIECES))]
    refs = refs[far * (3 + len(PIECES)) :]
    begun, parts = refs[: far + 1], refs[far + 1 : 2 * far + 1]
    rate, early, outs = refs[2 * far + 1], refs[2 * far + 2], refs[2 * far + 3 :]
    other = [step_weight(n, 1, b) for b in families(n)[0]]
    states = [planes(x) for x in zip(*pieces)]
    here, there = families(n)
    rest = [[step_weight(n, a, b) for b in here[1:] + there[1:]] for a in here]
    strips = outs[0].shape[1] // STRIP
    row = lax.broadcasted_iota(jnp.int32, (STRIP, near.shape[2]), 0)
    for s in range(strips):
        sizes = [x[0, strip(s), :] for x in (own, *cells)]
        far_sizes = sizes[1:] + [x[0, strip(s), :] for x in beyond_volumes]
        rates = [sums[a, strip(s), :] + weighted(rest[a], far_sizes) for a in range(far + 1)]
        factors = [rates[a] / sizes[a] for a in range(far + 1)]
        rate[strip(s), :] = factors[0]
        for v in range(nvar):
            values = [near[v, strip(s), :]] + [x[v][strip(s), :] for x in states]
            others = values[1:] + [x[0, v, strip(s), :] for x in beyond_states]
            moved = [
                begun[a][v, strip(s), :] - weighted(rest[a], others) - factors[a] * values[a]
                for a in range(far + 1)
            ]
            moved = moved[:1] + [moved[a] + parts[a - 1][v, strip(s), :] for a in range(1, far + 1)]
            if s == 0:
                moved[0] = moved[0] + jnp.where(row == 0, pseudo_step * kept[nvar + v][0:1], 0.0) / sizes[0]
            if s == strips - 1:
                lacking = jnp.where(row == STRIP - 1, pseudo_step * kept[nvar + v][1:2], 0.0)
                moved[0] = moved[0] + lacking / sizes[0]
            for a in range(far + 1):
                outs[a][v, strip(s), :] = moved[a]
            early[v, strip(s), :] = weighted(other, moved)


def base_kernel(n, nvar, coefs, stepped, cell, row_normals, rate, *refs):
    parts, out = refs[:-1], refs[-1]
    strips = out.shape[1] // STRIP
    half = half_jacobians(coefs, nvar)
    weight, *rest = [step_weight(n, 0, b) for b in families(n)[0]]

    def at(s):
        cells = [stepped[v, strip(s), :] for v in range(nvar)]
        return [row_normals[d, strip(s), :] for d in range(2)], cells, transformed(half, cells)

    for s, cells, cells_j, along in row_changes(strips, at, lambda v: 0.0, lambda v: 0.0):
        beside = col_change([cell[1 + d, strip(s), :] for d in range(2)], cells, cells_j)
        inverse = 1.0 / cell[0, strip(s), :]
        kept = (1.0 - weight) - rate[strip(s), :]
        for v in range(nvar):
            value = kept * cells[v] - (pseudo_step * inverse) * (along[v] + beside[v])
            out[v, strip(s), :] = value - weighted(rest, [x[v, strip(s), :] for x in parts])


def far_step_kernel(n, nvar, coefs, early, edge, *refs):
    far = n // 2 - 1
    edges, cells_of, beside, *pieces = [refs[far * t : far * (t + 1)] for t in range(3 + len(PIECES))]
    states = [planes(x) for x in zip(*pieces)]
    shared, outs = refs[far * (3 + len(PIECES))], refs[far * (3 + len(PIECES)) + 1 :]
    depth, columns = early.shape[1], early.shape[2]
    strips = depth // STRIP
    other = [step_weight(n, 1, b) for b in families(n)[0]]
    head = edge.shape[0] - 2 * depth
    half = half_jacobians(coefs, nvar)
    is_below = lax.broadcasted_iota(jnp.int32, (2, columns), 0) == 0
    row = lax.broadcasted_iota(jnp.int32, (STRIP, columns), 0)

    def interface(a):
        ends = [pair(states[a][v][pl.ds(0, 1), :], states[a][v][pl.ds(depth - 1, 1), :]) for v in range(nvar)]
        rims = [pair(edges[a][pl.ds(v, 1), :], edges[a][pl.ds(nvar + 1 + v, 1), :]) for v in range(nvar)]
        face = [
            pair(edges[a][pl.ds(head + d * depth, 1), :], edges[a][pl.ds(2 * nvar + 2 + d, 1), :])
            for d in range(2)
        ]
        ends_j = transformed(half, [x + y for x, y in zip(ends, rims)])
        spread = jnp.where(is_below, spread_of(face), -spread_of(face))
        return [
            face[0] * ends_j[0][v] + face[1] * ends_j[1][v] - spread * (ends[v] - rims[v]) for v in range(nvar)
        ]

    def flux_of(a, s):
        normal = [edges[a][pl.ds(head + d * depth + s * STRIP, STRIP), :] for d in range(2)]
        spread = spread_of(normal)
        flux = []
        for v in range(nvar):
            sums, difference = [beside[a][d, v, strip(s), :] for d in range(2)], beside[a][2, v, strip(s), :]
            flux.append(normal[0] * sums[0] + normal[1] * sums[1] - spread * difference)
        return flux, [pltpu.roll(x, STRIP - 1, 0) for x in flux]

    across = [None] * far
    fluxes = [[None] * (strips + 1) for _ in range(far)]
    for s in list(range(2, strips)) + [1, strips, 0]:
        for a in range(far):
            if s in (strips, 0) and across[a] is None:
                across[a] = interface(a)
            if s == strips:
                fluxes[a][s] = (None, [across[a][v][1:2] for v in range(nvar)])
            else:
                fluxes[a][s] = flux_of(a, s)
            if s == 0:
                flux = [jnp.where(row == 0, across[a][v][0:1], fluxes[a][0][0][v]) for v in range(nvar)]
                fluxes[a][0] = (flux, fluxes[a][0][1])
        for t in {2: [], 1: [1], strips: [strips - 1], 0: [0]}.get(s, [s - 1]):
            factors = [pseudo_step / cells_of[a][0, strip(t), :] for a in range(far)]
            for v in range(nvar):
                total = early[v, strip(t), :]
                for a in range(far):
                    above = jnp.where(row == STRIP - 1, fluxes[a][t + 1][1][v], fluxes[a][t][1][v])
                    value = factors[a] * (above - fluxes[a][t][0][v])
                    outs[a][v, strip(t), :] = value
                    total = total - other[1 + a] * value
                shared[pl.ds(v * depth + t * STRIP, STRIP), :] = total
    rims = pl.ds(0, 2 * nvar + 2)
    shared[pl.ds(nvar * depth, 2 * nvar + 2), :] = weighted(
        other, [edge[rims, :]] + [edges[a][rims, :] for a in range(far)]
    )


def rim_kernel(n, nvar, coefs, edge, kept, others, cell, stepped, *refs):
    far = n // 2 - 1
    edges, out = refs[:far], refs[far]
    depth, columns = stepped.shape[1], stepped.shape[2]
    half = half_jacobians(coefs, nvar)
    weights = [step_weight(n, 0, b) for b in families(n)[0]]
    is_below = lax.broadcasted_iota(jnp.int32, (2, columns), 0) == 0

    def rim(v):
        return weighted(
            weights,
            [
                pair(ref[pl.ds(v, 1), :], ref[pl.ds(nvar + 1 + v, 1), :])
                for ref in [edge] + list(edges)
            ],
        )

    inverse = 1.0 / kept[2 * nvar]
    volume_rate = rim(nvar)
    face = [kept[2 * nvar + 1], kept[2 * nvar + 2]]
    spread = spread_of(face)
    inside = [pair(stepped[v, pl.ds(0, 1), :], stepped[v, pl.ds(depth - 1, 1), :]) for v in range(nvar)]
    inside_j = transformed(half, inside)
    for v in range(nvar):
        change = pseudo_step * (kept[nvar + v] + others[v])
        out[v] = kept[v] - rim(v) - inverse * (kept[v] * volume_rate + change)
        out[nvar + v] = inverse * kept[v]
        out[2 * nvar + v] = (
            face[0] * inside_j[0][v]
            + face[1] * inside_j[1][v]
            + jnp.where(is_below, -spread, spread) * inside[v]
        )
    volume = pair(cell[0, pl.ds(0, 1), :], cell[0, pl.ds(depth - 1, 1), :])
    factor = pseudo_step / volume
    out[3 * nvar] = jnp.where(is_below, factor, -factor)


def final_kernel(n, nvar, coefs, rims, kept, base, shared, *refs):
    rows, (out, held, sems) = refs[:-3], refs[-3:]
    weights = [step_weight(n, 0, b) for b in families(n)[0][1:]]
    depth, columns = base.shape[1], base.shape[2]
    strips = depth // STRIP
    half = half_jacobians(coefs, nvar)
    is_below = lax.broadcasted_iota(jnp.int32, (2, columns), 0) == 0

    def summed(v):
        return pair(shared[pl.ds(nvar * depth + v, 1), :], shared[pl.ds(nvar * depth + nvar + 1 + v, 1), :])

    def value(v, s):
        total = base[v, strip(s), :] - shared[pl.ds(v * depth + s * STRIP, STRIP), :]
        return total + weighted(weights, [x[v, strip(s), :] for x in rows])

    copies = []

    def send(t, first, count):
        where = pl.ds(first * STRIP, count * STRIP)
        copies.append(pltpu.make_async_copy(held.at[:, where], out.at[0, :, where], sems.at[t]))
        copies[-1].start()

    for s in range(1, strips - 1):
        for v in range(nvar):
            held[v, strip(s), :] = value(v, s)
    send(0, 1, strips - 2)
    volume_rate = summed(nvar)
    outside = [rims[v] - summed(v) - rims[nvar + v] * volume_rate for v in range(nvar)]
    outside_j = transformed(half, outside)
    face = [kept[2 * nvar + 1], kept[2 * nvar + 2]]
    spread = spread_of(face)
    signed = jnp.where(is_below, spread, -spread)
    row = lax.broadcasted_iota(jnp.int32, (STRIP, columns), 0)
    for v in range(nvar):
        across = face[0] * outside_j[0][v] + face[1] * outside_j[1][v] + signed * outside[v]
        lacking = rims[3 * nvar] * (across + rims[2 * nvar + v])
        held[v, strip(0), :] = value(v, 0) + jnp.where(row == 0, lacking[0:1], 0.0)
        held[v, strip(strips - 1), :] = value(v, strips - 1) + jnp.where(
            row == STRIP - 1, lacking[1:2], 0.0
        )
    send(1, 0, 1)
    send(2, strips - 1, 1)
    for copy in copies:
        copy.wait()


def body(states, volumes, row_normals, col_normals, face_links, jacobians):
    n = lax.axis_size("inst")
    slabs = lax.axis_size("slab")
    _, nvar, depth, columns = states.shape
    far = list(range(2, n, 2))
    down_rows = -(-(2 * nvar + 8) // 8) * 8
    up_rows = down_rows + 8
    head = -(-(2 * nvar + 4) // 8) * 8

    def f32(*shape):
        return jax.ShapeDtypeStruct(shape, jnp.float32)

    vmem = pl.BlockSpec(memory_space=pltpu.VMEM)
    smem = pl.BlockSpec(memory_space=pltpu.SMEM)
    hbm = pl.BlockSpec(memory_space=pltpu.HBM)
    params = pltpu.CompilerParams(vmem_limit_bytes=24 * 1024 * 1024)

    def call(kernel, name, shapes, *operands, scratch=(), out_spec=vmem):
        single = not isinstance(shapes, list)
        return pl.pallas_call(
            kernel,
            out_shape=shapes,
            in_specs=[smem if x is jacobians else vmem for x in operands],
            out_specs=out_spec if single else [out_spec] * len(shapes),
            scratch_shapes=list(scratch),
            compiler_params=params,
            name=name,
        )(*operands)

    def swapped(x, k):
        return lax.ppermute(x, "inst", [(i, i ^ k) for i in range(n)])

    state_of = {k: swapped(states, k) for k in far}
    inputs = [
        pltpu.with_memory_space_constraint(x, pltpu.HBM)
        for x in (states, volumes, row_normals, col_normals, face_links)
    ]
    near, own_cell, own_rows, own_links, upward, downward = pl.pallas_call(
        pack_kernel,
        out_shape=[
            f32(nvar, depth, columns),
            f32(3, depth, columns),
            f32(2, depth, columns),
            jax.ShapeDtypeStruct(face_links.shape, face_links.dtype),
            f32(up_rows, columns),
            f32(down_rows, columns),
        ],
        in_specs=[hbm] * 5,
        out_specs=[vmem] * 6,
        scratch_shapes=[pltpu.SemaphoreType.DMA((5,))],
        compiler_params=params,
        name="pack",
    )(*inputs)
    cell_of = {k: swapped(own_cell, k + 1) for k in far}
    below = lax.ppermute(upward, "slab", [(i, (i + 1) % slabs) for i in range(slabs)])
    above = lax.ppermute(downward, "slab", [(i, (i - 1) % slabs) for i in range(slabs)])
    field = f32(nvar, depth, columns)
    own_part, coefs = call(
        functools.partial(own_flux_kernel, nvar),
        "own_flux",
        [field, f32(-(-2 * nvar * nvar // 8) * 8, columns)],
        jacobians,
        near,
        own_cell,
        own_rows,
    )
    parts = []
    edge, kept = call(
        functools.partial(edge_kernel, nvar),
        "edges",
        [f32(head + 2 * depth, columns), f32(2 * nvar + 3, 2, columns)],
        coefs,
        below,
        above,
        near,
        own_rows,
        own_links,
        own_part,
        scratch=[pltpu.VMEM((-(-(2 * nvar + 6) // 8) * 8, columns), jnp.float32)],
    )
    others = call(
        functools.partial(behind_kernel, nvar),
        "behind",
        f32(nvar, 2, columns),
        coefs,
        below,
        above,
        own_links,
        scratch=[pltpu.VMEM((-(-2 * nvar // 8) * 8, columns), jnp.float32)],
    )
    edge_of = {k: swapped(edge, k + 1) for k in far}
    beyond = swapped(near, 1)
    sums, *begun = call(
        functools.partial(near_kernel, n, nvar),
        "near",
        [f32(len(far) + 1, depth, columns)] + [field] * (len(far) + 1),
        near,
        beyond,
        own_cell,
        swapped(call(volume_kernel, "volumes", f32(1, depth, columns), own_cell, others), 1),
        own_part,
    )
    pieces_of, beyond_volumes = dict(), dict()
    for k in far:
        pieces, at = [], 0
        for t, count in enumerate(PIECES):
            before = begun[0] if t + 1 == len(PIECES) else edge
            shape = f32(count, depth, columns)
            kernel = functools.partial(state_kernel, at)
            held = call(kernel, "states", shape, state_of[k], before)
            pieces.append(swapped(held, 1))
            at += count
        pieces_of[k] = pieces
        held = call(volume_kernel, "volumes", f32(1, depth, columns), cell_of[k], begun[0])
        beyond_volumes[k] = swapped(held, 1)

    faces = {}
    for k in far:
        shape = f32(3, nvar, depth, columns)
        faces[k] = call(functools.partial(far_face_kernel, nvar), "far_faces", shape, coefs, *pieces_of[k])
        parts.append(
            call(functools.partial(far_col_kernel, nvar), "far_col", field, coefs, cell_of[k], *pieces_of[k])
        )
    rate, early, stepped, *parts = call(
        functools.partial(time_kernel, n, nvar),
        "time",
        [f32(depth, columns)] + [field] * (len(far) + 2),
        near,
        own_cell,
        sums,
        kept,
        *[state_of[k] for k in far],
        *[cell_of[k] for k in far],
        *[beyond_volumes[k] for k in far],
        *[pieces_of[k][t] for t in range(len(PIECES)) for k in far],
        *begun,
        *parts,
    )
    base = call(
        functools.partial(base_kernel, n, nvar),
        "base",
        field,
        coefs,
        stepped,
        own_cell,
        own_rows,
        rate,
        *parts,
    )
    shared, *rows = call(
        functools.partial(far_step_kernel, n, nvar),
        "far_step",
        [f32(nvar * depth + 16, columns)] + [field] * len(far),
        coefs,
        early,
        edge,
        *[edge_of[k] for k in far],
        *[cell_of[k] for k in far],
        *[faces[k] for k in far],
        *[pieces_of[k][t] for t in range(len(PIECES)) for k in far],
    )
    rims = call(
        functools.partial(rim_kernel, n, nvar),
        "rims",
        f32(3 * nvar + 1, 2, columns),
        coefs,
        edge,
        kept,
        others,
        own_cell,
        stepped,
        *[edge_of[k] for k in far],
    )
    return call(
        functools.partial(final_kernel, n, nvar),
        "final",
        f32(1, nvar, depth, columns),
        coefs,
        rims,
        kept,
        base,
        swapped(shared, 1),
        *rows,
        scratch=[pltpu.VMEM((nvar, depth, columns), jnp.float32), pltpu.SemaphoreType.DMA((3,))],
        out_spec=hbm,
    )


def solution(mesh):
    return jax.shard_map(
        body,
        mesh=mesh,
        in_specs=(
            P(("grp", "inst"), None, "slab", None),
            P(("grp", "inst"), "slab", None),
            P(("grp", "inst"), None, "slab", None),
            P(("grp", "inst"), None, "slab", None),
            P("slab", None),
            P(),
        ),
        out_specs=P(("grp", "inst"), None, "slab", None),
        check_vma=False,
    )
```
